32 devices in a mesh: dp: 8 (over z, x), tensor: 4 (over y, core).
Axes of the slice: x: 2, y: 2, z: 4, core: 2. Of those that a mesh axis runs over, the one named last changes fastest.
Arguments:
- tokens: bfloat16 [16384, 1024], P(('dp', 'tensor')), may hold values from -6 to 6
- cotangent: bfloat16 [16384, 1024], P(('dp', 'tensor')), may hold values from -6 to 6
- group_ids: int32 [16384], P(('dp', 'tensor')), may hold values from 0 to 3
- assign_attn: int32 [1026], replicated, may hold values from 0 to 1375, as said below
- assign_mlp: int32 [2048], replicated, may hold values from 0 to 2735, as said below
- master_attn: float32 [4, 1376, 1024], P('tensor', 'dp'), as said below
- moment_attn: float32 [4, 1376, 1024], P('tensor', 'dp'), as said below
- square_attn: float32 [4, 1376, 1024], P('tensor', 'dp'), as said below
- master_mlp: float32 [4, 2736, 1024], P('tensor', 'dp'), as said below
- moment_mlp: float32 [4, 2736, 1024], P('tensor', 'dp'), as said below
- square_mlp: float32 [4, 2736, 1024], P('tensor', 'dp'), as said below
Outputs:
- layer_out: bfloat16 [16384, 1024], P(('dp', 'tensor'))
- d_tokens: float32 [16384, 1024], P(('dp', 'tensor'))
- new_master_attn: float32 [4, 1376, 1024], P('tensor', 'dp')
- new_moment_attn: float32 [4, 1376, 1024], P('tensor', 'dp')
- new_square_attn: float32 [4, 1376, 1024], P('tensor', 'dp')
- new_master_mlp: float32 [4, 2736, 1024], P('tensor', 'dp')
- new_moment_mlp: float32 [4, 2736, 1024], P('tensor', 'dp')
- new_square_mlp: float32 [4, 2736, 1024], P('tensor', 'dp')
The draws below stay inside these ranges and needn't reach their ends.
Inputs may be any that keep to these rules, and one draw needn't show every extreme that they name: `assign_attn`: entries are distinct slots; slot s belongs to dp index s / 172; every dp index holds at most 172 rows and some index holds exactly 172. `assign_mlp`: entries are distinct slots; slot s belongs to dp index s / 342; every dp index holds at most 342 rows and some index holds exactly 342. `master_attn`: parameters of every slot, free ones too. `moment_attn`: first moments. `square_attn`: second moments, positive. `master_mlp`: parameters of every slot, free ones too. `moment_mlp`: first moments. `square_mlp`: second moments, positive.
All inputs are finite; a program needn't handle non-finite values.
Results may differ from the reference program's by a relative error of at most 0.013.
Values may be sent and summed in bfloat16 or wider, within the bound.
No kernel may reach another device: no remote copies, remote signals or barrier semaphores. Data moves between devices by JAX's collectives and lax.ppermute only.
A program may use at most 192 MiB of HBM per device.

```python
import math
import jax
import jax.numpy as jnp
from jax import lax

D = 1024
HEADS = 16
HEAD = 64
FF = 4096
SEQ_LEN = 2048
GROUPS = 4
ADAM_STEP = 5
TOKENS = 16384
QA = 1026
QM = 2048
CAP_A = 172
CAP_M = 342
N_DP = 8
N_TENSOR = 4


def owner_slots(key, row_total, capacity):
    slot_total = N_DP * capacity
    subkeys = jax.random.split(key, 4)
    busiest = jax.random.randint(subkeys[0], (), 0, N_DP)
    leading = busiest * capacity + jax.random.permutation(subkeys[1], capacity)
    others = jax.random.permutation(subkeys[2], slot_total - capacity)
    others = jnp.where(others >= busiest * capacity, others + capacity, others)
    slot_list = jnp.concatenate([leading, others])[:row_total].astype(jnp.int32)
    shuffle = jax.random.permutation(subkeys[3], row_total)
    return jnp.zeros((row_total,), jnp.int32).at[shuffle].set(slot_list)


def slot_pieces_drawn(assign, slot_total):
    return jnp.full((slot_total,), -1, jnp.int32).at[assign].set(jnp.arange(assign.shape[0], dtype=jnp.int32))


def attn_kinds(key):
    assign = owner_slots(jax.random.fold_in(key, 11), QA, CAP_A)
    pieces = slot_pieces_drawn(assign, N_DP * CAP_A)[None, :, None]
    head_dims = D // N_TENSOR
    vector = jnp.arange(N_TENSOR, dtype=jnp.int32)[:, None, None] * (8 // N_TENSOR) + pieces - 4 * head_dims
    is_gain = (pieces >= 4 * head_dims) & (vector % 2 == 0)
    spread = jnp.where(pieces < 3 * head_dims, D ** (-0.5), jnp.where(pieces < 4 * head_dims, max(D // 64, 1) ** (-0.5), 0.2))
    gradient = jnp.where(pieces < 3 * head_dims, 0.3, jnp.where(pieces < 4 * head_dims, 0.2, 1.5)) * TOKENS ** 0.5
    full_shape = (N_TENSOR, N_DP * CAP_A, D)
    return (full_shape, jnp.broadcast_to(spread, full_shape), jnp.broadcast_to(is_gain, full_shape), jnp.broadcast_to(gradient, full_shape))


def mlp_kinds(key):
    assign = owner_slots(jax.random.fold_in(key, 12), QM, CAP_M)
    pieces = slot_pieces_drawn(assign, N_DP * CAP_M)[None, :, None]
    hidden_here = FF // N_TENSOR
    spread = jnp.where(pieces < hidden_here, D ** (-0.5), FF ** (-0.5))
    gradient = jnp.where(pieces < hidden_here, 0.5, 0.9) * TOKENS ** 0.5
    full_shape = (N_TENSOR, N_DP * CAP_M, D)
    return (full_shape, jnp.broadcast_to(spread, full_shape), jnp.broadcast_to(gradient, full_shape))


def draw_assign_attn(key, part):
    return owner_slots(jax.random.fold_in(key, 11), QA, CAP_A)


def draw_assign_mlp(key, part):
    return owner_slots(jax.random.fold_in(key, 12), QM, CAP_M)


def draw_master_attn(key, part):
    full_shape, spread, is_gain, gradient = attn_kinds(key)
    key = jax.random.fold_in(key, 21)
    noise = jax.random.normal(key, full_shape, jnp.float32)
    return jnp.where(is_gain, 1.0 + 0.12 * noise, spread * noise)


def draw_moment_attn(key, part):
    full_shape, spread, is_gain, gradient = attn_kinds(key)
    key = jax.random.fold_in(key, 22)
    noise = jax.random.normal(key, full_shape, jnp.float32)
    return gradient * noise


def draw_square_attn(key, part):
    full_shape, spread, is_gain, gradient = attn_kinds(key)
    key = jax.random.fold_in(key, 23)
    factor = jnp.exp(jax.random.uniform(key, full_shape, jnp.float32, 0.0, math.log(4.0)))
    return gradient * gradient * factor


def draw_master_mlp(key, part):
    full_shape, spread, gradient = mlp_kinds(key)
    key = jax.random.fold_in(key, 31)
    noise = jax.random.normal(key, full_shape, jnp.float32)
    return spread * noise


def draw_moment_mlp(key, part):
    full_shape, spread, gradient = mlp_kinds(key)
    key = jax.random.fold_in(key, 32)
    noise = jax.random.normal(key, full_shape, jnp.float32)
    return gradient * noise


def draw_square_mlp(key, part):
    full_shape, spread, gradient = mlp_kinds(key)
    key = jax.random.fold_in(key, 33)
    factor = jnp.exp(jax.random.uniform(key, full_shape, jnp.float32, 0.0, math.log(4.0)))
    return gradient * gradient * factor


def place_ends(result, own_key, smallest, largest):
    spot = [jax.random.randint(jax.random.fold_in(own_key, axis), (), 0, length) for axis, length in enumerate(result.shape)]
    main_axis = result.shape.index(max(result.shape))
    neighbour = spot[:main_axis] + [(spot[main_axis] + 1) % result.shape[main_axis]] + spot[main_axis + 1:]
    return result.at[tuple(spot)].set(smallest).at[tuple(neighbour)].set(largest)


def block_levels(key, shape, cuts, low, high):
    def one(position, parts):
        heights = jax.random.uniform(jax.random.fold_in(jax.random.fold_in(key, 6), position), (parts,), jnp.float32, low / len(cuts), high / len(cuts))
        return jnp.repeat(jnp.exp(heights), shape[position] // parts).reshape((-1,) + (1,) * (len(shape) - position - 1))

    gain = one(*cuts[0])
    for cut in cuts[1:]:
        gain = gain * one(*cut)
    return gain


def gaussian(rng, dims, scale, limit, cuts=(), kind=jnp.bfloat16):
    loudness = block_levels(rng, dims, cuts, -0.22, 0.18) if cuts else 1.0
    drawn = jax.random.normal(rng, dims, jnp.float32) * scale * loudness
    return jnp.minimum(jnp.maximum(drawn, -limit), limit).astype(kind)


def setup_inputs(seed: int = 0) -> dict:
    streams_of = jax.random.split(jax.random.key(seed), 12)
    tokens = gaussian(streams_of[0], (TOKENS, D), 1.0, 6.0, ((0, 32),))
    cotangent = gaussian(streams_of[1], (TOKENS, D), 1.0, 6.0, ((0, 32),))
    group_ids = place_ends(jax.random.randint(streams_of[2], (TOKENS,), 0, GROUPS), jax.random.fold_in(streams_of[2], 1), 0, GROUPS - 1).astype(jnp.int32)
    assign_attn = draw_assign_attn(jax.random.fold_in(streams_of[11], 71), 0)
    assign_mlp = draw_assign_mlp(jax.random.fold_in(streams_of[11], 71), 0)
    master_attn = draw_master_attn(jax.random.fold_in(streams_of[11], 71), 0)
    moment_attn = draw_moment_attn(jax.random.fold_in(streams_of[11], 71), 0)
    square_attn = draw_square_attn(jax.random.fold_in(streams_of[11], 71), 0)
    master_mlp = draw_master_mlp(jax.random.fold_in(streams_of[11], 71), 0)
    moment_mlp = draw_moment_mlp(jax.random.fold_in(streams_of[11], 71), 0)
    square_mlp = draw_square_mlp(jax.random.fold_in(streams_of[11], 71), 0)
    return dict(tokens=tokens, cotangent=cotangent, group_ids=group_ids, assign_attn=assign_attn, assign_mlp=assign_mlp, master_attn=master_attn, moment_attn=moment_attn, square_attn=square_attn, master_mlp=master_mlp, moment_mlp=moment_mlp, square_mlp=square_mlp)


@jax.custom_vjp
def low(v):
    return lax.optimization_barrier(v.astype(jnp.bfloat16)).astype(jnp.float32)

@jax.custom_vjp
def low_back(v):
    return v

def low_keep(v):
    return (low(v), None)

def low_pass(kept, grad):
    return (grad,)

def back_keep(v):
    return (v, None)

def back_low(kept, grad):
    return (low(grad),)
low.defvjp(low_keep, low_pass)
low_back.defvjp(back_keep, back_low)
EPS_NORM = 1e-05
EPS_ADAM = 1e-08
BETA_FIRST = 0.5
BETA_SECOND = 0.5
DECAY_RATE = 0.1
HIGHEST = lax.Precision.HIGHEST

def layer_norm(values, gain_vec, shift_vec):
    average = lax.optimization_barrier(jnp.mean(values, axis=-1, keepdims=True))
    centred = values - average
    variance = lax.optimization_barrier(jnp.mean(centred * centred, axis=-1, keepdims=True))
    return centred * lax.rsqrt(variance + EPS_NORM) * gain_vec + shift_vec

def rotary_tables(length, head_size):
    half_width = head_size // 2
    frequency = 10000.0 ** (-jnp.arange(half_width, dtype=jnp.float32) / half_width)
    angles = jnp.arange(length, dtype=jnp.float32)[:, None] * frequency[None, :]
    return (jnp.cos(angles)[:, None, :], jnp.sin(angles)[:, None, :])

def rotate(values, cosines, sines):
    half_width = values.shape[-1] // 2
    leading = values[..., :half_width]
    trailing = values[..., half_width:]
    return jnp.concatenate([leading * cosines - trailing * sines, trailing * cosines + leading * sines], axis=-1)

def attend(queries, keys_all, values):
    length = queries.shape[0]
    block_rows = min(512, length)
    score_scale = HEAD ** (-0.5)
    key_places = jnp.arange(length, dtype=jnp.int32)

    def one_block(block_index):
        offset = (block_index * block_rows).astype(jnp.int32)
        query_rows = lax.dynamic_slice_in_dim(queries, offset, block_rows, 0)
        scores = low_back(jnp.einsum('qhd,khd->hqk', query_rows, keys_all, precision=HIGHEST) * score_scale)
        places = offset + jnp.arange(block_rows, dtype=jnp.int32)
        visible = places[:, None] >= key_places[None, :]
        scores = jnp.where(visible[None], scores, -1e+30)
        highest = lax.optimization_barrier(jnp.max(scores, axis=-1, keepdims=True))
        weights = jnp.exp(scores - highest)
        probs_low = low(weights / lax.optimization_barrier(jnp.sum(weights, axis=-1, keepdims=True)))
        return jnp.einsum('hqk,khd->qhd', probs_low, values, precision=HIGHEST)
    attended = lax.map(jax.checkpoint(one_block), jnp.arange(length // block_rows, dtype=jnp.int32))
    return attended.reshape(length, queries.shape[1] * queries.shape[2])

def sequence_forward(inputs, weights, cosines, sines):
    w_query, w_key, w_value, w_output, w_up, w_down, norms = weights
    length = inputs.shape[0]

    def split_heads(values):
        return values.reshape(length, HEADS, HEAD)
    normed = low(layer_norm(inputs, norms[0], norms[1]))
    queries = low(rotate(split_heads(low_back(jnp.dot(normed, w_query.T, precision=HIGHEST))), cosines, sines))
    keys_all = low(rotate(split_heads(low_back(jnp.dot(normed, w_key.T, precision=HIGHEST))), cosines, sines))
    values = low(split_heads(low_back(jnp.dot(normed, w_value.T, precision=HIGHEST))))
    attended = low_back(low(attend(queries, keys_all, values)))
    branch = low_back(jnp.dot(attended, w_output, precision=HIGHEST))
    residual = inputs + layer_norm(branch, norms[2], norms[3])
    mlp_input = low(layer_norm(residual, norms[4], norms[5]))
    pre_act = low_back(jnp.dot(mlp_input, w_up.T, precision=HIGHEST))
    activated = low(jax.nn.gelu(pre_act, approximate=False))
    mlp_branch = low_back(jnp.dot(activated, w_down, precision=HIGHEST))
    return residual + layer_norm(mlp_branch, norms[6], norms[7])

def assemble(master_attn, master_mlp, assign_attn, assign_mlp):
    head_dims = D // N_TENSOR
    hidden_here = FF // N_TENSOR
    norm_here = 8 // N_TENSOR
    attn_rows = low(master_attn)[:, assign_attn, :]
    mlp_rows = low(master_mlp)[:, assign_mlp, :]

    def gather_rows(lower, upper):
        return attn_rows[:, lower:upper, :].reshape(-1, D)
    return (gather_rows(0, head_dims), gather_rows(head_dims, 2 * head_dims), gather_rows(2 * head_dims, 3 * head_dims), gather_rows(3 * head_dims, 4 * head_dims), mlp_rows[:, :hidden_here, :].reshape(FF, D), mlp_rows[:, hidden_here:, :].reshape(FF, D), gather_rows(4 * head_dims, 4 * head_dims + norm_here))

def slot_pieces(assign, slot_total):
    return jnp.full((slot_total,), -1, jnp.int32).at[assign].set(jnp.arange(assign.shape[0], dtype=jnp.int32))

def attn_rates(pieces):
    head_dims = D // N_TENSOR
    return jnp.where(pieces < 3 * head_dims, 0.06, jnp.where(pieces < 4 * head_dims, 0.4, 0.2)).astype(jnp.float32)

def mlp_rates(pieces):
    return jnp.where(pieces < FF // N_TENSOR, 0.06, 0.03).astype(jnp.float32)

def adamw(master, moment, square, gradient, step_rate):
    moment_new = BETA_FIRST * moment + (1.0 - BETA_FIRST) * gradient
    square_new = BETA_SECOND * square + (1.0 - BETA_SECOND) * gradient * gradient
    moment_hat = moment_new / (1.0 - BETA_FIRST ** ADAM_STEP)
    square_hat = square_new / (1.0 - BETA_SECOND ** ADAM_STEP)
    update = moment_hat / (jnp.sqrt(square_hat) + EPS_ADAM) + DECAY_RATE * master
    return (master - step_rate[None, :, None] * update, moment_new, square_new)

def reference(tokens, cotangent, group_ids, assign_attn, assign_mlp, master_attn, moment_attn, square_attn, master_mlp, moment_mlp, square_mlp):
    cosines, sines = rotary_tables(SEQ_LEN, HEAD)
    inputs = tokens.astype(jnp.float32).reshape(N_DP, SEQ_LEN, D)

    def forward(inputs, master_attn, master_mlp):
        weights = assemble(master_attn, master_mlp, assign_attn, assign_mlp)

        def one_sequence(carried, sequence):
            return (carried, sequence_forward(sequence, weights, cosines, sines))
        _, outputs = lax.scan(one_sequence, jnp.zeros((), jnp.float32), inputs)
        return outputs
    outputs, pullback = jax.vjp(forward, inputs, master_attn, master_mlp)
    weighting = 0.5 + 0.5 * group_ids.astype(jnp.float32)
    weighted = cotangent.astype(jnp.float32) * weighting[:, None]
    d_inputs, grad_attn, grad_mlp = pullback(weighted.reshape(N_DP, SEQ_LEN, D))
    new_master_attn, new_moment_attn, new_square_attn = adamw(master_attn, moment_attn, square_attn, grad_attn, attn_rates(slot_pieces(assign_attn, N_DP * CAP_A)))
    new_master_mlp, new_moment_mlp, new_square_mlp = adamw(master_mlp, moment_mlp, square_mlp, grad_mlp, mlp_rates(slot_pieces(assign_mlp, N_DP * CAP_M)))
    layer_out = outputs.reshape(TOKENS, D).astype(jnp.bfloat16)
    d_tokens = d_inputs.reshape(TOKENS, D)
    return (layer_out, d_tokens, new_master_attn, new_moment_attn, new_square_attn, new_master_mlp, new_moment_mlp, new_square_mlp)
```

```python
import functools
import jax
import jax.numpy as jnp
from jax import lax
from jax.sharding import PartitionSpec as P
from jax.experimental import pallas as pl
from jax.experimental.pallas import tpu as pltpu

BF = jnp.bfloat16
F32 = jnp.float32
EPS = 1e-5
HEAD = 64
LIMIT = 48 * 1024 * 1024


def dot_nn(a, b):
    return lax.dot_general(a, b, (((1,), (0,)), ((), ())), preferred_element_type=F32)


def dot_nt(a, b):
    return lax.dot_general(a, b, (((1,), (1,)), ((), ())), preferred_element_type=F32)


def params():
    return pltpu.CompilerParams(vmem_limit_bytes=LIMIT)


def whole(shape):
    return pl.BlockSpec(shape, lambda *_: (0,) * len(shape))


def qkv_kernel(perm, x_ref, w_ref, n_ref, cos_ref, sin_ref, a_ref, qt_ref, kt_ref, vt_ref, k4_ref, v4_ref):
    x = x_ref[0].astype(F32)
    mean = jnp.mean(x, axis=-1, keepdims=True)
    xc = x - mean
    var = jnp.mean(xc * xc, axis=-1, keepdims=True)
    a = (xc * lax.rsqrt(var + EPS) * n_ref[0:1, :] + n_ref[1:2, :]).astype(BF)
    a_ref[0] = a
    cos, sin = cos_ref[...], sin_ref[...]
    heads = qt_ref.shape[0] // HEAD
    half = HEAD // 2
    dims = heads * HEAD
    for part in range(3):
        proj = dot_nt(w_ref[part * dims:(part + 1) * dims, :], a)
        for h in range(heads):
            lo = slice(h * HEAD, h * HEAD + half)
            hi = slice(h * HEAD + half, (h + 1) * HEAD)
            hd = slice(h * HEAD, (h + 1) * HEAD)
            if part < 2:
                first, second = proj[lo], proj[hi]
                r1 = first * cos - second * sin
                r2 = second * cos + first * sin
                if part == 0:
                    qt_ref[lo, :] = (r1 * 0.125).astype(BF)
                    qt_ref[hi, :] = (r2 * 0.125).astype(BF)
                else:
                    full = jnp.concatenate([r1, r2], axis=0)
                    kt_ref[hd, :] = full.astype(BF)
                    k4_ref[h] = full.T.astype(BF)
            else:
                vt_ref[hd, :] = proj[hd].astype(BF)
                v4_ref[h] = proj[hd].T.astype(BF)


def qkv_call(perm, x_rel, w, norms, cos_t, sin_t):
    n, rows, width = x_rel.shape
    dims = w.shape[0] // 3
    heads = dims // HEAD
    length = n * rows
    tok = pl.BlockSpec((dims, rows), lambda k, p: (0, p[k]))
    hd = pl.BlockSpec((heads, rows, HEAD), lambda k, p: (0, p[k], 0))
    tab = pl.BlockSpec((HEAD // 2, rows), lambda k, p: (0, p[k]))
    xb = pl.BlockSpec((1, rows, width), lambda k, p: (k, 0, 0))
    return pl.pallas_call(
        qkv_kernel,
        grid_spec=pltpu.PrefetchScalarGridSpec(
            num_scalar_prefetch=1, grid=(n,),
            in_specs=[xb, whole(w.shape), whole(norms.shape), tab, tab],
            out_specs=[xb, tok, tok, tok, hd, hd],
        ),
        out_shape=[
            jax.ShapeDtypeStruct(x_rel.shape, BF),
            jax.ShapeDtypeStruct((dims, length), BF),
            jax.ShapeDtypeStruct((dims, length), BF),
            jax.ShapeDtypeStruct((dims, length), BF),
            jax.ShapeDtypeStruct((heads, length, HEAD), BF),
            jax.ShapeDtypeStruct((heads, length, HEAD), BF),
        ],
        compiler_params=params(),
    )(perm, x_rel, w, norms, cos_t, sin_t)


QB = 256


def attn_fwd_kernel(chunk, chunks, perm, qt_ref, k4_ref, vt_ref, wo_ref, zp_ref, ot_ref, lse_ref, acc):
    t = pl.program_id(0)
    b = chunks * t + chunk
    heads = qt_ref.shape[0] // HEAD
    rows = lax.broadcasted_iota(jnp.int32, (QB, QB), 0)
    cols = lax.broadcasted_iota(jnp.int32, (QB, QB), 1)
    seen = rows <= cols

    def block(kb, carry, first):
        ks = pl.ds(pl.multiple_of(kb * QB, QB), QB)
        out = []
        for h in range(heads):
            hd = slice(h * HEAD, (h + 1) * HEAD)
            s = dot_nn(k4_ref[h, ks, :], qt_ref[hd, :])
            if first:
                s = jnp.where(seen, s, -1e30)
                m = jnp.max(s, axis=0, keepdims=True)
                p = jnp.exp(s - m)
                l = jnp.sum(p, axis=0, keepdims=True)
                acc[hd, :] = dot_nn(vt_ref[hd, ks], p.astype(BF))
            else:
                m0, l0 = carry[2 * h], carry[2 * h + 1]
                m = jnp.maximum(m0, jnp.max(s, axis=0, keepdims=True))
                p = jnp.exp(s - m)
                alpha = jnp.exp(m0 - m)
                l = l0 * alpha + jnp.sum(p, axis=0, keepdims=True)
                acc[hd, :] = acc[hd, :] * alpha + dot_nn(vt_ref[hd, ks], p.astype(BF))
            out += [m, l]
        return tuple(out)

    carry = block(b, None, True)
    carry = lax.fori_loop(0, b, lambda kb, c: block(kb, c, False), carry)
    for h in range(heads):
        hd = slice(h * HEAD, (h + 1) * HEAD)
        m, l = carry[2 * h], carry[2 * h + 1]
        acc[hd, :] = acc[hd, :] / l
        lse_ref[h:h + 1, :] = m + jnp.log(l)
    o = acc[...]
    ot_ref[...] = o.astype(BF)
    zp_ref[0] = dot_nn(o.T.astype(BF), wo_ref[...]).astype(BF)


def attn_fwd_call(chunk, chunks, perm, qt, k4, vt, wo):
    dims, length = qt.shape
    heads = dims // HEAD
    n = length // (chunks * QB)
    return pl.pallas_call(
        functools.partial(attn_fwd_kernel, chunk, chunks),
        grid_spec=pltpu.PrefetchScalarGridSpec(
            num_scalar_prefetch=1, grid=(n,),
            in_specs=[
                pl.BlockSpec((dims, QB), lambda t, p: (0, chunks * t + chunk)),
                whole(k4.shape), whole(vt.shape), whole(wo.shape)],
            out_specs=[
                pl.BlockSpec((1, QB, wo.shape[1]), lambda t, p: (p[t], 0, 0)),
                pl.BlockSpec((dims, QB), lambda t, p: (0, t)),
                pl.BlockSpec((heads, QB), lambda t, p: (0, t)),
            ],
            scratch_shapes=[pltpu.VMEM((dims, QB), F32)],
        ),
        out_shape=[
            jax.ShapeDtypeStruct((n, QB, wo.shape[1]), BF),
            jax.ShapeDtypeStruct((dims, n * QB), BF),
            jax.ShapeDtypeStruct((heads, n * QB), F32),
        ],
        compiler_params=params(),
    )(perm, qt, k4, vt, wo)


def attn_bwd_kernel(chunk, chunks, perm, dz_ref, wo_ref, qt_ref, k4_ref, kt_ref, v4_ref, ot_ref, lse_ref,
                    cos_ref, sin_ref, *rest):
    if chunk == 0:
        dq_ref, dk_ref, dv_ref, gwo_ref, acc, dot_ref, dl_ref = rest
    else:
        dk0, dv0, gwo0, dq_ref, dk_ref, dv_ref, gwo_ref, acc, dot_ref, dl_ref = rest
    t = pl.program_id(0)
    b = chunks * t + chunk
    heads = qt_ref.shape[0] // HEAD
    half = HEAD // 2

    @pl.when(t == 0)
    def _():
        if chunk == 0:
            dk_ref[...] = jnp.zeros_like(dk_ref)
            dv_ref[...] = jnp.zeros_like(dv_ref)
            gwo_ref[...] = jnp.zeros_like(gwo_ref)
        else:
            dk_ref[...] = dk0[...]
            dv_ref[...] = dv0[...]
            gwo_ref[...] = gwo0[...]

    dz = dz_ref[0]
    do_t = dot_nt(wo_ref[...], dz).astype(BF)
    dot_ref[...] = do_t
    gwo_ref[...] += dot_nn(ot_ref[...], dz)
    prod = do_t.astype(F32) * ot_ref[...].astype(F32)
    for h in range(heads):
        dl_ref[h:h + 1, :] = jnp.sum(prod[h * HEAD:(h + 1) * HEAD], axis=0, keepdims=True)
    rows = lax.broadcasted_iota(jnp.int32, (QB, QB), 0)
    cols = lax.broadcasted_iota(jnp.int32, (QB, QB), 1)
    seen = rows <= cols

    def block(kb, first):
        ks = pl.ds(pl.multiple_of(kb * QB, QB), QB)
        for h in range(heads):
            hd = slice(h * HEAD, (h + 1) * HEAD)
            q, do = qt_ref[hd, :], dot_ref[hd, :]
            s = dot_nn(k4_ref[h, ks, :], q)
            p = jnp.exp(s - lse_ref[h:h + 1, :])
            if first:
                p = jnp.where(seen, p, 0.0)
            dp = dot_nn(v4_ref[h, ks, :], do)
            ds = (p * (dp - dl_ref[h:h + 1, :])).astype(BF)
            dv_ref[hd, ks] += dot_nt(do, p.astype(BF))
            dk_ref[hd, ks] += dot_nt(q, ds)
            dq = dot_nn(kt_ref[hd, ks], ds)
            if first:
                acc[hd, :] = dq
            else:
                acc[hd, :] += dq

    block(b, True)

    def step(kb, c):
        block(kb, False)
        return c

    lax.fori_loop(0, b, step, 0)
    cos, sin = cos_ref[...], sin_ref[...]
    for h in range(heads):
        lo = slice(h * HEAD, h * HEAD + half)
        hi = slice(h * HEAD + half, (h + 1) * HEAD)
        g1, g2 = acc[lo, :] * 0.125, acc[hi, :] * 0.125
        dq_ref[lo, :] = (g1 * cos + g2 * sin).astype(BF)
        dq_ref[hi, :] = (g2 * cos - g1 * sin).astype(BF)


def attn_bwd_call(chunk, chunks, perm, dz, wo, qt, k4, kt, v4, ot, lse, cos_t, sin_t, prev=()):
    dims, length = qt.shape
    heads = dims // HEAD
    n = length // (chunks * QB)
    qb = pl.BlockSpec((dims, QB), lambda t, p: (0, chunks * t + chunk))
    tab = pl.BlockSpec((HEAD // 2, QB), lambda t, p: (0, chunks * t + chunk))
    tb = pl.BlockSpec((dims, QB), lambda t, p: (0, t))
    full = whole((dims, length))
    in_specs = [
        pl.BlockSpec((1, QB, wo.shape[1]), lambda t, p: (p[t], 0, 0)),
        whole(wo.shape), qb, whole(k4.shape), full, whole(v4.shape), tb,
        pl.BlockSpec((heads, QB), lambda t, p: (0, t)), tab, tab]
    if chunk:
        in_specs += [full, full, whole(wo.shape)]
    aliases = {11: 1, 12: 2, 13: 3} if chunk else {}
    return pl.pallas_call(
        functools.partial(attn_bwd_kernel, chunk, chunks),
        grid_spec=pltpu.PrefetchScalarGridSpec(
            num_scalar_prefetch=1, grid=(n,),
            in_specs=in_specs,
            out_specs=[tb, full, full, whole(wo.shape)],
            scratch_shapes=[pltpu.VMEM((dims, QB), F32), pltpu.VMEM((dims, QB), BF), pltpu.VMEM((8, QB), F32)],
        ),
        out_shape=[
            jax.ShapeDtypeStruct((dims, n * QB), BF),
            jax.ShapeDtypeStruct((dims, length), F32),
            jax.ShapeDtypeStruct((dims, length), F32),
            jax.ShapeDtypeStruct(wo.shape, F32),
        ],
        input_output_aliases=aliases,
        compiler_params=params(),
    )(perm, dz, wo, qt, k4, kt, v4, ot, lse, cos_t, sin_t, *prev)


def qkv_bwd_kernel(chunks, perm, *refs):
    dqs = refs[:chunks]
    dk_ref, dv_ref, a_ref, w_ref, cos_ref, sin_ref, da_ref, gw_ref, dx = refs[chunks:]
    t = pl.program_id(0)
    dims = dk_ref.shape[0]
    half = HEAD // 2
    for i, r in enumerate(dqs):
        dx[0:dims, i * QB:(i + 1) * QB] = r[...]
    cos, sin = cos_ref[...], sin_ref[...]
    for h in range(dims // HEAD):
        lo = slice(h * HEAD, h * HEAD + half)
        hi = slice(h * HEAD + half, (h + 1) * HEAD)
        g1, g2 = dk_ref[lo, :], dk_ref[hi, :]
        dx[dims + h * HEAD:dims + h * HEAD + half, :] = (g1 * cos + g2 * sin).astype(BF)
        dx[dims + h * HEAD + half:dims + (h + 1) * HEAD, :] = (g2 * cos - g1 * sin).astype(BF)
    dx[2 * dims:, :] = dv_ref[...].astype(BF)
    grad = dx[...]
    da_ref[0] = dot_nn(grad.astype(F32).T.astype(BF), w_ref[...]).astype(BF)
    part = dot_nn(grad, a_ref[0])

    @pl.when(t == 0)
    def _():
        gw_ref[...] = part

    @pl.when(t > 0)
    def _():
        gw_ref[...] += part


def qkv_bwd_call(perm, dqs, dk, dv, a_rel, w, cos_t, sin_t):
    chunks = len(dqs)
    n, rows, width = a_rel.shape
    dims = dk.shape[0]
    return pl.pallas_call(
        functools.partial(qkv_bwd_kernel, chunks),
        grid_spec=pltpu.PrefetchScalarGridSpec(
            num_scalar_prefetch=1, grid=(n,),
            in_specs=[pl.BlockSpec((dims, QB), lambda t, p: (0, t))] * chunks + [
                pl.BlockSpec((dims, rows), lambda t, p: (0, t)),
                pl.BlockSpec((dims, rows), lambda t, p: (0, t)),
                pl.BlockSpec((1, rows, width), lambda t, p: (p[t], 0, 0)),
                whole(w.shape),
                pl.BlockSpec((HEAD // 2, rows), lambda t, p: (0, t)),
                pl.BlockSpec((HEAD // 2, rows), lambda t, p: (0, t)),
            ],
            out_specs=[pl.BlockSpec((1, rows, width), lambda t, p: (p[t], 0, 0)), whole(w.shape)],
            scratch_shapes=[pltpu.VMEM((3 * dims, rows), BF)],
        ),
        out_shape=[
            jax.ShapeDtypeStruct(a_rel.shape, BF),
            jax.ShapeDtypeStruct(w.shape, F32),
        ],
        compiler_params=params(),
    )(perm, *dqs, dk, dv, a_rel, w, cos_t, sin_t)


def mlp_fwd_kernel(c_ref, w1_ref, w2_ref, r_ref, g_ref, m_ref):
    u = dot_nt(c_ref[0], w1_ref[...])
    cdf = 0.5 * (1.0 + lax.erf(u * 0.7071067811865476))
    r = (u * cdf).astype(BF)
    r_ref[0] = r
    g_ref[0] = (cdf + u * (0.3989422804014327 * jnp.exp(-0.5 * u * u))).astype(BF)
    m_ref[0] = dot_nn(r, w2_ref[...]).astype(BF)


def mlp_fwd_call(c, w1, w2):
    n, rows, width = c.shape
    hid = w1.shape[0]
    blk = pl.BlockSpec((1, rows, width), lambda k: (k, 0, 0))
    hb = pl.BlockSpec((1, rows, hid), lambda k: (k, 0, 0))
    return pl.pallas_call(
        mlp_fwd_kernel, grid=(n,),
        in_specs=[blk, whole(w1.shape), whole(w2.shape)],
        out_specs=[hb, hb, blk],
        out_shape=[jax.ShapeDtypeStruct((n, rows, hid), BF)] * 2 + [jax.ShapeDtypeStruct(c.shape, BF)],
        compiler_params=params(),
    )(c, w1, w2)


def mlp_bwd_kernel(dm_ref, g_ref, w1_ref, w2_ref, du_ref, dc_ref):
    dr = dot_nt(dm_ref[0], w2_ref[...])
    du = (dr * g_ref[0].astype(F32)).astype(BF)
    du_ref[0] = du
    dc_ref[0] = dot_nn(du, w1_ref[...]).astype(BF)


def mlp_bwd_call(dm, g, w1, w2):
    n, rows, width = dm.shape
    hid = w1.shape[0]
    blk = pl.BlockSpec((1, rows, width), lambda k: (k, 0, 0))
    hb = pl.BlockSpec((1, rows, hid), lambda k: (k, 0, 0))
    return pl.pallas_call(
        mlp_bwd_kernel, grid=(n,),
        in_specs=[blk, hb, whole(w1.shape), whole(w2.shape)],
        out_specs=[hb, blk],
        out_shape=[jax.ShapeDtypeStruct((n, rows, hid), BF), jax.ShapeDtypeStruct(dm.shape, BF)],
        compiler_params=params(),
    )(dm, g, w1, w2)


def rotary_tables_t(length):
    half = HEAD // 2
    frequency = 10000.0 ** (-jnp.arange(half, dtype=F32) / half)
    angles = frequency[:, None] * jnp.arange(length, dtype=F32)[None, :]
    return jnp.cos(angles), jnp.sin(angles)


def centre(v):
    mean = jnp.mean(v, axis=-1, keepdims=True)
    vc = v - mean
    s = lax.rsqrt(jnp.mean(vc * vc, axis=-1, keepdims=True) + EPS)
    return vc * s, s


def norm_back(n, s, y, gain):
    dn = y * gain
    return s * (dn - jnp.mean(dn, axis=-1, keepdims=True) - n * jnp.mean(dn * n, axis=-1, keepdims=True))


def total(parts):
    out = parts[0].astype(F32)
    for p in parts[1:]:
        out = out + p.astype(F32)
    return out


def residual_kernel(p0, p1, p2, x_ref, norms, z_ref, h_ref, c_ref):
    z = total([p0[...], p1[...], p2[...]])
    z_ref[...] = z
    n, _ = centre(z)
    h = x_ref[...].astype(F32) + n * norms[2:3, :] + norms[3:4, :]
    h_ref[...] = h
    n, _ = centre(h)
    c_ref[...] = (n * norms[4:5, :] + norms[5:6, :]).astype(BF)


def rows_call(kernel, outs, *args):
    return pl.pallas_call(kernel, out_shape=outs, compiler_params=params())(*args)


def residual_call(parts, x, norms):
    sh = jax.ShapeDtypeStruct(x.shape, F32)
    return rows_call(residual_kernel, [sh, sh, jax.ShapeDtypeStruct(x.shape, BF)], *parts, x, norms)


def out_kernel(p0, p1, p2, h_ref, ct_ref, wt_ref, norms, lo_ref, dm_ref, dn_ref):
    m = total([p0[...], p1[...], p2[...]])
    n, s = centre(m)
    lo_ref[...] = (h_ref[...] + n * norms[6:7, :] + norms[7:8, :]).astype(BF)
    e = ct_ref[...].astype(F32) * wt_ref[...]
    dm_ref[...] = norm_back(n, s, e, norms[6:7, :]).astype(BF)
    dn_ref[0:1, :] = jnp.sum(e * n, axis=0, keepdims=True)
    dn_ref[1:2, :] = jnp.sum(e, axis=0, keepdims=True)


def out_call(parts, h, ct, wt, norms):
    sh = jax.ShapeDtypeStruct(h.shape, BF)
    return rows_call(out_kernel, [sh, sh, jax.ShapeDtypeStruct((2, h.shape[1]), F32)], *parts, h, ct, wt, norms)


def mid_kernel(p0, p1, p2, h_ref, z_ref, ct_ref, wt_ref, norms, dh_ref, dz_ref, dn_ref):
    dc = total([p0[...], p1[...], p2[...]])
    n3, s3 = centre(h_ref[...])
    dh = ct_ref[...].astype(F32) * wt_ref[...] + norm_back(n3, s3, dc, norms[4:5, :])
    dh_ref[...] = dh
    n2, s2 = centre(z_ref[...])
    dz_ref[...] = norm_back(n2, s2, dh, norms[2:3, :]).astype(BF)
    dn_ref[0:1, :] = jnp.sum(dh * n2, axis=0, keepdims=True)
    dn_ref[1:2, :] = jnp.sum(dh, axis=0, keepdims=True)
    dn_ref[2:3, :] = jnp.sum(dc * n3, axis=0, keepdims=True)
    dn_ref[3:4, :] = jnp.sum(dc, axis=0, keepdims=True)


def mid_call(parts, h, z, ct, wt, norms):
    return rows_call(mid_kernel, [
        jax.ShapeDtypeStruct(h.shape, F32), jax.ShapeDtypeStruct(h.shape, BF),
        jax.ShapeDtypeStruct((4, h.shape[1]), F32)], *parts, h, z, ct, wt, norms)


def in_kernel(p0, p1, p2, x_ref, dh_ref, norms, dx_ref, dn_ref):
    da = total([p0[...], p1[...], p2[...]])
    n1, s1 = centre(x_ref[...].astype(F32))
    dx_ref[...] = dh_ref[...] + norm_back(n1, s1, da, norms[0:1, :])
    dn_ref[0:1, :] = jnp.sum(da * n1, axis=0, keepdims=True)
    dn_ref[1:2, :] = jnp.sum(da, axis=0, keepdims=True)


def in_call(parts, x, dh, norms):
    return rows_call(in_kernel, [
        jax.ShapeDtypeStruct(x.shape, F32), jax.ShapeDtypeStruct((2, x.shape[1]), F32)], *parts, x, dh, norms)


ADAM_STEP = 5
CHUNKS = 2
TOP = [(0, 1), (1, 0), (2, 3), (3, 2)]
SIDE = [(0, 2), (1, 3), (2, 0), (3, 1)]
RINGS = {8: [0, 2, 4, 6, 7, 5, 3, 1]}


def to_core(v):
    return lax.ppermute(v, "tensor", TOP)


def to_chip(v):
    return lax.ppermute(v, "tensor", SIDE)


def gather_rel(own):
    side = to_chip(own)
    both = to_core(jnp.stack([own, side]))
    return jnp.stack([own, both[0], side, both[1]])


def scatter_rel(keep, send):
    got = to_core(send)
    side = to_chip((keep[1].astype(F32) + got[1].astype(F32)).astype(BF))
    return keep[0], got[0], side


def reorder(v, me):
    v = jnp.where(me % 2 == 1, jnp.stack([v[1], v[0], v[3], v[2]]), v)
    return jnp.where(me // 2 == 1, jnp.stack([v[2], v[3], v[0], v[1]]), v)


def ring_steps(ring):
    n = len(ring)
    right = [(ring[i], ring[(i + 1) % n]) for i in range(n)]
    return right, [(b, a) for a, b in right]


def ring_at(ring, where):
    where = where % len(ring)
    return sum(jnp.where(where == i, d, 0) for i, d in enumerate(ring))


def place_of(ring):
    me = lax.axis_index("dp")
    return sum(jnp.where(me == d, i, 0) for i, d in enumerate(ring)), lambda where: ring_at(ring, where)


def pick(assign, slots):
    return (assign[:, None] == slots[None, :]).astype(BF)


def owner_rows(shard, assign):
    owners = lax.axis_size("dp")
    cap, width = shard.shape
    ring = RINGS.get(owners)
    if ring is None:
        return lax.all_gather(shard, "dp", axis=0, tiled=True)[assign]
    right, left = ring_steps(ring)
    me, order = place_of(ring)
    iota = jnp.arange(cap, dtype=jnp.int32)
    half = width // 2

    def part(v, where):
        return dot_nn(pick(assign, order(where) * cap + iota), v).astype(BF)

    a, b = shard[:, :half], shard[:, half:]
    rows_a, rows_b = part(a, me), part(b, me)
    for s in range(1, owners):
        a = lax.ppermute(a, "dp", right)
        b = lax.ppermute(b, "dp", left)
        rows_a = rows_a + part(a, me - s + owners)
        rows_b = rows_b + part(b, me + s)
    return jnp.concatenate([rows_a, rows_b], axis=1)


def owner_sums(grads, assign, cap):
    owners = lax.axis_size("dp")
    ring = RINGS.get(owners)
    width = grads.shape[1]
    if ring is None:
        pad = -cap % 8
        slots = jnp.arange(owners * (cap + pad), dtype=jnp.int32)
        slots = jnp.where(slots % (cap + pad) < cap, slots // (cap + pad) * cap + slots % (cap + pad), -1)
        bucket = dot_nn(pick(slots, assign), grads).astype(BF)
        return lax.psum_scatter(bucket, "dp", scatter_dimension=0, tiled=True)[:cap].astype(F32)
    right, left = ring_steps(ring)
    me, order = place_of(ring)
    block = cap + (-cap % 16)
    iota = jnp.arange(block, dtype=jnp.int32)
    own = jnp.where(iota < cap, iota, -(1 << 20))
    half = width // 2
    hops = jnp.arange(1, owners + 1, dtype=jnp.int32)

    def bucket(where, v):
        slots = (order(where)[:, None] * cap + own[None, :]).reshape(-1)
        return dot_nn(pick(slots, assign), v).astype(BF).reshape(owners, block, half)

    mine_a = bucket(me - hops + owners, grads[:, :half])
    mine_b = bucket(me + hops, grads[:, half:])
    a, b = mine_a[0], mine_b[0]
    for s in range(1, owners):
        a = lax.ppermute(a, "dp", right).astype(F32) + mine_a[s].astype(F32)
        b = lax.ppermute(b, "dp", left).astype(F32) + mine_b[s].astype(F32)
        if s < owners - 1:
            a, b = a.astype(BF), b.astype(BF)
    return jnp.concatenate([a, b], axis=1)[:cap]


def owner_sums_xla(grads, assign, cap):
    owners = lax.axis_size("dp")
    block = cap + (-cap % 8)
    slots = jnp.arange(owners * block, dtype=jnp.int32)
    slots = jnp.where(slots % block < cap, slots // block * cap + slots % block, -1)
    bucket = dot_nn(pick(slots, assign), grads).astype(BF)
    return lax.psum_scatter(bucket, "dp", scatter_dimension=0, tiled=True)[:cap].astype(F32)


def adamw(master, moment, square, gradient, rate):
    moment = 0.5 * moment + 0.5 * gradient
    square = 0.5 * square + 0.5 * gradient * gradient
    m_hat = moment / (1.0 - 0.5**ADAM_STEP)
    s_hat = square / (1.0 - 0.5**ADAM_STEP)
    update = m_hat / (jnp.sqrt(s_hat) + 1e-8) + 0.1 * master
    return master - rate * update, moment, square


def split_rel(v):
    return jnp.stack([v[0], v[2]]), jnp.stack([v[1], v[3]])


def on_device(tokens, cotangent, group_ids, assign_attn, assign_mlp,
              master_attn, moment_attn, square_attn, master_mlp, moment_mlp, square_mlp):
    owners = lax.axis_size("dp")
    tensor = lax.axis_size("tensor")
    rows_here, width = tokens.shape
    length = rows_here * tensor
    me = lax.axis_index("tensor")
    perm = jnp.arange(tensor, dtype=jnp.int32) ^ me
    head_dims = width // tensor
    cap_attn, cap_mlp = master_attn.shape[1], master_mlp.shape[1]
    hidden = assign_mlp.shape[0] // 2
    part_rows = rows_here // CHUNKS
    cuts = [slice(j * part_rows, (j + 1) * part_rows) for j in range(CHUNKS)]

    attn_rows = owner_rows(master_attn[0].astype(BF), assign_attn)
    x_rel = gather_rel(tokens)
    block = cap_mlp + (-cap_mlp % 16)
    mlp_all = lax.all_gather(jnp.pad(master_mlp[0].astype(BF), ((0, block - cap_mlp), (0, 0))), "dp", axis=0, tiled=True)
    cos_t, sin_t = rotary_tables_t(length)
    weight = (0.5 + 0.5 * group_ids.astype(F32))[:, None]

    own_norms = attn_rows[4 * head_dims:]
    norms = reorder(gather_rel(own_norms), me).reshape(2 * tensor, width).astype(F32)
    w_qkv = attn_rows[:3 * head_dims]
    w_out = attn_rows[3 * head_dims:4 * head_dims]

    a_rel, qt, kt, vt, k4, v4 = qkv_call(perm, x_rel, w_qkv, norms, cos_t, sin_t)
    places = assign_mlp // cap_mlp * block + assign_mlp % cap_mlp
    mlp_rows = dot_nn(pick(places, jnp.arange(owners * block, dtype=jnp.int32)), mlp_all).astype(BF)
    w_up, w_down = mlp_rows[:hidden], mlp_rows[hidden:]

    saved = []
    for j in range(CHUNKS):
        zp, ot, lse = attn_fwd_call(j, CHUNKS, perm, qt, k4, vt, w_out)
        saved.append((zp, ot, lse))
    outs, dnorm4 = [], 0.0
    state = []
    for j in range(CHUNKS):
        zp, ot, lse = saved[j]
        z, h, c = residual_call(scatter_rel(*split_rel(zp)), tokens[cuts[j]], norms)
        c_rel = gather_rel(c)
        r, g, mp = mlp_fwd_call(c_rel, w_up, w_down)
        lo, dm, dn4 = out_call(scatter_rel(*split_rel(mp)), h, cotangent[cuts[j]], weight[cuts[j]], norms)
        outs.append(lo)
        dnorm4 = dnorm4 + dn4
        dm_rel = gather_rel(dm)
        state.append((z, h, c_rel, r, g, dm_rel))
    dhs, dzs = [], []
    dnorm23 = 0.0
    grad_up, grad_down = 0.0, 0.0
    for j in range(CHUNKS):
        z, h, c_rel, r, g, dm_rel = state[j]
        du, dcp = mlp_bwd_call(dm_rel, g, w_up, w_down)
        dh, dz, dn = mid_call(scatter_rel(*split_rel(dcp)), h, z, cotangent[cuts[j]], weight[cuts[j]], norms)
        dhs.append(dh)
        dnorm23 = dnorm23 + dn
        dzs.append(gather_rel(dz))
        toks = (((0, 1), (0, 1)), ((), ()))
        grad_down = grad_down + lax.dot_general(r, dm_rel, toks, preferred_element_type=F32)
        grad_up = grad_up + lax.dot_general(du, c_rel, toks, preferred_element_type=F32)
    mlp_grads = jnp.concatenate([grad_up.astype(BF), grad_down.astype(BF)], axis=0)
    mlp_sum = owner_sums_xla(mlp_grads, assign_mlp, cap_mlp)

    prev, dqs = (), []
    for j in range(CHUNKS):
        _, ot, lse = saved[j]
        dq, *prev = attn_bwd_call(j, CHUNKS, perm, dzs[j], w_out, qt, k4, kt, v4, ot, lse, cos_t, sin_t, tuple(prev))
        dqs.append(dq)
    dk, dv, grad_out = prev
    dap, grad_qkv = qkv_bwd_call(perm, dqs, dk, dv, a_rel, w_qkv, cos_t, sin_t)
    attn_grads = jnp.concatenate([grad_qkv.astype(BF), grad_out.astype(BF)], axis=0)
    attn_sum = owner_sums(attn_grads, assign_attn[:4 * head_dims], cap_attn)

    dx, dn1 = in_call(scatter_rel(*split_rel(dap)), tokens, jnp.concatenate(dhs, axis=0), norms)
    terms = jnp.concatenate([dn1, dnorm23, dnorm4], axis=0).reshape(tensor, 2, width)
    terms = reorder(terms, me)
    got = to_core(jnp.stack([terms[1], terms[3]]))
    norm_sum = terms[0] + got[0] + to_chip(terms[2] + got[1])
    bit = 1
    while bit < owners:
        norm_sum = norm_sum + lax.ppermute(norm_sum, "dp", [(i, i ^ bit) for i in range(owners)])
        bit *= 2

    owner = lax.axis_index("dp")
    slots_a = owner * cap_attn + jnp.arange(cap_attn, dtype=jnp.int32)
    slots_m = owner * cap_mlp + jnp.arange(cap_mlp, dtype=jnp.int32)
    for i in range(2):
        attn_sum = attn_sum + jnp.where(slots_a == assign_attn[4 * head_dims + i], 1.0, 0.0)[:, None] * norm_sum[i][None]

    def named(slots, part):
        return jnp.any(slots[:, None] == part[None, :], axis=1)

    rate_a = jnp.where(named(slots_a, assign_attn[4 * head_dims:]), 0.2,
                       jnp.where(named(slots_a, assign_attn[3 * head_dims:4 * head_dims]), 0.4, 0.06)).astype(F32)
    rate_m = jnp.where(named(slots_m, assign_mlp[hidden:]), 0.03, 0.06).astype(F32)
    new_a = adamw(master_attn, moment_attn, square_attn, attn_sum[None], rate_a[None, :, None])
    new_m = adamw(master_mlp, moment_mlp, square_mlp, mlp_sum[None], rate_m[None, :, None])
    return (jnp.concatenate(outs, axis=0), dx, *new_a, *new_m)


def solution(mesh):
    tok = P(("dp", "tensor"), None)
    par = P("tensor", "dp", None)
    return jax.shard_map(
        on_device, mesh=mesh,
        in_specs=(tok, tok, P(("dp", "tensor")), P(), P(), par, par, par, par, par, par),
        out_specs=(tok, tok, par, par, par, par, par, par),
        check_vma=False,
    )
```

```python
import functools
import jax
import jax.numpy as jnp
from jax import lax
from jax.sharding import PartitionSpec as P
from jax.experimental import pallas as pl
from jax.experimental.pallas import tpu as pltpu

BF = jnp.bfloat16
F32 = jnp.float32
EPS = 1e-5
HEAD = 64
LANES = 128
QB = 256
CHUNKS = 2
ADAM_STEP = 5
LIMIT = 48 * 1024 * 1024


def dot_nn(a, b):
    return lax.dot_general(a, b, (((1,), (0,)), ((), ())), preferred_element_type=F32)


def dot_nt(a, b):
    return lax.dot_general(a, b, (((1,), (1,)), ((), ())), preferred_element_type=F32)


def params():
    return pltpu.CompilerParams(vmem_limit_bytes=LIMIT)


def cost(us):
    return pl.CostEstimate(flops=int(us * 1e9), bytes_accessed=int(us * 3e6), transcendentals=0)


def whole(shape, at=None):
    at = at or (0,) * len(shape)
    return pl.BlockSpec(shape, lambda *_: at)


def shape(dims, dtype):
    return jax.ShapeDtypeStruct(dims, dtype)


def choose(index, refs, into):
    for i, r in enumerate(refs):
        @pl.when(index == i)
        def _():
            into[...] = r[...]


def spread(index, refs, value):
    for i, r in enumerate(refs):
        @pl.when(index == i)
        def _():
            r[...] = value


def centre(v):
    mean = jnp.mean(v, axis=-1, keepdims=True)
    vc = v - mean
    s = lax.rsqrt(jnp.mean(vc * vc, axis=-1, keepdims=True) + EPS)
    return vc * s, s


def norm_back(n, s, y, gain):
    dn = y * gain
    return s * (dn - jnp.mean(dn, axis=-1, keepdims=True) - n * jnp.mean(dn * n, axis=-1, keepdims=True))


def total(parts):
    return sum(p[...].astype(F32) for p in parts)


def rows_call(kernel, outs, *args):
    return pl.pallas_call(kernel, out_shape=outs, compiler_params=params(), cost_estimate=cost(2.5))(*args)


def input_kernel(*refs):
    xs, norms, a_ref, cur = refs[:-3], refs[-3], refs[-2], refs[-1]
    choose(pl.program_id(0), xs, cur)
    n, _ = centre(cur[...].astype(F32))
    a_ref[0] = (n * norms[0:1, :] + norms[1:2, :]).astype(BF)


def input_call(xs, norms):
    rows, width = xs[0].shape
    return pl.pallas_call(
        input_kernel, grid=(len(xs),),
        in_specs=[whole(x.shape) for x in xs] + [whole(norms.shape)],
        out_specs=pl.BlockSpec((1, rows, width), lambda k: (k, 0, 0)),
        out_shape=shape((len(xs), rows, width), BF),
        scratch_shapes=[pltpu.VMEM((rows, width), BF)],
        compiler_params=params(), cost_estimate=cost(4),
    )(*xs, norms)


def residual_kernel(p0, p1, p2, x_ref, norms, z_ref, h_ref, c_ref):
    z = total([p0, p1, p2])
    z_ref[...] = z
    n, _ = centre(z)
    h = x_ref[...].astype(F32) + n * norms[2:3, :] + norms[3:4, :]
    h_ref[...] = h
    n, _ = centre(h)
    c_ref[...] = (n * norms[4:5, :] + norms[5:6, :]).astype(BF)


def residual_call(parts, x, norms):
    return rows_call(residual_kernel, [shape(x.shape, F32), shape(x.shape, F32), shape(x.shape, BF)], *parts, x, norms)


def out_kernel(p0, p1, p2, h_ref, ct_ref, wt_ref, norms, lo_ref, dm_ref, dn_ref):
    n, s = centre(total([p0, p1, p2]))
    lo_ref[...] = (h_ref[...] + n * norms[6:7, :] + norms[7:8, :]).astype(BF)
    e = ct_ref[...].astype(F32) * wt_ref[...]
    dm_ref[...] = norm_back(n, s, e, norms[6:7, :]).astype(BF)
    dn_ref[0:1, :] = jnp.sum(e * n, axis=0, keepdims=True)
    dn_ref[1:2, :] = jnp.sum(e, axis=0, keepdims=True)


def out_call(parts, h, ct, wt, norms):
    return rows_call(out_kernel, [shape(h.shape, BF), shape(h.shape, BF), shape((2, h.shape[1]), F32)], *parts, h, ct, wt, norms)


def mid_kernel(p0, p1, p2, h_ref, z_ref, ct_ref, wt_ref, norms, dh_ref, dz_ref, dn_ref):
    dc = total([p0, p1, p2])
    n3, s3 = centre(h_ref[...])
    dh = ct_ref[...].astype(F32) * wt_ref[...] + norm_back(n3, s3, dc, norms[4:5, :])
    dh_ref[...] = dh
    n2, s2 = centre(z_ref[...])
    dz_ref[...] = norm_back(n2, s2, dh, norms[2:3, :]).astype(BF)
    dn_ref[0:1, :] = jnp.sum(dh * n2, axis=0, keepdims=True)
    dn_ref[1:2, :] = jnp.sum(dh, axis=0, keepdims=True)
    dn_ref[2:3, :] = jnp.sum(dc * n3, axis=0, keepdims=True)
    dn_ref[3:4, :] = jnp.sum(dc, axis=0, keepdims=True)


def mid_call(parts, h, z, ct, wt, norms):
    return rows_call(mid_kernel, [shape(h.shape, F32), shape(h.shape, BF), shape((4, h.shape[1]), F32)],
                     *parts, h, z, ct, wt, norms)


def last_kernel(p0, p1, p2, x_ref, dh_ref, norms, dx_ref, dn_ref):
    da = total([p0, p1, p2])
    n1, s1 = centre(x_ref[...].astype(F32))
    dx_ref[...] = dh_ref[...] + norm_back(n1, s1, da, norms[0:1, :])
    dn_ref[0:1, :] = jnp.sum(da * n1, axis=0, keepdims=True)
    dn_ref[1:2, :] = jnp.sum(da, axis=0, keepdims=True)


def last_call(parts, x, dh, norms):
    return rows_call(last_kernel, [shape(x.shape, F32), shape((2, x.shape[1]), F32)], *parts, x, dh, norms)


def qkv_kernel(perm, a_ref, w_ref, cos_ref, sin_ref, qt_ref, kt_ref, vt_ref, k4_ref, v4_ref):
    a = a_ref[0]
    cos, sin = cos_ref[...], sin_ref[...]
    dims = qt_ref.shape[0]
    half = HEAD // 2
    for part in range(3):
        proj = dot_nt(w_ref[part * dims:(part + 1) * dims, :], a)
        for h in range(dims // HEAD):
            lo = slice(h * HEAD, h * HEAD + half)
            hi = slice(h * HEAD + half, (h + 1) * HEAD)
            hd = slice(h * HEAD, (h + 1) * HEAD)
            if part < 2:
                first, second = proj[lo], proj[hi]
                r1 = first * cos - second * sin
                r2 = second * cos + first * sin
                if part == 0:
                    qt_ref[lo, :] = (r1 * 0.125).astype(BF)
                    qt_ref[hi, :] = (r2 * 0.125).astype(BF)
                else:
                    full = jnp.concatenate([r1, r2], axis=0)
                    kt_ref[hd, :] = full.astype(BF)
                    k4_ref[h] = full.T.astype(BF)
            else:
                vt_ref[hd, :] = proj[hd].astype(BF)
                v4_ref[h] = proj[hd].T.astype(BF)


def qkv_call(perm, a_rel, w, cos_t, sin_t):
    n, rows, width = a_rel.shape
    dims = w.shape[0] // 4
    heads = dims // HEAD
    length = n * rows
    tok = pl.BlockSpec((dims, rows), lambda k, p: (0, p[k]))
    hd = pl.BlockSpec((heads, rows, HEAD), lambda k, p: (0, p[k], 0))
    tab = pl.BlockSpec((HEAD // 2, rows), lambda k, p: (0, p[k]))
    return pl.pallas_call(
        qkv_kernel,
        grid_spec=pltpu.PrefetchScalarGridSpec(
            num_scalar_prefetch=1, grid=(n,),
            in_specs=[pl.BlockSpec((1, rows, width), lambda k, p: (k, 0, 0)), whole((3 * dims, width)), tab, tab],
            out_specs=[tok, tok, tok, hd, hd],
        ),
        out_shape=[shape((dims, length), BF)] * 3 + [shape((heads, length, HEAD), BF)] * 2,
        compiler_params=params(), cost_estimate=cost(9),
    )(perm, a_rel, w, cos_t, sin_t)


def visible(chunk, diag):
    return (lax.broadcasted_iota(jnp.int32, (diag, QB), 0)
            <= lax.broadcasted_iota(jnp.int32, (diag, QB), 1) + chunk * QB)


def key_spans(n, wide, diag):
    return ([pl.ds(0, n * wide)] if n else []) + [pl.ds(n * wide, diag)]


def pipelined(heads, first, second, third):
    ahead, behind = first(0), None
    for h in range(heads):
        now = ahead
        if h + 1 < heads:
            ahead = first(h + 1)
        done = second(h, now)
        if behind is not None:
            third(h - 1, behind)
        behind = done
    third(heads - 1, behind)


def attn_fwd_kernel(chunk, chunks, count, perm, qt_ref, k4_ref, vt_ref, wo_ref, *rest):
    zs, (ot_ref, lse_ref, acc) = rest[:count], rest[count:]
    t = pl.program_id(0)
    heads = qt_ref.shape[0] // HEAD
    diag = (chunk + 1) * QB
    seen = visible(chunk, diag)
    hd = [slice(h * HEAD, (h + 1) * HEAD) for h in range(heads)]

    def one_row(n):
        spans = key_spans(n, chunks * QB, diag)

        def scores(h):
            return [dot_nn(k4_ref[h, ks, :], qt_ref[hd[h], :]) for ks in spans]

        def soft(h, s):
            s = s[:-1] + [jnp.where(seen, s[-1], -1e30)]
            m = functools.reduce(jnp.maximum, [jnp.max(v, axis=0, keepdims=True) for v in s])
            p = [jnp.exp(v - m) for v in s]
            l = sum(jnp.sum(v, axis=0, keepdims=True) for v in p)
            lse_ref[h:h + 1, :] = m + jnp.log(l)
            return [v.astype(BF) for v in p], l

        def attend(h, done):
            acc[hd[h], :] = sum(dot_nn(vt_ref[hd[h], ks], v) for ks, v in zip(spans, done[0])) / done[1]

        pipelined(heads, scores, soft, attend)

    for n in range(count):
        pl.when(t == n)(functools.partial(one_row, n))
    o = acc[...]
    ot_ref[...] = o.astype(BF)
    spread(perm[t], zs, dot_nn(o.T.astype(BF), wo_ref[...]).astype(BF))


def attn_fwd_call(chunk, chunks, perm, qt, k4, vt, w):
    dims, length = qt.shape
    width = w.shape[1]
    heads = dims // HEAD
    n = length // (chunks * QB)
    return pl.pallas_call(
        functools.partial(attn_fwd_kernel, chunk, chunks, n),
        grid_spec=pltpu.PrefetchScalarGridSpec(
            num_scalar_prefetch=1, grid=(n,),
            in_specs=[
                pl.BlockSpec((dims, QB), lambda t, p: (0, chunks * t + chunk)),
                whole(k4.shape), whole(vt.shape), whole((dims, width), (3, 0))],
            out_specs=[whole((QB, width))] * n + [
                pl.BlockSpec((dims, QB), lambda t, p: (0, t)), pl.BlockSpec((heads, QB), lambda t, p: (0, t))],
            scratch_shapes=[pltpu.VMEM((dims, QB), F32)],
        ),
        out_shape=[shape((QB, width), BF)] * n + [shape((dims, n * QB), BF), shape((heads, n * QB), F32)],
        compiler_params=params(), cost_estimate=cost(9.5 + 1.5 * chunk),
    )(perm, qt, k4, vt, w)


def attn_bwd_kernel(chunk, chunks, count, perm, *refs):
    dzs, refs = refs[:count], refs[count:]
    wo_ref, qt_ref, k4_ref, kt_ref, v4_ref, ot_ref, lse_ref, cos_ref, sin_ref = refs[:9]
    if chunk == 0:
        dq_ref, dk_ref, dv_ref, gwo_ref, acc, dot_ref, dl_ref, dz_ref = refs[9:]
    else:
        call, sall, dk0, dv0, gwo0, dq_ref, dkl_ref, dvl_ref, gwo_ref, acc, dot_ref, dl_ref, dz_ref, dk_ref, dv_ref = refs[9:]
    t = pl.program_id(0)
    heads = qt_ref.shape[0] // HEAD
    half = HEAD // 2
    diag = (chunk + 1) * QB
    seen = visible(chunk, diag)
    hd = [slice(h * HEAD, (h + 1) * HEAD) for h in range(heads)]

    @pl.when(t == 0)
    def _():
        if chunk == 0:
            dk_ref[...] = jnp.zeros_like(dk_ref)
            dv_ref[...] = jnp.zeros_like(dv_ref)
            gwo_ref[...] = jnp.zeros_like(gwo_ref)
        else:
            dk_ref[...] = dk0[...]
            dv_ref[...] = dv0[...]
            gwo_ref[...] = gwo0[...]

    choose(perm[t], dzs, dz_ref)
    dz = dz_ref[...]
    do_t = dot_nt(wo_ref[...], dz).astype(BF)
    dot_ref[...] = do_t
    prod = do_t.astype(F32) * ot_ref[...].astype(F32)
    for h in range(heads):
        dl_ref[h:h + 1, :] = jnp.sum(prod[hd[h]], axis=0, keepdims=True)

    def one_row(n):
        spans = key_spans(n, chunks * QB, diag)

        def scores(h):
            return [(dot_nn(k4_ref[h, ks, :], qt_ref[hd[h], :]), dot_nn(v4_ref[h, ks, :], dot_ref[hd[h], :])) for ks in spans]

        def soft(h, pairs):
            out = []
            for i, (s, dp) in enumerate(pairs):
                p = jnp.exp(s - lse_ref[h:h + 1, :])
                if i == len(pairs) - 1:
                    p = jnp.where(seen, p, 0.0)
                out.append((p.astype(BF), (p * (dp - dl_ref[h:h + 1, :])).astype(BF)))
            return out

        def back(h, pairs):
            q, do = qt_ref[hd[h], :], dot_ref[hd[h], :]
            dq = 0.0
            for ks, (p, ds) in zip(spans, pairs):
                dv_ref[hd[h], ks] += dot_nt(do, p)
                dk_ref[hd[h], ks] += dot_nt(q, ds)
                dq = dq + dot_nn(kt_ref[hd[h], ks], ds)
            acc[hd[h], :] = dq

        pipelined(heads, scores, soft, back)

    for n in range(count):
        pl.when(t == n)(functools.partial(one_row, n))
    gwo_ref[...] += dot_nn(ot_ref[...], dz)

    def unturn(src, cos, sin, scale, out):
        for h in range(heads):
            lo = slice(h * HEAD, h * HEAD + half)
            hi = slice(h * HEAD + half, (h + 1) * HEAD)
            g1, g2 = src[lo, :] * scale, src[hi, :] * scale
            out[lo, :] = (g1 * cos + g2 * sin).astype(BF)
            out[hi, :] = (g2 * cos - g1 * sin).astype(BF)

    unturn(acc, cos_ref[...], sin_ref[...], 0.125, dq_ref)
    if chunk == chunks - 1:
        @pl.when(t == count - 1)
        def _():
            unturn(dk_ref, call[...], sall[...], 1.0, dkl_ref)
            dvl_ref[...] = dv_ref[...].astype(BF)


def attn_bwd_call(chunk, chunks, perm, dzs, w, qt, k4, kt, v4, ot, lse, cos_t, sin_t, prev=()):
    dims, length = qt.shape
    width = w.shape[1]
    heads = dims // HEAD
    n = length // (chunks * QB)
    qb = pl.BlockSpec((dims, QB), lambda t, p: (0, chunks * t + chunk))
    tab = pl.BlockSpec((HEAD // 2, QB), lambda t, p: (0, chunks * t + chunk))
    tb = pl.BlockSpec((dims, QB), lambda t, p: (0, t))
    full, out_w = whole((dims, length)), whole((dims, width))
    in_specs = [whole((QB, width))] * n + [
        whole((dims, width), (3, 0)), qb, whole(k4.shape), full, whole(v4.shape), tb,
        pl.BlockSpec((heads, QB), lambda t, p: (0, t)), tab, tab]
    scratch = [pltpu.VMEM((dims, QB), F32), pltpu.VMEM((dims, QB), BF), pltpu.VMEM((8, QB), F32), pltpu.VMEM((QB, width), BF)]
    extra = ()
    kv = F32
    if chunk:
        in_specs += [whole(cos_t.shape), whole(sin_t.shape), full, full, out_w]
        scratch += [pltpu.VMEM((dims, length), F32)] * 2
        extra = (cos_t, sin_t)
        kv = BF
    return pl.pallas_call(
        functools.partial(attn_bwd_kernel, chunk, chunks, n),
        grid_spec=pltpu.PrefetchScalarGridSpec(
            num_scalar_prefetch=1, grid=(n,), in_specs=in_specs,
            out_specs=[tb, full, full, out_w],
            scratch_shapes=scratch,
        ),
        out_shape=[shape((dims, n * QB), BF), shape((dims, length), kv), shape((dims, length), kv), shape((dims, width), F32)],
        compiler_params=params(), cost_estimate=cost(18 + 4 * chunk),
    )(perm, *dzs, w, qt, k4, kt, v4, ot, lse, cos_t, sin_t, *extra, *prev)


def qkv_in_kernel(count, perm, dq_ref, dk_ref, dv_ref, w_ref, *rest):
    das, dx = rest[:count], rest[count]
    dims = dq_ref.shape[0]
    dx[0:dims, :] = dq_ref[...]
    dx[dims:2 * dims, :] = dk_ref[...]
    dx[2 * dims:, :] = dv_ref[...]
    grad = dx[...].astype(F32).T.astype(BF)
    spread(perm[pl.program_id(0)], das, dot_nn(grad, w_ref[...]).astype(BF))


def qkv_in_call(chunk, chunks, perm, dq, dk, dv, w):
    dims, length = dk.shape
    width = w.shape[1]
    n = length // (chunks * QB)
    at = pl.BlockSpec((dims, QB), lambda t, p: (0, chunks * t + chunk))
    return pl.pallas_call(
        functools.partial(qkv_in_kernel, n),
        grid_spec=pltpu.PrefetchScalarGridSpec(
            num_scalar_prefetch=1, grid=(n,),
            in_specs=[pl.BlockSpec((dims, QB), lambda t, p: (0, t)), at, at, whole((3 * dims, width))],
            out_specs=[whole((QB, width))] * n,
            scratch_shapes=[pltpu.VMEM((3 * dims, QB), BF)],
        ),
        out_shape=[shape((QB, width), BF)] * n,
        compiler_params=params(), cost_estimate=cost(5),
    )(perm, dq, dk, dv, w)


def qkv_grad_kernel(chunks, perm, *refs):
    dqs, (dk_ref, dv_ref, a_ref, gw_ref, dx) = refs[:chunks], refs[chunks:]
    dims = dk_ref.shape[0]
    for i, r in enumerate(dqs):
        dx[0:dims, i * QB:(i + 1) * QB] = r[...]
    dx[dims:2 * dims, :] = dk_ref[...]
    dx[2 * dims:, :] = dv_ref[...]
    part = dot_nn(dx[...], a_ref[0])
    t = pl.program_id(0)

    @pl.when(t == 0)
    def _():
        gw_ref[...] = part

    @pl.when(t > 0)
    def _():
        gw_ref[...] += part


def qkv_grad_call(perm, dqs, dk, dv, a_rel):
    chunks = len(dqs)
    n, rows, width = a_rel.shape
    dims = dk.shape[0]
    tb = pl.BlockSpec((dims, rows), lambda t, p: (0, t))
    return pl.pallas_call(
        functools.partial(qkv_grad_kernel, chunks),
        grid_spec=pltpu.PrefetchScalarGridSpec(
            num_scalar_prefetch=1, grid=(n,),
            in_specs=[pl.BlockSpec((dims, QB), lambda t, p: (0, t))] * chunks + [
                tb, tb, pl.BlockSpec((1, rows, width), lambda t, p: (p[t], 0, 0))],
            out_specs=whole((3 * dims, width)),
            scratch_shapes=[pltpu.VMEM((3 * dims, rows), BF)],
        ),
        out_shape=shape((3 * dims, width), F32),
        compiler_params=params(), cost_estimate=cost(6),
    )(perm, *dqs, dk, dv, a_rel)


def mlp_fwd_kernel(*refs):
    n = 4
    cs, (w1_ref, w2_ref) = refs[:n], refs[n:n + 2]
    ms, (c_ref, r_ref, g_ref) = refs[n + 2:2 * n + 2], refs[2 * n + 2:]
    k = pl.program_id(0)
    for i, r in enumerate(cs):
        @pl.when(k == i)
        def _():
            c_ref[0] = r[...]
    u = dot_nt(c_ref[0], w1_ref[...])
    cdf = 0.5 * (1.0 + lax.erf(u * 0.7071067811865476))
    r = (u * cdf).astype(BF)
    r_ref[0] = r
    g_ref[0] = (cdf + u * (0.3989422804014327 * jnp.exp(-0.5 * u * u))).astype(BF)
    spread(k, ms, dot_nn(r, w2_ref[...]).astype(BF))


def mlp_fwd_call(cs, w):
    rows, width = cs[0].shape
    n, hid = len(cs), w.shape[0] // 2
    blk = pl.BlockSpec((1, rows, width), lambda k: (k, 0, 0))
    hb = pl.BlockSpec((1, rows, hid), lambda k: (k, 0, 0))
    return pl.pallas_call(
        mlp_fwd_kernel, grid=(n,),
        in_specs=[whole(c.shape) for c in cs] + [whole((hid, width), (0, 0)), whole((hid, width), (1, 0))],
        out_specs=[whole((rows, width))] * n + [blk, hb, hb],
        out_shape=[shape((rows, width), BF)] * n + [shape((n, rows, width), BF)] + [shape((n, rows, hid), BF)] * 2,
        compiler_params=params(), cost_estimate=cost(9),
    )(*cs, w, w)


def mlp_bwd_kernel(*refs):
    n = 4
    dms, (g_ref, w1_ref, w2_ref) = refs[:n], refs[n:n + 3]
    dcs, (dm_ref, du_ref) = refs[n + 3:2 * n + 3], refs[2 * n + 3:]
    k = pl.program_id(0)
    for i, r in enumerate(dms):
        @pl.when(k == i)
        def _():
            dm_ref[0] = r[...]
    dr = dot_nt(dm_ref[0], w2_ref[...])
    du = (dr * g_ref[0].astype(F32)).astype(BF)
    du_ref[0] = du
    spread(k, dcs, dot_nn(du, w1_ref[...]).astype(BF))


def mlp_bwd_call(dms, g, w):
    rows, width = dms[0].shape
    n, hid = len(dms), w.shape[0] // 2
    blk = pl.BlockSpec((1, rows, width), lambda k: (k, 0, 0))
    hb = pl.BlockSpec((1, rows, hid), lambda k: (k, 0, 0))
    return pl.pallas_call(
        mlp_bwd_kernel, grid=(n,),
        in_specs=[whole(d.shape) for d in dms] + [hb, whole((hid, width), (0, 0)), whole((hid, width), (1, 0))],
        out_specs=[whole((rows, width))] * n + [blk, hb],
        out_shape=[shape((rows, width), BF)] * n + [shape((n, rows, width), BF), shape((n, rows, hid), BF)],
        compiler_params=params(), cost_estimate=cost(8),
    )(*dms, g, w, w)


def place_kernel(sizes, count, starts, pieces, *refs):
    srcs, out_ref, mid = refs[:-2], refs[-2], refs[-1]
    sub = srcs[0].shape[1]
    for k, src in enumerate(srcs):
        base = starts[k]
        step = next(u for u in (8, 6, 4, 3, 2, 1) if sizes[k] % u == 0)

        def body(i, c, src=src, base=base, step=step):
            for u in range(step):
                n = i * step + u
                to = pieces[base + n]
                mid[pl.ds(pl.multiple_of(to * sub, sub), sub), :] = src[n].astype(F32)
            return c

        lax.fori_loop(0, sizes[k] // step, body, 0)
    rows = 64

    def spread(i, c):
        r = pl.multiple_of(i * rows, rows)
        for j in range(sub):
            part = mid[pl.ds(r * sub + j, rows, stride=sub), :]
            out_ref[pl.ds(r, rows), j * LANES:(j + 1) * LANES] = part.astype(BF)
        return c

    lax.fori_loop(0, count // rows, spread, 0)


def place_call(blocks, starts, pieces, count):
    sub = blocks[0].shape[1]
    sizes = [b.shape[0] for b in blocks]
    return pl.pallas_call(
        functools.partial(place_kernel, sizes, count),
        grid_spec=pltpu.PrefetchScalarGridSpec(
            num_scalar_prefetch=2, grid=(1,),
            in_specs=[whole(b.shape) for b in blocks],
            out_specs=whole((count, sub * LANES)),
            scratch_shapes=[pltpu.VMEM(((count + 8) * sub, LANES), F32)],
        ),
        out_shape=jax.ShapeDtypeStruct((count, sub * LANES), BF),
        compiler_params=params(), cost_estimate=cost(count / 450),
    )(starts, pieces, *blocks)


def bucket_kernel(sizes, starts, pieces, *refs):
    n = len(sizes)
    grads, outs, mid = refs[:-n - 1], refs[-n - 1:-1], refs[-1]
    width = grads[0].shape[1]
    sub = width // LANES
    rows = 64
    at = 0
    for g in grads:
        def split(i, c, g=g, at=at):
            r = pl.multiple_of(i * rows, rows)
            for j in range(sub):
                mid[pl.ds((at + r) * sub + j, rows, stride=sub), :] = g[pl.ds(r, rows), j * LANES:(j + 1) * LANES].astype(F32)
            return c

        lax.fori_loop(0, g.shape[0] // rows, split, 0)
        at += g.shape[0]
    mid[at * sub:(at + 1) * sub, :] = jnp.zeros((sub, LANES), F32)
    for k, out in enumerate(outs):
        base = starts[k]
        step = next(u for u in (8, 6, 4, 3, 2, 1) if sizes[k] % u == 0)

        def body(i, c, out=out, base=base, step=step):
            for u in range(step):
                m = i * step + u
                src = pieces[base + m]
                out[m] = mid[pl.ds(pl.multiple_of(src * sub, sub), sub), :].astype(BF)
            return c

        lax.fori_loop(0, sizes[k] // step, body, 0)


def bucket_call(grads, starts, pieces, sizes):
    width = grads[0].shape[1]
    sub = width // LANES
    count = sum(g.shape[0] for g in grads)
    shapes = [(s, sub, LANES) for s in sizes]
    return pl.pallas_call(
        functools.partial(bucket_kernel, sizes),
        grid_spec=pltpu.PrefetchScalarGridSpec(
            num_scalar_prefetch=2, grid=(1,),
            in_specs=[whole(g.shape) for g in grads],
            out_specs=[whole(s) for s in shapes],
            scratch_shapes=[pltpu.VMEM(((count + 8) * sub, LANES), F32)],
        ),
        out_shape=[jax.ShapeDtypeStruct(s, BF) for s in shapes],
        compiler_params=params(), cost_estimate=cost(count / 350),
    )(starts, pieces, *grads)


TOP = [(0, 1), (1, 0), (2, 3), (3, 2)]
SIDE = [(0, 2), (1, 3), (2, 0), (3, 1)]
RINGS = {8: [0, 2, 4, 6, 7, 5, 3, 1]}


def to_core(v):
    return lax.ppermute(v, "tensor", TOP)


def to_chip(v):
    return lax.ppermute(v, "tensor", SIDE)


def after(v, *first):
    return lax.optimization_barrier((v, *first))[0]


def gather_rel(own):
    side = to_chip(own)
    return [own, to_core(own), side, to_core(side)]


def scatter_rel(parts):
    far = to_core(parts[3])
    sent = (parts[2].astype(F32) + far.astype(F32)).astype(BF)
    return (parts[0], to_core(parts[1]), to_chip(sent)), sent


def reorder(v, me):
    v = jnp.where(me % 2 == 1, jnp.stack([v[1], v[0], v[3], v[2]]), v)
    return jnp.where(me // 2 == 1, jnp.stack([v[2], v[3], v[0], v[1]]), v)


class Owners:
    def __init__(self, cap):
        self.cap, self.count = cap, lax.axis_size("dp")
        self.ring = RINGS.get(self.count)
        self.cut = cap // 2 // 8 * 8
        if self.ring:
            n = self.count
            self.right = [(self.ring[i], self.ring[(i + 1) % n]) for i in range(n)]
            self.left = [(b, a) for a, b in self.right]
            self.far = n // 2
            me = lax.axis_index("dp")
            place = sum(jnp.where(me == d, i, 0) for i, d in enumerate(self.ring))
            self.at = lambda hop: sum(jnp.where((place + hop) % n == i, d, 0) for i, d in enumerate(self.ring)) * cap
            offsets = [self.at(0)]
            self.sizes = [cap]
            for s in range(1, self.far):
                offsets += [self.at(n - s), self.at(s)]
                self.sizes += [cap, cap]
            offsets += [self.at(self.far), self.at(self.far) + self.cut]
            self.sizes += [self.cut, cap - self.cut]
            self.starts = jnp.stack(offsets).astype(jnp.int32)
        else:
            self.sizes = [self.count * cap]
            self.starts = jnp.zeros((1,), jnp.int32)

    def gather(self, shard, ready):
        if not self.ring:
            return [lax.all_gather(shard, "dp", axis=0, tiled=True)]
        blocks = [shard]
        a = b = shard
        for s in range(1, self.far):
            if ready[s - 1] is not None:
                a, b = after(a, ready[s - 1]), after(b, ready[s - 1])
            a, b = lax.ppermute(a, "dp", self.right), lax.ppermute(b, "dp", self.left)
            blocks += [a, b]
        if ready[self.far - 1] is not None:
            a, b = after(a, ready[self.far - 1]), after(b, ready[self.far - 1])
        return blocks + [lax.ppermute(a[:self.cut], "dp", self.right), lax.ppermute(b[self.cut:], "dp", self.left)]

    def scatter(self, blocks, ready):
        if not self.ring:
            cap = self.cap
            pad = -cap % 8
            v = blocks[0].reshape(self.count, cap, *blocks[0].shape[1:])
            v = jnp.pad(v, ((0, 0), (0, pad), (0, 0), (0, 0))).reshape(-1, *blocks[0].shape[1:])
            return [lax.psum_scatter(v, "dp", scatter_dimension=0, tiled=True)[:cap]]

        def add(x, y):
            return (x.astype(F32) + y.astype(F32)).astype(BF)

        a, b = blocks[-2], blocks[-1]
        a, b = lax.ppermute(a, "dp", self.right), lax.ppermute(b, "dp", self.left)
        for s in range(self.far - 1, 0, -1):
            x, y = blocks[2 * s], blocks[2 * s - 1]
            step = self.far - s
            if ready[step - 1] is not None:
                x, y = after(x, ready[step - 1]), after(y, ready[step - 1])
            if s == self.far - 1:
                a = jnp.concatenate([add(x[:self.cut], a), x[self.cut:]], axis=0)
                b = jnp.concatenate([y[:self.cut], add(y[self.cut:], b)], axis=0)
            else:
                a, b = add(x, a), add(y, b)
            a, b = lax.ppermute(a, "dp", self.right), lax.ppermute(b, "dp", self.left)
        return [blocks[0], a, b]


def slot_rows(assign, slots):
    n = assign.shape[0]
    here = lax.broadcasted_iota(jnp.int32, (n, slots), 1) == assign[:, None]
    back = lax.broadcasted_iota(jnp.int32, (n, slots), 0) - n
    return jnp.sum(jnp.where(here, back, 0), axis=0) + n


def adamw(master, moment, square, gradient, rate):
    moment = 0.5 * moment + 0.5 * gradient
    square = 0.5 * square + 0.5 * gradient * gradient
    m_hat = moment / (1.0 - 0.5**ADAM_STEP)
    s_hat = square / (1.0 - 0.5**ADAM_STEP)
    update = m_hat / (jnp.sqrt(s_hat) + 1e-8) + 0.1 * master
    return master - rate * update, moment, square


def rotary_tables(length):
    half = HEAD // 2
    frequency = 10000.0 ** (-jnp.arange(half, dtype=F32) / half)
    angles = frequency[:, None] * jnp.arange(length, dtype=F32)[None, :]
    return jnp.cos(angles), jnp.sin(angles)


def on_device(tokens, cotangent, group_ids, assign_attn, assign_mlp,
              master_attn, moment_attn, square_attn, master_mlp, moment_mlp, square_mlp):
    owners = lax.axis_size("dp")
    tensor = lax.axis_size("tensor")
    rows_here, width = tokens.shape
    sub = width // LANES
    length = rows_here * tensor
    me, owner = lax.axis_index("tensor"), lax.axis_index("dp")
    perm = jnp.arange(tensor, dtype=jnp.int32) ^ me
    n_attn, n_mlp = width, assign_mlp.shape[0]
    dims, hidden = width // tensor, n_mlp // 2
    cap_a, cap_m = master_attn.shape[1], master_mlp.shape[1]
    part_rows = rows_here // CHUNKS
    cuts = [slice(j * part_rows, (j + 1) * part_rows) for j in range(CHUNKS)]

    def by_slot(v):
        return v.reshape(v.shape[1], sub, LANES)

    own_a, own_m = Owners(cap_a), Owners(cap_m)
    slots_a = owner * cap_a + jnp.arange(cap_a, dtype=jnp.int32)
    slots_m = owner * cap_m + jnp.arange(cap_m, dtype=jnp.int32)
    low_a, low_m = by_slot(master_attn).astype(BF), by_slot(master_mlp).astype(BF)

    blocks_a = own_a.gather(low_a, [None] * 8)
    xs = gather_rel(tokens)
    held = [slots_a == assign_attn[n_attn + i] for i in range(2)]
    mine = jnp.stack([jnp.sum(jnp.where(h[:, None, None], low_a.astype(F32), 0.0), axis=0) for h in held])
    mine = mine.reshape(2, width)
    bit = 1
    while bit < owners:
        mine = mine + lax.ppermute(mine, "dp", [(i, i ^ bit) for i in range(owners)])
        bit *= 2
    norms = reorder(jnp.stack(gather_rel(mine)), me).reshape(2 * tensor, width)
    a_rel = input_call(xs, norms)
    cos_t, sin_t = rotary_tables(length)
    weight = (0.5 + 0.5 * group_ids.astype(F32))[:, None]
    pieces_a = slot_rows(assign_attn[:n_attn], owners * cap_a)
    pieces_m = slot_rows(assign_mlp, owners * cap_m)

    def named(slots, part):
        return jnp.any(slots[:, None] == part[None, :], axis=1)

    rate_a = jnp.where(held[0] | held[1], 0.2, jnp.where(named(slots_a, assign_attn[3 * dims:n_attn]), 0.4, 0.06)).astype(F32)
    rate_m = jnp.where(named(slots_m, assign_mlp[hidden:]), 0.03, 0.06).astype(F32)

    blocks_a, a_rel, pieces_a = lax.optimization_barrier((blocks_a, a_rel, pieces_a))
    w_attn = place_call(blocks_a, own_a.starts, pieces_a, n_attn)
    qt, kt, vt, k4, v4 = qkv_call(perm, a_rel, w_attn, cos_t, sin_t)

    fwd = []
    state = []
    *zp, ot, lse = attn_fwd_call(0, CHUNKS, perm, qt, k4, vt, w_attn)
    terms, sent = scatter_rel(zp)
    fwd.append((terms, ot, lse))
    gate = [qt, ot]
    for j in range(1, CHUNKS):
        *zp, ot, lse = attn_fwd_call(j, CHUNKS, perm, after(qt, sent), k4, vt, w_attn)
        terms, sent = scatter_rel(zp)
        fwd.append((terms, ot, lse))
        gate.append(ot)
    blocks_m = own_m.gather(low_m, [blocks_a[-1], *gate])

    last = sent
    for j in range(CHUNKS):
        terms, ot, lse = fwd[j]
        z, h, c = residual_call(terms, after(tokens[cuts[j]], last), norms)
        last = c
        state.append((z, h, c))
    cs = [gather_rel(s[2]) for s in state]
    blocks_m[0] = after(blocks_m[0], last)
    w_mlp = place_call(blocks_m, own_m.starts, pieces_m, n_mlp)
    mids = []
    sent = None
    for j in range(CHUNKS):
        args = cs[j] if sent is None else [after(cs[j][0], sent), *cs[j][1:]]
        *mp, c_rel, r, g = mlp_fwd_call(args, w_mlp)
        terms, sent = scatter_rel(mp)
        mids.append((terms, c_rel, r, g))
    last = sent
    outs, dms = [], []
    dnorm4 = 0.0
    for j in range(CHUNKS):
        z, h, c = state[j]
        lo, dm, dn = out_call(mids[j][0], after(h, last), cotangent[cuts[j]], weight[cuts[j]], norms)
        last = dm
        outs.append(lo)
        dnorm4 = dnorm4 + dn
        dms.append(gather_rel(dm))

    sent = None
    backs = []
    for j in range(CHUNKS):
        args = dms[j] if sent is None else [after(dms[j][0], sent), *dms[j][1:]]
        *dcp, dm_rel, du = mlp_bwd_call(args, mids[j][3], w_mlp)
        terms, sent = scatter_rel(dcp)
        backs.append((terms, dm_rel, du))
    toks = (((0, 1), (0, 1)), ((), ()))

    def over_tokens(x, y):
        return lax.dot_general(x, y, toks, preferred_element_type=F32)

    last = sent
    dhs, dzs = [], []
    dnorm23 = 0.0
    grad_up = grad_down = 0.0
    for j in range(CHUNKS):
        z, h, c = state[j]
        _, c_rel, r, g = mids[j]
        terms, dm_rel, du = backs[j]
        dh, dz, dn = mid_call(terms, after(h, last), z, cotangent[cuts[j]], weight[cuts[j]], norms)
        last = dz
        dhs.append(dh)
        dnorm23 = dnorm23 + dn
        dzs.append(gather_rel(dz))
        grad_down = grad_down + over_tokens(r, dm_rel)
        grad_up = grad_up + over_tokens(du, c_rel)
    buckets_m = bucket_call([after(grad_up, last), grad_down], own_m.starts, pieces_m, own_m.sizes)

    prev, dqs = (), []
    last = buckets_m[0]
    for j in range(CHUNKS):
        _, ot, lse = fwd[j]
        dq, *prev = attn_bwd_call(j, CHUNKS, perm, [after(dzs[j][0], last), *dzs[j][1:]], w_attn, qt, k4, kt, v4, ot, lse, cos_t, sin_t, tuple(prev))
        last = dq
        dqs.append(dq)
    dk, dv, grad_out = prev
    da0 = qkv_in_call(0, CHUNKS, perm, dqs[0], dk, dv, w_attn)
    terms0, sent = scatter_rel(da0)
    grad_qkv = qkv_grad_call(perm, [after(dqs[0], sent), *dqs[1:]], dk, dv, a_rel)
    buckets_a = bucket_call([grad_qkv, grad_out], own_a.starts, pieces_a, own_a.sizes)
    sums_m = own_m.scatter(buckets_m, [dqs[0], dqs[1], grad_qkv])
    sums_a = own_a.scatter(buckets_a, [None] * 8)
    da_terms = [terms0]
    last = buckets_a[0]
    for j in range(1, CHUNKS):
        terms, sent = scatter_rel(qkv_in_call(j, CHUNKS, perm, after(dqs[j], last), dk, dv, w_attn))
        last = sent
        da_terms.append(terms)
    dxs = []
    dnorm1 = 0.0
    for j in range(CHUNKS):
        dx, dn = last_call(da_terms[j], tokens[cuts[j]], dhs[j], norms)
        dxs.append(dx)
        dnorm1 = dnorm1 + dn
    dn_all = reorder(jnp.concatenate([dnorm1, dnorm23, dnorm4], axis=0).reshape(tensor, 2, width), me)
    near = dn_all[0] + to_core(dn_all[1])
    norm_sum = near + to_chip(dn_all[2] + to_core(dn_all[3]))
    bit = 1
    while bit < owners:
        norm_sum = norm_sum + lax.ppermute(norm_sum, "dp", [(i, i ^ bit) for i in range(owners)])
        bit *= 2
    norm_sum = norm_sum.reshape(2, sub, LANES)

    grad_a = sum(p.astype(F32) for p in sums_a)
    grad_m = sum(p.astype(F32) for p in sums_m)
    for i in range(2):
        grad_a = grad_a + jnp.where(held[i][:, None, None], norm_sum[i][None], 0.0)
    new_m = adamw(by_slot(master_mlp), by_slot(moment_mlp), by_slot(square_mlp), grad_m, rate_m[:, None, None])
    new_a = adamw(by_slot(master_attn), by_slot(moment_attn), by_slot(square_attn), grad_a, rate_a[:, None, None])
    return (jnp.concatenate(outs, axis=0), jnp.concatenate(dxs, axis=0),
            *(v.reshape(master_attn.shape) for v in new_a), *(v.reshape(master_mlp.shape) for v in new_m))


def solution(mesh):
    tok = P(("dp", "tensor"), None)
    par = P("tensor", "dp", None)
    return jax.shard_map(
        on_device, mesh=mesh,
        in_specs=(tok, tok, P(("dp", "tensor")), P(), P(), par, par, par, par, par, par),
        out_specs=(tok, tok, par, par, par, par, par, par),
        check_vma=False,
    )
```

```python
import functools
import jax
import jax.numpy as jnp
from jax import lax
from jax.sharding import PartitionSpec as P
from jax.experimental import pallas as pl
from jax.experimental.pallas import tpu as pltpu

BF = jnp.bfloat16
F32 = jnp.float32
EPS = 1e-5
HEAD = 64
LANES = 128
QB = 256
CHUNKS = 2
ADAM_STEP = 5


def dot_nn(a, b):
    return lax.dot_general(a, b, (((1,), (0,)), ((), ())), preferred_element_type=F32)


def dot_nt(a, b):
    return lax.dot_general(a, b, (((1,), (1,)), ((), ())), preferred_element_type=F32)


def params(mib):
    return pltpu.CompilerParams(vmem_limit_bytes=mib * 1024 * 1024)


def cost(us):
    return pl.CostEstimate(flops=int(us * 3e7), bytes_accessed=int(us * 1e5), transcendentals=0)


def whole(shape, at=None):
    at = at or (0,) * len(shape)
    return pl.BlockSpec(shape, lambda *_: at)


def shape(dims, dtype):
    return jax.ShapeDtypeStruct(dims, dtype)


def choose(index, refs, into):
    for i in range(4):
        @pl.when(index == i)
        def _():
            if i == 3 and len(refs) == 5:
                half = refs[3].shape[0]
                into[0:half, :] = refs[3][...]
                into[half:, :] = refs[4][...]
            else:
                into[...] = refs[i][...]


def spread(index, refs, value):
    for i in range(4):
        @pl.when(index == i)
        def _():
            if i == 3:
                half = refs[3].shape[0]
                refs[3][...] = value[0:half]
                refs[4][...] = value[half:]
            else:
                refs[i][...] = value


def block_dims(rows, width):
    return [(rows, width)] * 3 + [(rows // 2, width)] * 2


def centre(v):
    mean = jnp.mean(v, axis=-1, keepdims=True)
    vc = v - mean
    s = lax.rsqrt(jnp.mean(vc * vc, axis=-1, keepdims=True) + EPS)
    return vc * s, s


def norm_back(n, s, y, gain):
    dn = y * gain
    return s * (dn - jnp.mean(dn, axis=-1, keepdims=True) - n * jnp.mean(dn * n, axis=-1, keepdims=True))


def total(parts):
    return sum(p[...].astype(F32) for p in parts)


def rows_call(kernel, outs, *args):
    return pl.pallas_call(kernel, out_shape=outs, compiler_params=params(10), cost_estimate=cost(2.5))(*args)


def residual_kernel(p0, p1, p2, x_ref, norms, z_ref, h_ref, c_ref):
    z = total([p0, p1, p2])
    z_ref[...] = z
    n, _ = centre(z)
    h = x_ref[...].astype(F32) + n * norms[2:3, :] + norms[3:4, :]
    h_ref[...] = h
    n, _ = centre(h)
    c_ref[...] = (n * norms[4:5, :] + norms[5:6, :]).astype(BF)


def residual_call(parts, x, norms):
    return rows_call(residual_kernel, [shape(x.shape, F32), shape(x.shape, F32), shape(x.shape, BF)], *parts, x, norms)


def out_kernel(p0, p1, p2, h_ref, ct_ref, wt_ref, norms, lo_ref, dm_ref, dn_ref):
    n, s = centre(total([p0, p1, p2]))
    lo_ref[...] = (h_ref[...] + n * norms[6:7, :] + norms[7:8, :]).astype(BF)
    e = ct_ref[...].astype(F32) * wt_ref[:, 0:1]
    dm_ref[...] = norm_back(n, s, e, norms[6:7, :]).astype(BF)
    dn_ref[0:1, :] = jnp.sum(e * n, axis=0, keepdims=True)
    dn_ref[1:2, :] = jnp.sum(e, axis=0, keepdims=True)


def out_call(parts, h, ct, wt, norms):
    return rows_call(out_kernel, [shape(h.shape, BF), shape(h.shape, BF), shape((2, h.shape[1]), F32)], *parts, h, ct, wt, norms)


def mid_kernel(p0, p1, p2, h_ref, z_ref, ct_ref, wt_ref, norms, dh_ref, dz_ref, dn_ref):
    dc = total([p0, p1, p2])
    n3, s3 = centre(h_ref[...])
    dh = ct_ref[...].astype(F32) * wt_ref[:, 0:1] + norm_back(n3, s3, dc, norms[4:5, :])
    dh_ref[...] = dh
    n2, s2 = centre(z_ref[...])
    dz_ref[...] = norm_back(n2, s2, dh, norms[2:3, :]).astype(BF)
    dn_ref[0:1, :] = jnp.sum(dh * n2, axis=0, keepdims=True)
    dn_ref[1:2, :] = jnp.sum(dh, axis=0, keepdims=True)
    dn_ref[2:3, :] = jnp.sum(dc * n3, axis=0, keepdims=True)
    dn_ref[3:4, :] = jnp.sum(dc, axis=0, keepdims=True)


def mid_call(parts, h, z, ct, wt, norms):
    return rows_call(mid_kernel, [shape(h.shape, F32), shape(h.shape, BF), shape((4, h.shape[1]), F32)],
                     *parts, h, z, ct, wt, norms)


def last_kernel(p0, p1, p2, x_ref, dh_ref, norms, dx_ref):
    n1, s1 = centre(x_ref[...].astype(F32))
    dx_ref[...] = dh_ref[...] + norm_back(n1, s1, total([p0, p1, p2]), norms[0:1, :])


def last_call(parts, x, dh, norms):
    return rows_call(last_kernel, shape(x.shape, F32), *parts, x, dh, norms)


def qkv_kernel(perm, *refs):
    xs, gs, (w_ref, cos_ref, sin_ref, norms, n_ref, qt_ref, kt_ref, vt_ref, k4_ref, v4_ref, cur) = refs[:4], refs[4:8], refs[8:]

    @pl.when(pl.program_id(0) == 0)
    def _():
        for t in range(4):
            for i, g in enumerate(gs):
                @pl.when(perm[t] == i)
                def _():
                    norms[2 * t:2 * t + 2, :] = g[0:2, :]

    choose(pl.program_id(0), xs, cur)
    n, _ = centre(cur[...].astype(F32))
    n_ref[0] = n.astype(BF)
    a = (n * norms[0:1, :] + norms[1:2, :]).astype(BF)
    cos, sin = cos_ref[...], sin_ref[...]
    dims = qt_ref.shape[0]
    half = HEAD // 2
    for part in range(3):
        proj = dot_nt(w_ref[part * dims:(part + 1) * dims, :], a)
        for h in range(dims // HEAD):
            lo = slice(h * HEAD, h * HEAD + half)
            hi = slice(h * HEAD + half, (h + 1) * HEAD)
            hd = slice(h * HEAD, (h + 1) * HEAD)
            if part < 2:
                first, second = proj[lo], proj[hi]
                r1 = first * cos - second * sin
                r2 = second * cos + first * sin
                if part == 0:
                    qt_ref[lo, :] = (r1 * 0.125).astype(BF)
                    qt_ref[hi, :] = (r2 * 0.125).astype(BF)
                else:
                    full = jnp.concatenate([r1, r2], axis=0)
                    kt_ref[hd, :] = full.astype(BF)
                    k4_ref[h] = full.T.astype(BF)
            else:
                vt_ref[hd, :] = proj[hd].astype(BF)
                v4_ref[h] = proj[hd].T.astype(BF)


def qkv_call(perm, xs, gains, w, cos_t, sin_t):
    rows, width = xs[0].shape
    n = len(xs)
    dims = w.shape[0] // 4
    heads = dims // HEAD
    length = n * rows
    tok = pl.BlockSpec((dims, rows), lambda k, p: (0, p[k]))
    hd = pl.BlockSpec((heads, rows, HEAD), lambda k, p: (0, p[k], 0))
    tab = pl.BlockSpec((HEAD // 2, rows), lambda k, p: (0, p[k]))
    return pl.pallas_call(
        qkv_kernel,
        grid_spec=pltpu.PrefetchScalarGridSpec(
            num_scalar_prefetch=1, grid=(n,),
            in_specs=[whole((rows, width))] * n + [whole(g.shape) for g in gains] + [whole((3 * dims, width)), tab, tab],
            out_specs=[whole((8, width)), pl.BlockSpec((1, rows, width), lambda k, p: (k, 0, 0)), tok, tok, tok, hd, hd],
            scratch_shapes=[pltpu.VMEM((rows, width), BF)],
        ),
        out_shape=[shape((8, width), F32), shape((n, rows, width), BF)] + [shape((dims, length), BF)] * 3 + [shape((heads, length, HEAD), BF)] * 2,
        compiler_params=params(20), cost_estimate=cost(10),
    )(perm, *xs, *gains, w, cos_t, sin_t)


def visible(chunk, diag):
    return (lax.broadcasted_iota(jnp.int32, (diag, QB), 0)
            <= lax.broadcasted_iota(jnp.int32, (diag, QB), 1) + chunk * QB)


def key_spans(n, wide, diag):
    return ([pl.ds(0, n * wide)] if n else []) + [pl.ds(n * wide, diag)]


def pipelined(heads, first, second, third):
    ahead, behind = first(0), None
    for h in range(heads):
        now = ahead
        if h + 1 < heads:
            ahead = first(h + 1)
        done = second(h, now)
        if behind is not None:
            third(h - 1, behind)
        behind = done
    third(heads - 1, behind)


def attn_fwd_kernel(chunk, chunks, count, perm, qt_ref, k4_ref, vt_ref, wo_ref, *rest):
    zs, (ot_ref, lse_ref, acc) = rest[:5], rest[5:]
    t = pl.program_id(0)
    heads = qt_ref.shape[0] // HEAD
    diag = (chunk + 1) * QB
    seen = visible(chunk, diag)
    hd = [slice(h * HEAD, (h + 1) * HEAD) for h in range(heads)]

    def one_row(n):
        spans = key_spans(n, chunks * QB, diag)

        def scores(h):
            return [dot_nn(k4_ref[h, ks, :], qt_ref[hd[h], :]) for ks in spans]

        def soft(h, s):
            s = s[:-1] + [jnp.where(seen, s[-1], -1e30)]
            m = functools.reduce(jnp.maximum, [jnp.max(v, axis=0, keepdims=True) for v in s])
            p = [jnp.exp(v - m) for v in s]
            l = sum(jnp.sum(v, axis=0, keepdims=True) for v in p)
            lse_ref[h:h + 1, :] = m + jnp.log(l)
            return [v.astype(BF) for v in p], l

        def attend(h, done):
            acc[hd[h], :] = sum(dot_nn(vt_ref[hd[h], ks], v) for ks, v in zip(spans, done[0])) / done[1]

        pipelined(heads, scores, soft, attend)

    for n in range(count):
        pl.when(t == n)(functools.partial(one_row, n))
    o = acc[...]
    ot_ref[...] = o.astype(BF)
    spread(perm[t], zs, dot_nn(o.T.astype(BF), wo_ref[...]).astype(BF))


def attn_fwd_call(chunk, chunks, perm, qt, k4, vt, w):
    dims, length = qt.shape
    width = w.shape[1]
    heads = dims // HEAD
    n = length // (chunks * QB)
    return pl.pallas_call(
        functools.partial(attn_fwd_kernel, chunk, chunks, n),
        grid_spec=pltpu.PrefetchScalarGridSpec(
            num_scalar_prefetch=1, grid=(n,),
            in_specs=[
                pl.BlockSpec((dims, QB), lambda t, p: (0, chunks * t + chunk)),
                whole(k4.shape), whole(vt.shape), whole((dims, width), (3, 0))],
            out_specs=[whole(d) for d in block_dims(QB, width)] + [
                pl.BlockSpec((dims, QB), lambda t, p: (0, t)), pl.BlockSpec((heads, QB), lambda t, p: (0, t))],
            scratch_shapes=[pltpu.VMEM((dims, QB), F32)],
        ),
        out_shape=[shape(d, BF) for d in block_dims(QB, width)] + [shape((dims, n * QB), BF), shape((heads, n * QB), F32)],
        compiler_params=params(14), cost_estimate=cost(9.5 + 1.5 * chunk),
    )(perm, qt, k4, vt, w)


def attn_bwd_kernel(chunk, chunks, count, pair, perm, *refs):
    dzs, refs = refs[:5], refs[5:]
    wo_ref, qt_ref, k4_ref, kt_ref, v4_ref, ot_ref, lse_ref, cos_ref, sin_ref = refs[:9]
    refs = refs[9:]
    if chunk == 0:
        dq_ref, dk_ref, dv_ref, gwo_ref, acc, dot_ref, dl_ref, dz_ref = refs
    else:
        dk0, dv0, gwo0, dq_ref, dkl_ref, dvl_ref, gwo_ref, acc, dot_ref, dl_ref, dz_ref, dk_ref, dv_ref = refs
    heads = k4_ref.shape[0]
    half = HEAD // 2
    wide = chunks * QB
    diag = (chunk + 1) * QB
    seen = visible(chunk, diag)
    hd = [slice(h * HEAD, (h + 1) * HEAD) for h in range(heads)]
    cols = [slice(t * QB, (t + 1) * QB) for t in range(count)]
    mine = [slice((chunks * t + chunk) * QB, (chunks * t + chunk + 1) * QB) for t in range(count)]
    if chunk == 0:
        dk_ref[...] = jnp.zeros_like(dk_ref)
        dv_ref[...] = jnp.zeros_like(dv_ref)
    else:
        dk_ref[...] = dk0[...]
        dv_ref[...] = dv0[...]
    for t in range(count):
        choose(perm[t], dzs, dz_ref.at[t])
        dot_ref[:, cols[t]] = dot_nt(wo_ref[...], dz_ref[t]).astype(BF)
    prod = dot_ref[...].astype(F32) * ot_ref[...].astype(F32)
    for h in range(heads):
        dl_ref[h:h + 1, :] = jnp.sum(prod[hd[h]], axis=0, keepdims=True)

    def unit(u):
        t, h = u // heads, u % heads
        return t, h, key_spans(t, wide, diag)

    def scores(u):
        t, h, spans = unit(u)
        return [(dot_nn(k4_ref[h, ks, :], qt_ref[hd[h], mine[t]]), dot_nn(v4_ref[h, ks, :], dot_ref[hd[h], cols[t]])) for ks in spans]

    def soft(u, pairs):
        t, h, spans = unit(u)
        lse, delta = lse_ref[heads * pair + h:heads * pair + h + 1, cols[t]], dl_ref[h:h + 1, cols[t]]
        out = []
        for i, (s, dp) in enumerate(pairs):
            p = jnp.exp(s - lse)
            if i == len(pairs) - 1:
                p = jnp.where(seen, p, 0.0)
            out.append((p.astype(BF), (p * (dp - delta)).astype(BF)))
        return out

    def back(u, pairs):
        t, h, spans = unit(u)
        q, do = qt_ref[hd[h], mine[t]], dot_ref[hd[h], cols[t]]
        dq = 0.0
        for ks, (p, ds) in zip(spans, pairs):
            dv_ref[hd[h], ks] += dot_nt(do, p)
            dk_ref[hd[h], ks] += dot_nt(q, ds)
            dq = dq + dot_nn(kt_ref[hd[h], ks], ds)
        acc[hd[h], cols[t]] = dq

    pipelined(heads * count, scores, soft, back)
    g = dot_nn(ot_ref[...], dz_ref[...].reshape(count * QB, dz_ref.shape[2]))
    gwo_ref[...] = g if chunk == 0 else gwo0[...] + g

    def unturn(src, at, to, scale, out):
        cos, sin = cos_ref[:, at], sin_ref[:, at]
        for h in range(heads):
            lo = slice(h * HEAD, h * HEAD + half)
            hi = slice(h * HEAD + half, (h + 1) * HEAD)
            g1, g2 = src[lo, to] * scale, src[hi, to] * scale
            out[lo, to] = (g1 * cos + g2 * sin).astype(BF)
            out[hi, to] = (g2 * cos - g1 * sin).astype(BF)

    for t in range(count):
        unturn(acc, mine[t], cols[t], 0.125, dq_ref)
    if chunk == chunks - 1:
        unturn(dk_ref, slice(None), slice(None), 1.0, dkl_ref)
        dvl_ref[...] = dv_ref[...].astype(BF)


def attn_bwd_call(chunk, chunks, pair, perm, dzs, w, qt, k4, kt, v4, ot, lse, cos_t, sin_t, prev=()):
    dims, length = qt.shape[0] // 2, qt.shape[1]
    width = w.shape[1]
    heads = dims // HEAD
    n = length // (chunks * QB)
    full, tb = whole((dims, length), (pair, 0)), whole((dims, n * QB), (pair, 0))
    kv4 = whole((heads, length, HEAD), (pair, 0, 0))
    out_full, out_tb, out_w = whole((dims, length)), whole((dims, n * QB)), whole((dims, width))
    in_specs = [whole(d) for d in block_dims(QB, width)] + [
        whole((dims, width), (6 + pair, 0)), full, kv4, full, kv4, tb, whole(lse.shape), whole(cos_t.shape), whole(sin_t.shape)]
    scratch = [pltpu.VMEM((dims, n * QB), F32), pltpu.VMEM((dims, n * QB), BF), pltpu.VMEM((8, n * QB), F32), pltpu.VMEM((n, QB, width), BF)]
    kv = F32
    if chunk:
        in_specs += [out_full, out_full, out_w]
        scratch += [pltpu.VMEM((dims, length), F32)] * 2
        kv = BF
    return pl.pallas_call(
        functools.partial(attn_bwd_kernel, chunk, chunks, n, pair),
        grid_spec=pltpu.PrefetchScalarGridSpec(
            num_scalar_prefetch=1, grid=(1,), in_specs=in_specs,
            out_specs=[out_tb, out_full, out_full, out_w], scratch_shapes=scratch,
        ),
        out_shape=[shape((dims, n * QB), BF), shape((dims, length), kv), shape((dims, length), kv), shape((dims, width), F32)],
        compiler_params=params(22), cost_estimate=cost(10 + 2 * chunk),
    )(perm, *dzs, w, qt, k4, kt, v4, ot, lse, cos_t, sin_t, *prev)


def stack_rows(refs, into, cols=slice(None)):
    at = 0
    for r in refs:
        into[at:at + r.shape[0], cols] = r[...]
        at += r.shape[0]


def qkv_in_kernel(perm, *refs):
    parts, w_ref, das, dx = refs[:6], refs[6], refs[7:12], refs[12]
    stack_rows(parts, dx)
    grad = dx[...].astype(F32).T.astype(BF)
    spread(perm[pl.program_id(0)], das, dot_nn(grad, w_ref[...]).astype(BF))


def qkv_in_call(chunk, chunks, perm, dq, dk, dv, w):
    dims, length = dk[0].shape
    width = w.shape[1]
    n = length // (chunks * QB)
    at = pl.BlockSpec((dims, QB), lambda t, p: (0, chunks * t + chunk))
    return pl.pallas_call(
        qkv_in_kernel,
        grid_spec=pltpu.PrefetchScalarGridSpec(
            num_scalar_prefetch=1, grid=(n,),
            in_specs=[pl.BlockSpec((dims, QB), lambda t, p: (0, t))] * 2 + [at] * 4 + [whole((6 * dims, width))],
            out_specs=[whole(d) for d in block_dims(QB, width)],
            scratch_shapes=[pltpu.VMEM((6 * dims, QB), BF)],
        ),
        out_shape=[shape(d, BF) for d in block_dims(QB, width)],
        compiler_params=params(8), cost_estimate=cost(5),
    )(perm, *dq, *dk, *dv, w)


def qkv_grad_kernel(chunks, count, perm, *refs):
    dqs, kvs, refs = refs[:2 * chunks], refs[2 * chunks:2 * chunks + 4], refs[2 * chunks + 4:]
    d23, d4, (n_ref, w_ref, norms, gw_ref), dns, (dx, rows) = refs[:chunks], refs[chunks:2 * chunks], refs[2 * chunks:2 * chunks + 4], refs[2 * chunks + 4:2 * chunks + 8], refs[2 * chunks + 8:]
    dims = kvs[0].shape[0]
    wide = chunks * QB

    @pl.when(pl.program_id(0) == 0)
    def _():
        for i in range(chunks):
            for p in range(2):
                for t in range(count):
                    to = slice(t * wide + i * QB, t * wide + (i + 1) * QB)
                    dx[p * dims:(p + 1) * dims, to] = dqs[2 * i + p][:, t * QB:(t + 1) * QB]
        stack_rows(kvs, dx.at[2 * dims:])

    grad = sum(dot_nn(dx[:, t * wide:(t + 1) * wide], n_ref[perm[t]]) for t in range(count))
    sums = jnp.sum(dx[...].astype(F32), axis=1, keepdims=True)
    w = w_ref[...].astype(F32)
    gw_ref[...] = (grad * norms[0:1, :] + sums * norms[1:2, :]).astype(BF)
    rows[0:1, :] = jnp.sum(grad * w, axis=0, keepdims=True)
    rows[1:2, :] = jnp.sum(sums * w, axis=0, keepdims=True)
    rows[2:6, :] = total(d23)
    rows[6:8, :] = total(d4)
    for i, out in enumerate(dns):
        for t in range(4):
            @pl.when(perm[i] == t)
            def _():
                out[...] = rows[2 * t:2 * t + 2, :]


def qkv_grad_call(perm, dqs, dk, dv, d23, d4, n_rel, w, norms):
    chunks = len(dqs)
    n, rows, width = n_rel.shape
    dims = dk[0].shape[0]
    cols = 256
    args = [v for dq in dqs for v in dq] + [*dk, *dv]
    return pl.pallas_call(
        functools.partial(qkv_grad_kernel, chunks, n),
        grid_spec=pltpu.PrefetchScalarGridSpec(
            num_scalar_prefetch=1, grid=(width // cols,),
            in_specs=[whole(v.shape) for v in args] + [pl.BlockSpec((v.shape[0], cols), lambda i, p: (0, i)) for v in (*d23, *d4)] + [
                pl.BlockSpec((n, rows, cols), lambda i, p: (0, 0, i)), pl.BlockSpec((6 * dims, cols), lambda i, p: (0, i)),
                pl.BlockSpec((8, cols), lambda i, p: (0, i))],
            out_specs=[pl.BlockSpec((6 * dims, cols), lambda i, p: (0, i))] + [pl.BlockSpec((2, cols), lambda i, p: (0, i))] * 4,
            scratch_shapes=[pltpu.VMEM((6 * dims, n * rows), BF), pltpu.VMEM((8, cols), F32)],
        ),
        out_shape=[shape((6 * dims, width), BF)] + [shape((2, width), F32)] * 4,
        compiler_params=params(16), cost_estimate=cost(7),
    )(perm, *args, *d23, *d4, n_rel, w, norms)


def mlp_fwd_kernel(*refs):
    cs, (w1_ref, w2_ref), ms, (c_ref, r_ref, g_ref) = refs[:5], refs[5:7], refs[7:12], refs[12:]
    k = pl.program_id(0)
    choose(k, cs, c_ref.at[0])
    u = dot_nt(c_ref[0], w1_ref[...])
    cdf = 0.5 * (1.0 + lax.erf(u * 0.7071067811865476))
    r = (u * cdf).astype(BF)
    r_ref[0] = r
    g_ref[0] = (cdf + u * (0.3989422804014327 * jnp.exp(-0.5 * u * u))).astype(BF)
    spread(k, ms, dot_nn(r, w2_ref[...]).astype(BF))


def mlp_fwd_call(cs, w):
    rows, width = cs[0].shape
    n, hid = 4, w.shape[0] // 2
    dims = block_dims(rows, width)
    blk = pl.BlockSpec((1, rows, width), lambda k: (k, 0, 0))
    hb = pl.BlockSpec((1, rows, hid), lambda k: (k, 0, 0))
    return pl.pallas_call(
        mlp_fwd_kernel, grid=(n,),
        in_specs=[whole(c.shape) for c in cs] + [whole((hid, width), (0, 0)), whole((hid, width), (1, 0))],
        out_specs=[whole(d) for d in dims] + [blk, hb, hb],
        out_shape=[shape(d, BF) for d in dims] + [shape((n, rows, width), BF)] + [shape((n, rows, hid), BF)] * 2,
        compiler_params=params(16), cost_estimate=cost(9),
    )(*cs, w, w)


def mlp_bwd_kernel(*refs):
    dms, (g_ref, w1_ref, w2_ref), dcs, (dm_ref, du_ref) = refs[:5], refs[5:8], refs[8:13], refs[13:]
    k = pl.program_id(0)
    choose(k, dms, dm_ref.at[0])
    dr = dot_nt(dm_ref[0], w2_ref[...])
    du = (dr * g_ref[0].astype(F32)).astype(BF)
    du_ref[0] = du
    spread(k, dcs, dot_nn(du, w1_ref[...]).astype(BF))


def mlp_bwd_call(dms, g, w):
    rows, width = dms[0].shape
    n, hid = 4, w.shape[0] // 2
    dims = block_dims(rows, width)
    blk = pl.BlockSpec((1, rows, width), lambda k: (k, 0, 0))
    hb = pl.BlockSpec((1, rows, hid), lambda k: (k, 0, 0))
    return pl.pallas_call(
        mlp_bwd_kernel, grid=(n,),
        in_specs=[whole(d.shape) for d in dms] + [hb, whole((hid, width), (0, 0)), whole((hid, width), (1, 0))],
        out_specs=[whole(d) for d in dims] + [blk, hb],
        out_shape=[shape(d, BF) for d in dims] + [shape((n, rows, width), BF), shape((n, rows, hid), BF)],
        compiler_params=params(16), cost_estimate=cost(8),
    )(*dms, g, w, w)


def place_kernel(sizes, count, starts, pieces, *refs):
    srcs, out_ref, rest_ref, mid = refs[:-3], refs[-3], refs[-2], refs[-1]
    sub = srcs[0].shape[1]
    for k, src in enumerate(srcs):
        base = starts[k]
        step = next(u for u in (8, 6, 4, 3, 2, 1) if sizes[k] % u == 0)

        def body(i, c, src=src, base=base, step=step):
            for u in range(step):
                n = i * step + u
                to = pieces[base + n]
                mid[pl.ds(pl.multiple_of(to * sub, sub), sub), :] = src[n].astype(F32)
            return c

        lax.fori_loop(0, sizes[k] // step, body, 0)
    rows = 64

    def spread(i, c):
        r = pl.multiple_of(i * rows, rows)
        for j in range(sub):
            part = mid[pl.ds(r * sub + j, rows, stride=sub), :]
            out_ref[pl.ds(r, rows), j * LANES:(j + 1) * LANES] = part.astype(BF)
        return c

    lax.fori_loop(0, count // rows, spread, 0)
    for j in range(sub):
        rest_ref[:, j * LANES:(j + 1) * LANES] = mid[pl.ds(count * sub + j, 8, stride=sub), :]


def place_call(blocks, starts, pieces, count):
    sub = blocks[0].shape[1]
    sizes = [b.shape[0] for b in blocks]
    return pl.pallas_call(
        functools.partial(place_kernel, sizes, count),
        grid_spec=pltpu.PrefetchScalarGridSpec(
            num_scalar_prefetch=2, grid=(1,),
            in_specs=[whole(b.shape) for b in blocks],
            out_specs=[whole((count, sub * LANES)), whole((8, sub * LANES))],
            scratch_shapes=[pltpu.VMEM(((count + 8) * sub, LANES), F32)],
        ),
        out_shape=[shape((count, sub * LANES), BF), shape((8, sub * LANES), F32)],
        compiler_params=params(10 + count // 146), cost_estimate=cost(count / 450),
    )(starts, pieces, *blocks)


def bucket_kernel(sizes, starts, pieces, *refs):
    n = len(sizes)
    grads, outs, mid = refs[:-n - 1], refs[-n - 1:-1], refs[-1]
    width = grads[0].shape[1]
    sub = width // LANES
    rows = 64
    at = 0
    for g in grads:
        def split(i, c, g=g, at=at):
            r = pl.multiple_of(i * rows, rows)
            for j in range(sub):
                mid[pl.ds((at + r) * sub + j, rows, stride=sub), :] = g[pl.ds(r, rows), j * LANES:(j + 1) * LANES].astype(F32)
            return c

        lax.fori_loop(0, g.shape[0] // rows, split, 0)
        at += g.shape[0]
    mid[at * sub:(at + 8) * sub, :] = jnp.zeros((8 * sub, LANES), F32)
    for k, out in enumerate(outs):
        base = starts[k]
        step = next(u for u in (8, 6, 4, 3, 2, 1) if sizes[k] % u == 0)

        def body(i, c, out=out, base=base, step=step):
            for u in range(step):
                m = i * step + u
                src = pieces[base + m]
                out[m] = mid[pl.ds(pl.multiple_of(src * sub, sub), sub), :].astype(BF)
            return c

        lax.fori_loop(0, sizes[k] // step, body, 0)


def bucket_call(grads, starts, pieces, sizes):
    width = grads[0].shape[1]
    sub = width // LANES
    count = sum(g.shape[0] for g in grads)
    shapes = [(s, sub, LANES) for s in sizes]
    return pl.pallas_call(
        functools.partial(bucket_kernel, sizes),
        grid_spec=pltpu.PrefetchScalarGridSpec(
            num_scalar_prefetch=2, grid=(1,),
            in_specs=[whole(g.shape) for g in grads],
            out_specs=[whole(s) for s in shapes],
            scratch_shapes=[pltpu.VMEM(((count + 8) * sub, LANES), F32)],
        ),
        out_shape=[jax.ShapeDtypeStruct(s, BF) for s in shapes],
        compiler_params=params(8 + count // 146), cost_estimate=cost(count / 350),
    )(starts, pieces, *grads)


def adam_kernel(n_parts, *refs):
    parts, (rate, m_ref, f_ref, s_ref), rest = refs[:n_parts], refs[n_parts:n_parts + 4], refs[n_parts + 4:]
    extra, (om, of, os) = rest[:-3], rest[-3:]
    g = total(parts)
    if extra:
        for i in range(2):
            g = g + extra[i][...] * extra[2][i:i + 1]
    first = 0.5 * f_ref[...] + 0.5 * g
    second = 0.5 * s_ref[...] + 0.5 * g * g
    of[...] = first
    os[...] = second
    w = m_ref[...]
    first = first / (1.0 - 0.5**ADAM_STEP)
    second = second / (1.0 - 0.5**ADAM_STEP)
    om[...] = w - rate[...] * (first / (jnp.sqrt(second) + 1e-8) + 0.1 * w)


def adam_call(parts, rate, states, extra=()):
    cap, sub, lanes = states[0].shape
    step = next(d for d in range(64, 0, -1) if cap % d == 0)
    blk = pl.BlockSpec((step, sub, lanes), lambda i: (i, 0, 0))
    one = pl.BlockSpec((step, 1, lanes), lambda i: (i, 0, 0))

    def per_slot(v):
        return jnp.broadcast_to(v.astype(F32)[:, None, None], (cap, 1, lanes))

    more = [per_slot(v) for v in extra[:-1]] + list(extra[-1:])
    return pl.pallas_call(
        functools.partial(adam_kernel, len(parts)), grid=(cap // step,),
        in_specs=[blk] * len(parts) + [one] + [blk] * 3 + ([one, one, whole((2, sub, lanes))] if extra else []),
        out_specs=[blk] * 3,
        out_shape=[shape(v.shape, F32) for v in states],
        compiler_params=params(6), cost_estimate=cost(cap / 80),
    )(*parts, per_slot(rate), *states, *more)


def low_kernel(x_ref, o_ref):
    o_ref[...] = x_ref[...].astype(BF)


def low_call(v):
    cap, sub, lanes = v.shape
    step = next(d for d in range(64, 0, -1) if cap % d == 0)
    blk = pl.BlockSpec((step, sub, lanes), lambda i: (i, 0, 0))
    return pl.pallas_call(
        low_kernel, grid=(cap // step,), in_specs=[blk], out_specs=blk, out_shape=shape(v.shape, BF),
        compiler_params=params(4), cost_estimate=cost(1),
    )(v)


TOP = [(0, 1), (1, 0), (2, 3), (3, 2)]
SIDE = [(0, 2), (1, 3), (2, 0), (3, 1)]
RINGS = {8: [0, 2, 4, 6, 7, 5, 3, 1]}


def to_core(v):
    return lax.ppermute(v, "tensor", TOP)


def to_chip(v):
    return lax.ppermute(v, "tensor", SIDE)


def after(v, *first):
    return lax.optimization_barrier((v, *first))[0]


class Clock:
    def __init__(self):
        self.last = []

    def set(self, *values):
        self.last = list(values)

    def add(self, value):
        self.last.append(value)

    def at(self, value):
        return lax.optimization_barrier((value, *self.last))[0] if self.last else value


def gather_rel(own):
    side = to_chip(own)
    return [own, to_core(own), side, to_core(side)]


class Owners:
    def __init__(self, cap):
        self.cap, self.count = cap, lax.axis_size("dp")
        self.ring = RINGS.get(self.count)
        self.cut = cap // 2 // 8 * 8
        if self.ring:
            n, ring = self.count, self.ring
            self.right = [(ring[i], ring[(i + 1) % n]) for i in range(n)]
            self.left = [(b, a) for a, b in self.right]
            self.far = n // 2
            self.sizes = [cap] * (2 * self.far - 1) + [self.cut, cap - self.cut]
            table = [[0] * len(self.sizes) for _ in ring]
            for i, d in enumerate(ring):
                near = [ring[i]] + [ring[(i + h) % n] for s in range(1, self.far) for h in (-s, s)]
                other = ring[(i + self.far) % n] * cap
                table[d] = [v * cap for v in near] + [other, other + self.cut]
            self.starts = lax.dynamic_index_in_dim(jnp.asarray(table, jnp.int32), lax.axis_index("dp"), 0, keepdims=False)
        else:
            self.sizes = [self.count * cap]
            self.starts = jnp.zeros((1,), jnp.int32)

    def gather_steps(self, shard):
        return GatherSteps(self, shard)

    def scatter_steps(self, blocks):
        return ScatterSteps(self, blocks)


class GatherSteps:
    def __init__(self, own, shard):
        self.own, self.out, self.s = own, [shard], 1
        self.a = self.b = shard
        if own.ring:
            self.step(Clock())

    def step(self, clock):
        own = self.own
        if not own.ring or self.s > own.far:
            return
        a, b = clock.at((self.a, self.b))
        if self.s == own.far:
            a, b = a[:own.cut], b[own.cut:]
        self.a, self.b = lax.ppermute(a, "dp", own.right), lax.ppermute(b, "dp", own.left)
        self.out += [self.a, self.b]
        self.s += 1

    def pin(self, clock):
        if self.own.ring:
            for v in self.out[-4:-2]:
                clock.add(v)

    def blocks(self):
        if not self.own.ring:
            return [lax.all_gather(self.out[0], "dp", axis=0, tiled=True)]
        while self.s <= self.own.far:
            self.step(Clock())
        return list(self.out)


class ScatterSteps:
    def __init__(self, own, blocks):
        self.own, self.blocks, self.s = own, blocks, own.count // 2 - 1
        if own.ring:
            self.a = lax.ppermute(blocks[-2], "dp", own.right)
            self.b = lax.ppermute(blocks[-1], "dp", own.left)

    def more(self):
        return self.own.ring and self.s > 0

    def step(self, clock):
        own, s = self.own, self.s
        if not self.more():
            return

        def add(x, y):
            return (x.astype(F32) + y.astype(F32)).astype(BF)

        x, y = clock.at((self.blocks[2 * s], self.blocks[2 * s - 1]))
        a, b = self.a, self.b
        if s == own.far - 1:
            a = jnp.concatenate([add(x[:own.cut], a), x[own.cut:]], axis=0)
            b = jnp.concatenate([y[:own.cut], add(y[own.cut:], b)], axis=0)
        else:
            a, b = add(x, a), add(y, b)
        self.sent = a, b
        self.a, self.b = lax.ppermute(a, "dp", own.right), lax.ppermute(b, "dp", own.left)
        self.s -= 1

    def pin(self, clock):
        if self.own.ring:
            clock.add(self.sent[0])
            clock.add(self.sent[1])

    def terms(self):
        own, blocks = self.own, self.blocks
        if own.ring:
            return [blocks[0], self.a, self.b]
        pad = -own.cap % 8
        v = blocks[0].reshape(own.count, own.cap, *blocks[0].shape[1:])
        v = jnp.pad(v, ((0, 0), (0, pad), (0, 0), (0, 0))).reshape(-1, *blocks[0].shape[1:])
        return [lax.psum_scatter(v, "dp", scatter_dimension=0, tiled=True)[:own.cap]]


def slot_rows(assign, slots):
    n = assign.shape[0]
    here = lax.broadcasted_iota(jnp.int32, (n, slots), 1) == assign[:, None]
    back = lax.broadcasted_iota(jnp.int32, (n, slots), 0) - n
    return jnp.sum(jnp.where(here, back, 0), axis=0) + n


def rotary_tables(places):
    half = HEAD // 2
    frequency = 10000.0 ** (-jnp.arange(half, dtype=F32) / half)
    angles = frequency[:, None] * places.astype(F32)[None, :]
    return jnp.cos(angles), jnp.sin(angles)


def on_device(tokens, cotangent, group_ids, assign_attn, assign_mlp,
              master_attn, moment_attn, square_attn, master_mlp, moment_mlp, square_mlp):
    owners = lax.axis_size("dp")
    tensor = lax.axis_size("tensor")
    rows_here, width = tokens.shape
    sub = width // LANES
    length = rows_here * tensor
    me, owner = lax.axis_index("tensor"), lax.axis_index("dp")
    perm = jnp.arange(tensor, dtype=jnp.int32) ^ me
    n_attn, n_mlp = width, assign_mlp.shape[0]
    dims, hidden = width // tensor, n_mlp // 2
    cap_a, cap_m = master_attn.shape[1], master_mlp.shape[1]
    part_rows = rows_here // CHUNKS
    cuts = [slice(j * part_rows, (j + 1) * part_rows) for j in range(CHUNKS)]

    def by_slot(v):
        return v.reshape(v.shape[1], sub, LANES)

    own_a, own_m = Owners(cap_a), Owners(cap_m)
    slots_a = owner * cap_a + jnp.arange(cap_a, dtype=jnp.int32)
    slots_m = owner * cap_m + jnp.arange(cap_m, dtype=jnp.int32)
    low_a = low_call(after(by_slot(master_attn), perm, own_a.starts, own_m.starts, slots_a, slots_m))

    def named(slots, part):
        return jnp.any(slots[:, None] == part[None, :], axis=1)

    ring_a = own_a.gather_steps(low_a)
    side = to_chip(after(tokens, low_a))
    phase = Clock()

    def step():
        ring_a.step(Clock())
        phase.set(*ring_a.out[-4:-2])

    step()
    tokens_near = to_core(phase.at(tokens))
    names_a = phase.at(assign_attn)
    pieces_a = slot_rows(names_a, owners * cap_a)
    held = [slots_a == names_a[n_attn + i] for i in range(2)]
    rate_a = jnp.where(held[0] | held[1], 0.2, jnp.where(named(slots_a, names_a[3 * dims:n_attn]), 0.4, 0.06)).astype(F32)
    weight = jnp.broadcast_to((0.5 + 0.5 * phase.at(group_ids).astype(F32))[:, None], (rows_here, LANES))
    step()
    low_m = low_call(by_slot(phase.at(master_mlp)))
    names_m = phase.at(assign_mlp)
    pieces_m = slot_rows(names_m, owners * cap_m)
    rate_m = jnp.where(named(slots_m, names_m[hidden:]), 0.03, 0.06).astype(F32)
    cos_t, sin_t = rotary_tables(phase.at(jnp.arange(length, dtype=jnp.int32)))
    step()
    phase.set(side, low_m, cos_t, sin_t, pieces_a, pieces_m, rate_a, rate_m, weight, *ring_a.out[-4:-2])
    xs = [tokens, tokens_near, side, to_core(phase.at(side))]
    blocks_a = ring_a.blocks()
    clock = Clock()
    clock.set(xs[3])
    blocks_a[0] = clock.at(blocks_a[0])
    w_attn, held_norms = place_call(blocks_a, own_a.starts, pieces_a, n_attn)
    clock.set(w_attn)
    ring_m = own_m.gather_steps(after(low_m, *blocks_a[-2:]))
    norms_side = to_chip(held_norms)
    gains = [held_norms, to_core(held_norms), norms_side, to_core(norms_side)]
    norms, n_rel, qt, kt, vt, k4, v4 = qkv_call(perm, xs, gains, w_attn, cos_t, sin_t)
    clock.set(qt)
    ring_m.step(clock)
    ring_m.pin(clock)

    def summed(parts):
        far = [to_core(clock.at(p)) for p in parts[3:]]
        near = to_core(parts[1])
        half = far[0].shape[0]
        sent = [(parts[2][i * half:(i + 1) * half].astype(F32) + f.astype(F32)).astype(BF) for i, f in enumerate(far)]
        sent = jnp.concatenate(sent, axis=0)
        clock.set(sent)
        return parts[0], near, to_chip(sent)

    fwd = []
    for j in range(CHUNKS):
        *zp, ot, lse = attn_fwd_call(j, CHUNKS, perm, clock.at(qt), k4, vt, w_attn)
        clock.set(ot)
        ring_m.step(clock)
        ring_m.pin(clock)
        if j:
            clock.add(fwd[-1][0][2])
        terms = summed(zp)
        fwd.append((terms, ot, lse))
    state, sides = [], []
    blocks_m = ring_m.blocks()
    for j in range(CHUNKS):
        z, h, c = residual_call(fwd[j][0], clock.at(tokens[cuts[j]]), norms)
        clock.set(c)
        state.append((z, h, c))
        sides.append((to_core(c), to_chip(c)))
        if j == 0:
            blocks_m[0] = clock.at(blocks_m[0])
            w_mlp, _ = place_call(blocks_m, own_m.starts, pieces_m, n_mlp)
            clock.set(w_mlp)
            clock.add(fwd[1][0][2])

    def gathered(own, near, side):
        half = side.shape[0] // 2
        side = clock.at(side)
        return [own, near, side, to_core(side[:half]), to_core(side[half:])]

    mids = []
    for j in range(CHUNKS):
        cs = gathered(state[j][2], *sides[j])
        cs[0] = clock.at(cs[0])
        *mp, c_rel, r, g = mlp_fwd_call(cs, w_mlp)
        clock.set(r)
        clock.add(sides[1][1] if j == 0 else mids[0][0][2])
        mids.append((summed(mp), c_rel, r, g))
    outs, sides, dms = [], [], []
    dnorm4 = []
    for j in range(CHUNKS):
        z, h, c = state[j]
        clock.add(mids[j][0][2])
        lo, dm, dn = out_call(mids[j][0], clock.at(h), cotangent[cuts[j]], weight[cuts[j]], norms)
        clock.set(dm)
        outs.append(lo)
        dnorm4.append(dn)
        dms.append(dm)
        sides.append((to_core(dm), to_chip(dm)))

    backs = []
    for j in range(CHUNKS):
        args = gathered(dms[j], *sides[j])
        args[0] = clock.at(args[0])
        *dcp, dm_rel, du = mlp_bwd_call(args, mids[j][3], w_mlp)
        clock.set(du)
        clock.add(sides[1][1] if j == 0 else backs[0][0][2])
        backs.append((summed(dcp), dm_rel, du))
    toks = (((0, 1), (0, 1)), ((), ()))

    def over_tokens(x, y):
        return lax.dot_general(x, y, toks, preferred_element_type=F32)

    dhs, dzs, sides = [], [], []
    dnorm23 = []
    grads = []
    for j in range(CHUNKS):
        z, h, c = state[j]
        _, c_rel, r, g = mids[j]
        terms, dm_rel, du = backs[j]
        r, du = clock.at((r, du))
        grads.append((over_tokens(du, c_rel), over_tokens(r, dm_rel)))
        if j == 0:
            clock.set(*grads[0])
        clock.add(terms[2])
        dh, dz, dn = mid_call(terms, clock.at(h), z, cotangent[cuts[j]], weight[cuts[j]], norms)
        clock.set(dz)
        dhs.append(dh)
        dnorm23.append(dn)
        dzs.append(dz)
        sides.append((to_core(dz), to_chip(dz)))
    grad_up, grad_down = (sum(g[i] for g in grads).astype(BF) for i in range(2))
    buckets_m = bucket_call([clock.at(grad_up), grad_down], own_m.starts, pieces_m, own_m.sizes)
    clock.set(buckets_m[0])

    prev, dqs = [(), ()], []
    sums_m = own_m.scatter_steps(buckets_m)
    for j in range(CHUNKS):
        _, ot, lse = fwd[j]
        args = gathered(dzs[j], *sides[j])
        dqs.append([])
        for i in range(2):
            args[0] = clock.at(args[0])
            dq, *prev[i] = attn_bwd_call(j, CHUNKS, i, perm, args, w_attn, qt, k4, kt, v4, ot, lse, cos_t, sin_t, tuple(prev[i]))
            clock.set(dq)
            dqs[j].append(dq)
            if (i, j) != (1, 0):
                sums_m.step(clock)
                sums_m.pin(clock)
    dk, dv, grad_out = zip(*prev)
    grad_qkv, *dns = qkv_grad_call(perm, [[clock.at(dqs[0][0]), dqs[0][1]], *dqs[1:]], dk, dv, dnorm23, dnorm4, n_rel, w_attn, norms)
    clock.set(grad_qkv)
    buckets_a = bucket_call([clock.at(grad_qkv), *grad_out], own_a.starts, pieces_a, own_a.sizes)
    clock.set(buckets_a[0])
    terms_m = sums_m.terms()
    for v in terms_m[1:]:
        clock.add(v)
    ring_a = own_a.scatter_steps([clock.at(v) for v in buckets_a])
    dns = clock.at(dns)
    norm_sum = dns[0] + to_core(dns[1]) + to_chip(dns[2] + to_core(dns[3]))
    hops = [1 << i for i in range(owners.bit_length() - 1)]

    def norm_hop():
        bit = hops.pop(0) if hops else None
        if bit:
            return norm_sum + lax.ppermute(clock.at(norm_sum), "dp", [(d, d ^ bit) for d in range(owners)])
        return norm_sum

    da_terms = []
    for j in range(CHUNKS):
        da = qkv_in_call(j, CHUNKS, perm, [clock.at(dqs[j][0]), dqs[j][1]], dk, dv, w_attn)
        clock.set(da[0])
        ring_a.step(clock)
        ring_a.pin(clock)
        norm_sum = norm_hop()
        da_terms.append(summed(da))
    new_m = adam_call(terms_m, clock.at(rate_m), [by_slot(v) for v in (master_mlp, moment_mlp, square_mlp)])
    clock.set(new_m[0])
    ring_a.step(clock)
    ring_a.pin(clock)
    while hops:
        norm_sum = norm_hop()
    norm_sum = norm_sum.reshape(2, sub, LANES)
    tokens, dhs = clock.at((tokens, dhs))
    dxs = [last_call(da_terms[j], tokens[cuts[j]], dhs[j], norms) for j in range(CHUNKS)]
    new_a = adam_call(ring_a.terms(), rate_a, [by_slot(v) for v in (master_attn, moment_attn, square_attn)], (*held, norm_sum))
    return (jnp.concatenate(outs, axis=0), jnp.concatenate(dxs, axis=0),
            *(v.reshape(master_attn.shape) for v in new_a), *(v.reshape(master_mlp.shape) for v in new_m))


def solution(mesh):
    tok = P(("dp", "tensor"), None)
    par = P("tensor", "dp", None)
    return jax.shard_map(
        on_device, mesh=mesh,
        in_specs=(tok, tok, P(("dp", "tensor")), P(), P(), par, par, par, par, par, par),
        out_specs=(tok, tok, par, par, par, par, par, par),
        check_vma=False,
    )
```

```python
import functools
import jax
import jax.numpy as jnp
from jax import lax
from jax.sharding import PartitionSpec as P
from jax.experimental import pallas as pl
from jax.experimental.pallas import tpu as pltpu

BF = jnp.bfloat16
F32 = jnp.float32
EPS = 1e-5
HEAD = 64
LANES = 128
QB = 256
CHUNKS = 2
ADAM_STEP = 5


def dot_nn(a, b):
    return lax.dot_general(a, b, (((1,), (0,)), ((), ())), preferred_element_type=F32)


def dot_nt(a, b):
    return lax.dot_general(a, b, (((1,), (1,)), ((), ())), preferred_element_type=F32)


def params(mib):
    return pltpu.CompilerParams(vmem_limit_bytes=mib * 1024 * 1024)


def cost(us):
    return pl.CostEstimate(flops=int(us * 3e7), bytes_accessed=int(us * 1e5), transcendentals=0)


def whole(shape, at=None):
    at = at or (0,) * len(shape)
    return pl.BlockSpec(shape, lambda *_: at)


def shape(dims, dtype):
    return jax.ShapeDtypeStruct(dims, dtype)


def choose(index, refs, into):
    for i in range(4):
        @pl.when(index == i)
        def _():
            if i == 3 and len(refs) == 5:
                half = refs[3].shape[0]
                into[0:half, :] = refs[3][...]
                into[half:, :] = refs[4][...]
            else:
                into[...] = refs[i][...]


def spread(index, refs, value):
    for i in range(4):
        @pl.when(index == i)
        def _():
            if i == 3:
                half = refs[3].shape[0]
                refs[3][...] = value[0:half]
                refs[4][...] = value[half:]
            else:
                refs[i][...] = value


def block_dims(rows, width):
    return [(rows, width)] * 3 + [(rows // 2, width)] * 2


def centre(v):
    mean = jnp.mean(v, axis=-1, keepdims=True)
    vc = v - mean
    s = lax.rsqrt(jnp.mean(vc * vc, axis=-1, keepdims=True) + EPS)
    return vc * s, s


def norm_back(n, s, y, gain):
    dn = y * gain
    return s * (dn - jnp.mean(dn, axis=-1, keepdims=True) - n * jnp.mean(dn * n, axis=-1, keepdims=True))


def total(parts):
    return sum(p[...].astype(F32) for p in parts)


def rows_call(kernel, outs, *args):
    return pl.pallas_call(kernel, out_shape=outs, compiler_params=params(10), cost_estimate=cost(2.5))(*args)


def residual_kernel(p0, p1, p2, x_ref, norms, z_ref, h_ref, c_ref):
    z = total([p0, p1, p2])
    z_ref[...] = z
    n, _ = centre(z)
    h = x_ref[...].astype(F32) + n * norms[2:3, :] + norms[3:4, :]
    h_ref[...] = h
    n, _ = centre(h)
    c_ref[...] = (n * norms[4:5, :] + norms[5:6, :]).astype(BF)


def residual_call(parts, x, norms):
    return rows_call(residual_kernel, [shape(x.shape, F32), shape(x.shape, F32), shape(x.shape, BF)], *parts, x, norms)


def out_kernel(p0, p1, p2, h_ref, ct_ref, wt_ref, norms, lo_ref, dm_ref, dn_ref):
    n, s = centre(total([p0, p1, p2]))
    lo_ref[...] = (h_ref[...] + n * norms[6:7, :] + norms[7:8, :]).astype(BF)
    e = ct_ref[...].astype(F32) * wt_ref[:, 0:1]
    dm_ref[...] = norm_back(n, s, e, norms[6:7, :]).astype(BF)
    dn_ref[0:1, :] = jnp.sum(e * n, axis=0, keepdims=True)
    dn_ref[1:2, :] = jnp.sum(e, axis=0, keepdims=True)


def out_call(parts, h, ct, wt, norms):
    return rows_call(out_kernel, [shape(h.shape, BF), shape(h.shape, BF), shape((2, h.shape[1]), F32)], *parts, h, ct, wt, norms)


def mid_kernel(p0, p1, p2, h_ref, z_ref, ct_ref, wt_ref, norms, dh_ref, dz_ref, dn_ref):
    dc = total([p0, p1, p2])
    n3, s3 = centre(h_ref[...])
    dh = ct_ref[...].astype(F32) * wt_ref[:, 0:1] + norm_back(n3, s3, dc, norms[4:5, :])
    dh_ref[...] = dh
    n2, s2 = centre(z_ref[...])
    dz_ref[...] = norm_back(n2, s2, dh, norms[2:3, :]).astype(BF)
    dn_ref[0:1, :] = jnp.sum(dh * n2, axis=0, keepdims=True)
    dn_ref[1:2, :] = jnp.sum(dh, axis=0, keepdims=True)
    dn_ref[2:3, :] = jnp.sum(dc * n3, axis=0, keepdims=True)
    dn_ref[3:4, :] = jnp.sum(dc, axis=0, keepdims=True)


def mid_call(parts, h, z, ct, wt, norms):
    return rows_call(mid_kernel, [shape(h.shape, F32), shape(h.shape, BF), shape((4, h.shape[1]), F32)],
                     *parts, h, z, ct, wt, norms)


def last_kernel(p0, p1, p2, x_ref, dh_ref, norms, dx_ref):
    n1, s1 = centre(x_ref[...].astype(F32))
    dx_ref[...] = dh_ref[...] + norm_back(n1, s1, total([p0, p1, p2]), norms[0:1, :])


def last_call(parts, x, dh, norms):
    return rows_call(last_kernel, shape(x.shape, F32), *parts, x, dh, norms)


def qkv_kernel(perm, *refs):
    xs, gs, (w_ref, cos_ref, sin_ref, norms, n_ref, qt_ref, kt_ref, vt_ref, k4_ref, v4_ref, cur) = refs[:4], refs[4:8], refs[8:]

    @pl.when(pl.program_id(0) == 0)
    def _():
        for t in range(4):
            for i, g in enumerate(gs):
                @pl.when(perm[t] == i)
                def _():
                    norms[2 * t:2 * t + 2, :] = g[0:2, :]

    choose(pl.program_id(0), xs, cur)
    n, _ = centre(cur[...].astype(F32))
    n_ref[0] = n.astype(BF)
    a = (n * norms[0:1, :] + norms[1:2, :]).astype(BF)
    cos, sin = cos_ref[...], sin_ref[...]
    dims = qt_ref.shape[0]
    half = HEAD // 2
    for part in range(3):
        proj = dot_nt(w_ref[part * dims:(part + 1) * dims, :], a)
        for h in range(dims // HEAD):
            lo = slice(h * HEAD, h * HEAD + half)
            hi = slice(h * HEAD + half, (h + 1) * HEAD)
            hd = slice(h * HEAD, (h + 1) * HEAD)
            if part < 2:
                first, second = proj[lo], proj[hi]
                r1 = first * cos - second * sin
                r2 = second * cos + first * sin
                if part == 0:
                    qt_ref[lo, :] = (r1 * 0.125).astype(BF)
                    qt_ref[hi, :] = (r2 * 0.125).astype(BF)
                else:
                    full = jnp.concatenate([r1, r2], axis=0)
                    kt_ref[hd, :] = full.astype(BF)
                    k4_ref[h] = full.T.astype(BF)
            else:
                vt_ref[hd, :] = proj[hd].astype(BF)
                v4_ref[h] = proj[hd].T.astype(BF)


def qkv_call(perm, xs, gains, w, cos_t, sin_t):
    rows, width = xs[0].shape
    n = len(xs)
    dims = w.shape[0] // 4
    heads = dims // HEAD
    length = n * rows
    tok = pl.BlockSpec((dims, rows), lambda k, p: (0, p[k]))
    hd = pl.BlockSpec((heads, rows, HEAD), lambda k, p: (0, p[k], 0))
    tab = pl.BlockSpec((HEAD // 2, rows), lambda k, p: (0, p[k]))
    return pl.pallas_call(
        qkv_kernel,
        grid_spec=pltpu.PrefetchScalarGridSpec(
            num_scalar_prefetch=1, grid=(n,),
            in_specs=[whole((rows, width))] * n + [whole(g.shape) for g in gains] + [whole((3 * dims, width)), tab, tab],
            out_specs=[whole((8, width)), pl.BlockSpec((1, rows, width), lambda k, p: (k, 0, 0)), tok, tok, tok, hd, hd],
            scratch_shapes=[pltpu.VMEM((rows, width), BF)],
        ),
        out_shape=[shape((8, width), F32), shape((n, rows, width), BF)] + [shape((dims, length), BF)] * 3 + [shape((heads, length, HEAD), BF)] * 2,
        compiler_params=params(20), cost_estimate=cost(10),
    )(perm, *xs, *gains, w, cos_t, sin_t)


def visible(chunk, diag):
    return (lax.broadcasted_iota(jnp.int32, (diag, QB), 0)
            <= lax.broadcasted_iota(jnp.int32, (diag, QB), 1) + chunk * QB)


def key_spans(n, wide, diag):
    return ([pl.ds(0, n * wide)] if n else []) + [pl.ds(n * wide, diag)]


def pipelined(heads, first, second, third):
    ahead, behind = first(0), None
    for h in range(heads):
        now = ahead
        if h + 1 < heads:
            ahead = first(h + 1)
        done = second(h, now)
        if behind is not None:
            third(h - 1, behind)
        behind = done
    third(heads - 1, behind)


def attn_fwd_kernel(chunk, chunks, count, perm, qt_ref, k4_ref, vt_ref, wo_ref, *rest):
    zs, (ot_ref, lse_ref, acc) = rest[:5], rest[5:]
    t = pl.program_id(0)
    heads = qt_ref.shape[0] // HEAD
    diag = (chunk + 1) * QB
    seen = visible(chunk, diag)
    hd = [slice(h * HEAD, (h + 1) * HEAD) for h in range(heads)]

    def one_row(n):
        spans = key_spans(n, chunks * QB, diag)

        def scores(h):
            return [dot_nn(k4_ref[h, ks, :], qt_ref[hd[h], :]) for ks in spans]

        def soft(h, s):
            s = s[:-1] + [jnp.where(seen, s[-1], -1e30)]
            m = functools.reduce(jnp.maximum, [jnp.max(v, axis=0, keepdims=True) for v in s])
            p = [jnp.exp(v - m) for v in s]
            l = sum(jnp.sum(v, axis=0, keepdims=True) for v in p)
            lse_ref[h:h + 1, :] = m + jnp.log(l)
            return [v.astype(BF) for v in p], l

        def attend(h, done):
            acc[hd[h], :] = sum(dot_nn(vt_ref[hd[h], ks], v) for ks, v in zip(spans, done[0])) / done[1]

        pipelined(heads, scores, soft, attend)

    for n in range(count):
        pl.when(t == n)(functools.partial(one_row, n))
    o = acc[...]
    ot_ref[...] = o.astype(BF)
    spread(perm[t], zs, dot_nn(o.T.astype(BF), wo_ref[...]).astype(BF))


def attn_fwd_call(chunk, chunks, perm, qt, k4, vt, w):
    dims, length = qt.shape
    width = w.shape[1]
    heads = dims // HEAD
    n = length // (chunks * QB)
    return pl.pallas_call(
        functools.partial(attn_fwd_kernel, chunk, chunks, n),
        grid_spec=pltpu.PrefetchScalarGridSpec(
            num_scalar_prefetch=1, grid=(n,),
            in_specs=[
                pl.BlockSpec((dims, QB), lambda t, p: (0, chunks * t + chunk)),
                whole(k4.shape), whole(vt.shape), whole((dims, width), (3, 0))],
            out_specs=[whole(d) for d in block_dims(QB, width)] + [
                pl.BlockSpec((dims, QB), lambda t, p: (0, t)), pl.BlockSpec((heads, QB), lambda t, p: (0, t))],
            scratch_shapes=[pltpu.VMEM((dims, QB), F32)],
        ),
        out_shape=[shape(d, BF) for d in block_dims(QB, width)] + [shape((dims, n * QB), BF), shape((heads, n * QB), F32)],
        compiler_params=params(14), cost_estimate=cost(9.5 + 1.5 * chunk),
    )(perm, qt, k4, vt, w)


def attn_bwd_kernel(chunk, chunks, count, pair, perm, *refs):
    dzs, refs = refs[:5], refs[5:]
    wo_ref, qt_ref, k4_ref, kt_ref, v4_ref, ot_ref, lse_ref, cos_ref, sin_ref = refs[:9]
    refs = refs[9:]
    if chunk == 0:
        dq_ref, dk_ref, dv_ref, gwo_ref, acc, dot_ref, dl_ref, dz_ref = refs
    else:
        dk0, dv0, gwo0, dq_ref, dkl_ref, dvl_ref, gwo_ref, acc, dot_ref, dl_ref, dz_ref, dk_ref, dv_ref = refs
    heads = k4_ref.shape[0]
    half = HEAD // 2
    wide = chunks * QB
    diag = (chunk + 1) * QB
    seen = visible(chunk, diag)
    hd = [slice(h * HEAD, (h + 1) * HEAD) for h in range(heads)]
    cols = [slice(t * QB, (t + 1) * QB) for t in range(count)]
    mine = [slice((chunks * t + chunk) * QB, (chunks * t + chunk + 1) * QB) for t in range(count)]
    if chunk == 0:
        dk_ref[...] = jnp.zeros_like(dk_ref)
        dv_ref[...] = jnp.zeros_like(dv_ref)
    else:
        dk_ref[...] = dk0[...]
        dv_ref[...] = dv0[...]
    for t in range(count):
        choose(perm[t], dzs, dz_ref.at[t])
        dot_ref[:, cols[t]] = dot_nt(wo_ref[...], dz_ref[t]).astype(BF)
    prod = dot_ref[...].astype(F32) * ot_ref[...].astype(F32)
    for h in range(heads):
        dl_ref[h:h + 1, :] = jnp.sum(prod[hd[h]], axis=0, keepdims=True)

    def unit(u):
        t, h = u // heads, u % heads
        return t, h, key_spans(t, wide, diag)

    def scores(u):
        t, h, spans = unit(u)
        return [(dot_nn(k4_ref[h, ks, :], qt_ref[hd[h], mine[t]]), dot_nn(v4_ref[h, ks, :], dot_ref[hd[h], cols[t]])) for ks in spans]

    def soft(u, pairs):
        t, h, spans = unit(u)
        lse, delta = lse_ref[heads * pair + h:heads * pair + h + 1, cols[t]], dl_ref[h:h + 1, cols[t]]
        out = []
        for i, (s, dp) in enumerate(pairs):
            p = jnp.exp(s - lse)
            if i == len(pairs) - 1:
                p = jnp.where(seen, p, 0.0)
            out.append((p.astype(BF), (p * (dp - delta)).astype(BF)))
        return out

    def back(u, pairs):
        t, h, spans = unit(u)
        q, do = qt_ref[hd[h], mine[t]], dot_ref[hd[h], cols[t]]
        dq = 0.0
        for ks, (p, ds) in zip(spans, pairs):
            dv_ref[hd[h], ks] += dot_nt(do, p)
            dk_ref[hd[h], ks] += dot_nt(q, ds)
            dq = dq + dot_nn(kt_ref[hd[h], ks], ds)
        acc[hd[h], cols[t]] = dq

    pipelined(heads * count, scores, soft, back)
    g = dot_nn(ot_ref[...], dz_ref[...].reshape(count * QB, dz_ref.shape[2]))
    gwo_ref[...] = g if chunk == 0 else gwo0[...] + g

    def unturn(src, at, to, scale, out):
        cos, sin = cos_ref[:, at], sin_ref[:, at]
        for h in range(heads):
            lo = slice(h * HEAD, h * HEAD + half)
            hi = slice(h * HEAD + half, (h + 1) * HEAD)
            g1, g2 = src[lo, to] * scale, src[hi, to] * scale
            out[lo, to] = (g1 * cos + g2 * sin).astype(BF)
            out[hi, to] = (g2 * cos - g1 * sin).astype(BF)

    for t in range(count):
        unturn(acc, mine[t], cols[t], 0.125, dq_ref)
    if chunk == chunks - 1:
        unturn(dk_ref, slice(None), slice(None), 1.0, dkl_ref)
        dvl_ref[...] = dv_ref[...].astype(BF)


def attn_bwd_call(chunk, chunks, pair, perm, dzs, w, qt, k4, kt, v4, ot, lse, cos_t, sin_t, prev=()):
    dims, length = qt.shape[0] // 2, qt.shape[1]
    width = w.shape[1]
    heads = dims // HEAD
    n = length // (chunks * QB)
    full, tb = whole((dims, length), (pair, 0)), whole((dims, n * QB), (pair, 0))
    kv4 = whole((heads, length, HEAD), (pair, 0, 0))
    out_full, out_tb, out_w = whole((dims, length)), whole((dims, n * QB)), whole((dims, width))
    in_specs = [whole(d) for d in block_dims(QB, width)] + [
        whole((dims, width), (6 + pair, 0)), full, kv4, full, kv4, tb, whole(lse.shape), whole(cos_t.shape), whole(sin_t.shape)]
    scratch = [pltpu.VMEM((dims, n * QB), F32), pltpu.VMEM((dims, n * QB), BF), pltpu.VMEM((8, n * QB), F32), pltpu.VMEM((n, QB, width), BF)]
    kv = F32
    if chunk:
        in_specs += [out_full, out_full, out_w]
        scratch += [pltpu.VMEM((dims, length), F32)] * 2
        kv = BF
    return pl.pallas_call(
        functools.partial(attn_bwd_kernel, chunk, chunks, n, pair),
        grid_spec=pltpu.PrefetchScalarGridSpec(
            num_scalar_prefetch=1, grid=(1,), in_specs=in_specs,
            out_specs=[out_tb, out_full, out_full, out_w], scratch_shapes=scratch,
        ),
        out_shape=[shape((dims, n * QB), BF), shape((dims, length), kv), shape((dims, length), kv), shape((dims, width), F32)],
        compiler_params=params(22), cost_estimate=cost(10 + 2 * chunk),
    )(perm, *dzs, w, qt, k4, kt, v4, ot, lse, cos_t, sin_t, *prev)


def stack_rows(refs, into, cols=slice(None)):
    at = 0
    for r in refs:
        into[at:at + r.shape[0], cols] = r[...]
        at += r.shape[0]


def qkv_in_kernel(perm, *refs):
    parts, w_ref, das, dx = refs[:6], refs[6], refs[7:12], refs[12]
    stack_rows(parts, dx)
    grad = dx[...].astype(F32).T.astype(BF)
    spread(perm[pl.program_id(0)], das, dot_nn(grad, w_ref[...]).astype(BF))


def qkv_in_call(chunk, chunks, perm, dq, dk, dv, w):
    dims, length = dk[0].shape
    width = w.shape[1]
    n = length // (chunks * QB)
    at = pl.BlockSpec((dims, QB), lambda t, p: (0, chunks * t + chunk))
    return pl.pallas_call(
        qkv_in_kernel,
        grid_spec=pltpu.PrefetchScalarGridSpec(
            num_scalar_prefetch=1, grid=(n,),
            in_specs=[pl.BlockSpec((dims, QB), lambda t, p: (0, t))] * 2 + [at] * 4 + [whole((6 * dims, width))],
            out_specs=[whole(d) for d in block_dims(QB, width)],
            scratch_shapes=[pltpu.VMEM((6 * dims, QB), BF)],
        ),
        out_shape=[shape(d, BF) for d in block_dims(QB, width)],
        compiler_params=params(8), cost_estimate=cost(5),
    )(perm, *dq, *dk, *dv, w)


def qkv_grad_kernel(chunks, count, perm, *refs):
    dqs, kvs, refs = refs[:2 * chunks], refs[2 * chunks:2 * chunks + 4], refs[2 * chunks + 4:]
    d23, d4, (n_ref, w_ref, norms, gw_ref), dns, (dx, rows, sums_ref) = refs[:chunks], refs[chunks:2 * chunks], refs[2 * chunks:2 * chunks + 4], refs[2 * chunks + 4:2 * chunks + 8], refs[2 * chunks + 8:]
    dims = kvs[0].shape[0]
    wide = chunks * QB

    @pl.when(pl.program_id(0) == 0)
    def _():
        for i in range(chunks):
            for p in range(2):
                for t in range(count):
                    to = slice(t * wide + i * QB, t * wide + (i + 1) * QB)
                    dx[p * dims:(p + 1) * dims, to] = dqs[2 * i + p][:, t * QB:(t + 1) * QB]
        stack_rows(kvs, dx.at[2 * dims:])
        sums_ref[...] = jnp.sum(dx[...].astype(F32), axis=1, keepdims=True)

    grad = sum(dot_nn(dx[:, t * wide:(t + 1) * wide], n_ref[perm[t]]) for t in range(count))
    sums = sums_ref[...]
    w = w_ref[...].astype(F32)
    gw_ref[...] = (grad * norms[0:1, :] + sums * norms[1:2, :]).astype(BF)
    rows[0:1, :] = jnp.sum(grad * w, axis=0, keepdims=True)
    rows[1:2, :] = jnp.sum(sums * w, axis=0, keepdims=True)
    rows[2:6, :] = total(d23)
    rows[6:8, :] = total(d4)
    for i, out in enumerate(dns):
        for t in range(4):
            @pl.when(perm[i] == t)
            def _():
                out[...] = rows[2 * t:2 * t + 2, :]


def qkv_grad_call(perm, dqs, dk, dv, d23, d4, n_rel, w, norms):
    chunks = len(dqs)
    n, rows, width = n_rel.shape
    dims = dk[0].shape[0]
    cols = 256
    args = [v for dq in dqs for v in dq] + [*dk, *dv]
    return pl.pallas_call(
        functools.partial(qkv_grad_kernel, chunks, n),
        grid_spec=pltpu.PrefetchScalarGridSpec(
            num_scalar_prefetch=1, grid=(width // cols,),
            in_specs=[whole(v.shape) for v in args] + [pl.BlockSpec((v.shape[0], cols), lambda i, p: (0, i)) for v in (*d23, *d4)] + [
                pl.BlockSpec((n, rows, cols), lambda i, p: (0, 0, i)), pl.BlockSpec((6 * dims, cols), lambda i, p: (0, i)),
                pl.BlockSpec((8, cols), lambda i, p: (0, i))],
            out_specs=[pl.BlockSpec((6 * dims, cols), lambda i, p: (0, i))] + [pl.BlockSpec((2, cols), lambda i, p: (0, i))] * 4,
            scratch_shapes=[pltpu.VMEM((6 * dims, n * rows), BF), pltpu.VMEM((8, cols), F32), pltpu.VMEM((6 * dims, 1), F32)],
        ),
        out_shape=[shape((6 * dims, width), BF)] + [shape((2, width), F32)] * 4,
        compiler_params=params(16), cost_estimate=cost(7),
    )(perm, *args, *d23, *d4, n_rel, w, norms)


def mlp_fwd_kernel(*refs):
    cs, (w1_ref, w2_ref), ms, (c_ref, r_ref, g_ref) = refs[:5], refs[5:7], refs[7:12], refs[12:]
    k = pl.program_id(0)
    choose(k, cs, c_ref.at[0])
    u = dot_nt(c_ref[0], w1_ref[...])
    cdf = 0.5 * (1.0 + lax.erf(u * 0.7071067811865476))
    r = (u * cdf).astype(BF)
    r_ref[0] = r
    g_ref[0] = (cdf + u * (0.3989422804014327 * jnp.exp(-0.5 * u * u))).astype(BF)
    spread(k, ms, dot_nn(r, w2_ref[...]).astype(BF))


def mlp_fwd_call(cs, w):
    rows, width = cs[0].shape
    n, hid = 4, w.shape[0] // 2
    dims = block_dims(rows, width)
    blk = pl.BlockSpec((1, rows, width), lambda k: (k, 0, 0))
    hb = pl.BlockSpec((1, rows, hid), lambda k: (k, 0, 0))
    return pl.pallas_call(
        mlp_fwd_kernel, grid=(n,),
        in_specs=[whole(c.shape) for c in cs] + [whole((hid, width), (0, 0)), whole((hid, width), (1, 0))],
        out_specs=[whole(d) for d in dims] + [blk, hb, hb],
        out_shape=[shape(d, BF) for d in dims] + [shape((n, rows, width), BF)] + [shape((n, rows, hid), BF)] * 2,
        compiler_params=params(16), cost_estimate=cost(9),
    )(*cs, w, w)


def mlp_bwd_kernel(*refs):
    dms, (g_ref, w1_ref, w2_ref), dcs, (dm_ref, du_ref) = refs[:5], refs[5:8], refs[8:13], refs[13:]
    k = pl.program_id(0)
    choose(k, dms, dm_ref.at[0])
    dr = dot_nt(dm_ref[0], w2_ref[...])
    du = (dr * g_ref[0].astype(F32)).astype(BF)
    du_ref[0] = du
    spread(k, dcs, dot_nn(du, w1_ref[...]).astype(BF))


def mlp_bwd_call(dms, g, w):
    rows, width = dms[0].shape
    n, hid = 4, w.shape[0] // 2
    dims = block_dims(rows, width)
    blk = pl.BlockSpec((1, rows, width), lambda k: (k, 0, 0))
    hb = pl.BlockSpec((1, rows, hid), lambda k: (k, 0, 0))
    return pl.pallas_call(
        mlp_bwd_kernel, grid=(n,),
        in_specs=[whole(d.shape) for d in dms] + [hb, whole((hid, width), (0, 0)), whole((hid, width), (1, 0))],
        out_specs=[whole(d) for d in dims] + [blk, hb],
        out_shape=[shape(d, BF) for d in dims] + [shape((n, rows, width), BF), shape((n, rows, hid), BF)],
        compiler_params=params(16), cost_estimate=cost(8),
    )(*dms, g, w, w)


def place_kernel(sizes, count, starts, pieces, *refs):
    srcs, out_ref, rest_ref, mid = refs[:-3], refs[-3], refs[-2], refs[-1]
    sub = srcs[0].shape[1]
    for k, src in enumerate(srcs):
        base = starts[k]
        step = next(u for u in (8, 6, 4, 3, 2, 1) if sizes[k] % u == 0)

        def body(i, c, src=src, base=base, step=step):
            for u in range(step):
                n = i * step + u
                to = pieces[base + n]
                mid[pl.ds(pl.multiple_of(to * sub, sub), sub), :] = src[n].astype(F32)
            return c

        lax.fori_loop(0, sizes[k] // step, body, 0)
    rows = 64

    def spread(i, c):
        r = pl.multiple_of(i * rows, rows)
        for j in range(sub):
            part = mid[pl.ds(r * sub + j, rows, stride=sub), :]
            out_ref[pl.ds(r, rows), j * LANES:(j + 1) * LANES] = part.astype(BF)
        return c

    lax.fori_loop(0, count // rows, spread, 0)
    for j in range(sub):
        rest_ref[:, j * LANES:(j + 1) * LANES] = mid[pl.ds(count * sub + j, 8, stride=sub), :]


def place_call(blocks, starts, pieces, count):
    sub = blocks[0].shape[1]
    sizes = [b.shape[0] for b in blocks]
    return pl.pallas_call(
        functools.partial(place_kernel, sizes, count),
        grid_spec=pltpu.PrefetchScalarGridSpec(
            num_scalar_prefetch=2, grid=(1,),
            in_specs=[whole(b.shape) for b in blocks],
            out_specs=[whole((count, sub * LANES)), whole((8, sub * LANES))],
            scratch_shapes=[pltpu.VMEM(((count + 8) * sub, LANES), F32)],
        ),
        out_shape=[shape((count, sub * LANES), BF), shape((8, sub * LANES), F32)],
        compiler_params=params(10 + count // 146), cost_estimate=cost(count / 450),
    )(starts, pieces, *blocks)


def bucket_kernel(sizes, starts, pieces, *refs):
    n = len(sizes)
    grads, outs, mid = refs[:-n - 1], refs[-n - 1:-1], refs[-1]
    width = grads[0].shape[1]
    sub = width // LANES
    rows = 64
    at = 0
    for g in grads:
        if g.shape[0] % rows:
            for j in range(sub):
                mid[pl.ds(at * sub + j, g.shape[0], stride=sub), :] = g[:, j * LANES:(j + 1) * LANES].astype(F32)
            at += g.shape[0]
            continue

        def split(i, c, g=g, at=at):
            r = pl.multiple_of(i * rows, rows)
            for j in range(sub):
                mid[pl.ds((at + r) * sub + j, rows, stride=sub), :] = g[pl.ds(r, rows), j * LANES:(j + 1) * LANES].astype(F32)
            return c

        lax.fori_loop(0, g.shape[0] // rows, split, 0)
        at += g.shape[0]
    mid[at * sub:(at + 8) * sub, :] = jnp.zeros((8 * sub, LANES), F32)
    for k, out in enumerate(outs):
        base = starts[k]
        step = next(u for u in (8, 6, 4, 3, 2, 1) if sizes[k] % u == 0)

        def body(i, c, out=out, base=base, step=step):
            for u in range(step):
                m = i * step + u
                src = pieces[base + m]
                out[m] = mid[pl.ds(pl.multiple_of(src * sub, sub), sub), :].astype(BF)
            return c

        lax.fori_loop(0, sizes[k] // step, body, 0)


def bucket_call(grads, starts, pieces, sizes):
    width = grads[0].shape[1]
    sub = width // LANES
    count = sum(g.shape[0] for g in grads)
    shapes = [(s, sub, LANES) for s in sizes]
    return pl.pallas_call(
        functools.partial(bucket_kernel, sizes),
        grid_spec=pltpu.PrefetchScalarGridSpec(
            num_scalar_prefetch=2, grid=(1,),
            in_specs=[whole(g.shape) for g in grads],
            out_specs=[whole(s) for s in shapes],
            scratch_shapes=[pltpu.VMEM(((count + 8) * sub, LANES), F32)],
        ),
        out_shape=[jax.ShapeDtypeStruct(s, BF) for s in shapes],
        compiler_params=params(8 + count // 146), cost_estimate=cost(count / 350),
    )(starts, pieces, *grads)


def adam_kernel(bounds, *refs):
    parts, (rate, m_ref, f_ref, s_ref, om, of, os) = refs[:-7], refs[-7:]
    each = len(parts) // len(bounds)
    for i, (lo, hi) in enumerate(bounds):
        at = slice(lo, hi)
        g = total(parts[i * each:(i + 1) * each])
        first = 0.5 * f_ref[at] + 0.5 * g
        second = 0.5 * s_ref[at] + 0.5 * g * g
        of[at] = first
        os[at] = second
        w = m_ref[at]
        first = first / (1.0 - 0.5**ADAM_STEP)
        second = second / (1.0 - 0.5**ADAM_STEP)
        om[at] = w - rate[at] * (first / (jnp.sqrt(second) + 1e-8) + 0.1 * w)


def adam_call(bounds, parts, rate, states):
    cap, sub, lanes = states[0].shape
    step = next(d for d in range(64, 0, -1) if cap % d == 0) if len(bounds) == 1 else cap
    if len(bounds) == 1:
        bounds = [(0, step)]
    blk = pl.BlockSpec((step, sub, lanes), lambda i: (i, 0, 0))
    terms = [v for part in parts for v in part]
    return pl.pallas_call(
        functools.partial(adam_kernel, bounds), grid=(cap // step,),
        in_specs=[blk if len(bounds) == 1 else whole(v.shape) for v in terms] + [
            pl.BlockSpec((step, 1, lanes), lambda i: (i, 0, 0))] + [blk] * 3,
        out_specs=[blk] * 3,
        out_shape=[shape(v.shape, F32) for v in states],
        compiler_params=params(12), cost_estimate=cost(cap / 80),
    )(*terms, rate, *states)


def low_kernel(bounds, x_ref, *outs):
    for (lo, hi), out in zip(bounds, outs):
        out[...] = x_ref[lo:hi].astype(BF)


def low_call(bounds, v):
    return list(pl.pallas_call(
        functools.partial(low_kernel, bounds), out_shape=[shape((hi - lo, *v.shape[1:]), BF) for lo, hi in bounds],
        compiler_params=params(6), cost_estimate=cost(1),
    )(v))


TOP = [(0, 1), (1, 0), (2, 3), (3, 2)]
SIDE = [(0, 2), (1, 3), (2, 0), (3, 1)]
RINGS = {8: [0, 2, 4, 6, 7, 5, 3, 1]}


def to_core(v):
    return lax.ppermute(v, "tensor", TOP)


def to_chip(v):
    return lax.ppermute(v, "tensor", SIDE)


def after(v, *first):
    if not first:
        return v
    return lax.optimization_barrier((v, *first))[0]


class Clock:
    def __init__(self):
        self.last = []

    def set(self, *values):
        self.last = list(values)

    def add(self, value):
        self.last.append(value)

    def at(self, value):
        return lax.optimization_barrier((value, *self.last))[0] if self.last else value


def gather_rel(own):
    side = to_chip(own)
    return [own, to_core(own), side, to_core(side)]


class Owners:
    def __init__(self, cap, halves):
        self.cap, self.count = cap, lax.axis_size("dp")
        self.ring = RINGS.get(self.count)
        self.cut = cap // 2 // 8 * 8
        if self.ring:
            n, ring = self.count, self.ring
            self.right = [(ring[i], ring[(i + 1) % n]) for i in range(n)]
            self.left = [(b, a) for a, b in self.right]
            self.far = n // 2
            self.parts = [(0, self.cut), (self.cut, cap)] if halves else [(0, cap)]
            hops = [0] + [h for s in range(1, self.far) for h in (-s, s)]
            ends = [(0, self.cut), (self.cut, cap)]
            self.sizes = [hi - lo for _ in hops for lo, hi in self.parts] + [hi - lo for lo, hi in ends]
            table = [[] for _ in ring]
            for i, d in enumerate(ring):
                table[d] = [ring[(i + h) % n] * cap + lo for h in hops for lo, _ in self.parts]
                table[d] += [ring[(i + self.far) % n] * cap + lo for lo, _ in ends]
            self.starts = lax.dynamic_index_in_dim(jnp.asarray(table, jnp.int32), lax.axis_index("dp"), 0, keepdims=False)
        else:
            self.parts = [(0, cap)]
            self.sizes = [self.count * cap]
            self.starts = jnp.zeros((1,), jnp.int32)

    def go(self, a, b):
        return [lax.ppermute(v, "dp", self.right) for v in a], [lax.ppermute(v, "dp", self.left) for v in b]


class GatherSteps:
    def __init__(self, own, shard):
        self.own, self.out, self.s = own, list(shard), 1
        self.a = self.b = list(shard)
        self.sent = []
        if own.ring:
            self.step(Clock())

    def step(self, clock):
        own = self.own
        if not own.ring or self.s > own.far:
            return
        a, b = clock.at((self.a, self.b))
        if self.s == own.far:
            a, b = ([a[0]], [b[1]]) if len(own.parts) == 2 else ([a[0][:own.cut]], [b[0][own.cut:]])
        self.sent = [*a, *b]
        self.a, self.b = own.go(a, b)
        self.out += [*self.a, *self.b]
        self.s += 1

    def pin(self, clock):
        for v in self.sent:
            clock.add(v)

    def blocks(self):
        if not self.own.ring:
            return [lax.all_gather(self.out[0], "dp", axis=0, tiled=True)]
        while self.s <= self.own.far:
            self.step(Clock())
        return list(self.out)


class ScatterSteps:
    def __init__(self, own, blocks):
        self.own, self.blocks, self.s = own, blocks, own.count // 2 - 1
        self.sent = []
        if own.ring:
            self.a, self.b = own.go([blocks[-2]], [blocks[-1]])

    def more(self):
        return self.own.ring and self.s > 0

    def step(self, clock):
        own, s = self.own, self.s
        if not self.more():
            return

        def add(x, y):
            return (x.astype(F32) + y.astype(F32)).astype(BF)

        n = len(own.parts)
        y, x = (list(clock.at(self.blocks[m * n:(m + 1) * n])) for m in (2 * s - 1, 2 * s))
        a, b = self.a, self.b
        if s < own.far - 1:
            a, b = [add(v, w) for v, w in zip(x, a)], [add(v, w) for v, w in zip(y, b)]
        elif n == 2:
            a, b = [add(x[0], a[0]), x[1]], [y[0], add(y[1], b[0])]
        else:
            a = [lax.dynamic_update_slice_in_dim(x[0], add(x[0][:own.cut], a[0]), 0, 0)]
            b = [lax.dynamic_update_slice_in_dim(y[0], add(y[0][own.cut:], b[0]), own.cut, 0)]
        self.sent = [*a, *b]
        self.a, self.b = own.go(a, b)
        self.s -= 1

    def pin(self, clock):
        for v in self.sent:
            clock.add(v)

    def terms(self):
        own, blocks = self.own, self.blocks
        if own.ring:
            return [list(v) for v in zip(blocks[:len(own.parts)], self.a, self.b)]
        pad = -own.cap % 8
        v = blocks[0].reshape(own.count, own.cap, *blocks[0].shape[1:])
        v = jnp.pad(v, ((0, 0), (0, pad), (0, 0), (0, 0))).reshape(-1, *blocks[0].shape[1:])
        return [[lax.psum_scatter(v, "dp", scatter_dimension=0, tiled=True)[:own.cap]]]


def slot_rows(assign, slots):
    n = assign.shape[0]
    here = lax.broadcasted_iota(jnp.int32, (n, slots), 1) == assign[:, None]
    back = lax.broadcasted_iota(jnp.int32, (n, slots), 0) - n
    return jnp.sum(jnp.where(here, back, 0), axis=0) + n


def rotary_tables(places):
    half = HEAD // 2
    frequency = 10000.0 ** (-jnp.arange(half, dtype=F32) / half)
    angles = frequency[:, None] * places.astype(F32)[None, :]
    return jnp.cos(angles), jnp.sin(angles)


def on_device(tokens, cotangent, group_ids, assign_attn, assign_mlp,
              master_attn, moment_attn, square_attn, master_mlp, moment_mlp, square_mlp):
    owners = lax.axis_size("dp")
    tensor = lax.axis_size("tensor")
    rows_here, width = tokens.shape
    sub = width // LANES
    length = rows_here * tensor
    me, owner = lax.axis_index("tensor"), lax.axis_index("dp")
    perm = jnp.arange(tensor, dtype=jnp.int32) ^ me
    n_attn, n_mlp = width, assign_mlp.shape[0]
    dims, hidden = width // tensor, n_mlp // 2
    cap_a, cap_m = master_attn.shape[1], master_mlp.shape[1]
    part_rows = rows_here // CHUNKS
    cuts = [slice(j * part_rows, (j + 1) * part_rows) for j in range(CHUNKS)]

    def by_slot(v):
        return v.reshape(v.shape[1], sub, LANES)

    own_a, own_m = Owners(cap_a, False), Owners(cap_m, False)
    slots_a = owner * cap_a + jnp.arange(cap_a, dtype=jnp.int32)
    slots_m = owner * cap_m + jnp.arange(cap_m, dtype=jnp.int32)
    low_a = low_call(own_a.parts, after(by_slot(master_attn), perm, own_a.starts, own_m.starts, slots_a, slots_m))

    def named(slots, part):
        return jnp.any(slots[:, None] == part[None, :], axis=1)

    ring_a = GatherSteps(own_a, low_a)
    side = to_chip(after(tokens, low_a[0]))

    def per_slot(v):
        return jnp.broadcast_to(v.astype(F32)[:, None, None], (v.shape[0], 1, LANES))

    def beside(made):
        made, ring_a.a, ring_a.b = lax.optimization_barrier((made, ring_a.a, ring_a.b))
        return made

    pieces_a = beside(slot_rows(after(assign_attn, low_a[0]), owners * cap_a))
    tokens_near = to_core(after(tokens, pieces_a))
    names_m = after(assign_mlp, ring_a.a[0])
    ring_a.step(Clock())
    pieces_m = beside(slot_rows(names_m, owners * cap_m))
    states_m, places, groups = after((by_slot(master_mlp), jnp.arange(length, dtype=jnp.int32), group_ids), ring_a.a[0])
    ring_a.step(Clock())
    weight = jnp.broadcast_to((0.5 + 0.5 * groups.astype(F32))[:, None], (rows_here, LANES))
    weight, low_m, (cos_t, sin_t) = beside((weight, low_call(own_m.parts, states_m), rotary_tables(places)))
    names_a, names_m = after((assign_attn, assign_mlp), ring_a.a[0])
    ring_a.step(Clock())
    in_norm = (slots_a == names_a[n_attn]) | (slots_a == names_a[n_attn + 1])
    rate_a = per_slot(jnp.where(in_norm, 0.2, jnp.where(named(slots_a, names_a[3 * dims:n_attn]), 0.4, 0.06)))
    rate_m = per_slot(jnp.where(named(slots_m, names_m[hidden:]), 0.03, 0.06))
    rate_a, rate_m = beside((rate_a, rate_m))
    if own_a.ring:
        ring_a.out[-2:] = [*ring_a.a, *ring_a.b]
    side = after(side, *ring_a.sent)
    xs = [tokens, tokens_near, side, to_core(side)]
    blocks_a = ring_a.blocks()
    clock = Clock()
    clock.set(xs[3])
    blocks_a[0] = clock.at(blocks_a[0])
    w_attn, held_norms = place_call(blocks_a, own_a.starts, pieces_a, n_attn)
    clock.set(w_attn)
    ring_m = GatherSteps(own_m, after(low_m, *blocks_a[-2:]))
    norms_side = to_chip(held_norms)
    gains = [held_norms, to_core(held_norms), norms_side, to_core(norms_side)]
    norms, n_rel, qt, kt, vt, k4, v4 = qkv_call(perm, xs, gains, w_attn, cos_t, sin_t)
    clock.set(qt)
    ring_m.step(clock)
    ring_m.pin(clock)

    def summed(parts, *first):
        far = [to_core(clock.at(p)) for p in parts[3:]]
        near = to_core(parts[1])
        half = far[0].shape[0]
        sent = [(parts[2][i * half:(i + 1) * half].astype(F32) + f.astype(F32)).astype(BF) for i, f in enumerate(far)]
        sent = after(jnp.concatenate(sent, axis=0), *first)
        clock.set(sent)
        return parts[0], near, to_chip(sent)

    fwd = []
    for j in range(CHUNKS):
        *zp, ot, lse = attn_fwd_call(j, CHUNKS, perm, clock.at(qt), k4, vt, w_attn)
        clock.set(ot)
        if j:
            clock.add(fwd[-1][0][2])
        ring_m.step(clock)
        terms = summed(zp, *ring_m.sent)
        fwd.append((terms, ot, lse))
    state, sides = [], []
    blocks_m = ring_m.blocks()
    for j in range(CHUNKS):
        z, h, c = residual_call(fwd[j][0], clock.at(tokens[cuts[j]]), norms)
        clock.set(c)
        state.append((z, h, c))
        sides.append((to_core(c), to_chip(c)))
        if j == 0:
            blocks_m[0] = clock.at(blocks_m[0])
            w_mlp, _ = place_call(blocks_m, own_m.starts, pieces_m, n_mlp)
            clock.set(w_mlp)
            clock.add(fwd[1][0][2])

    def gathered(own, near, side):
        half = side.shape[0] // 2
        side = clock.at(side)
        return [own, near, side, to_core(side[:half]), to_core(side[half:])]

    mids = []
    for j in range(CHUNKS):
        cs = gathered(state[j][2], *sides[j])
        cs[0] = clock.at(cs[0])
        *mp, c_rel, r, g = mlp_fwd_call(cs, w_mlp)
        clock.set(r)
        clock.add(sides[1][1] if j == 0 else mids[0][0][2])
        mids.append((summed(mp), c_rel, r, g))
    outs, sides, dms = [], [], []
    dnorm4 = []
    for j in range(CHUNKS):
        z, h, c = state[j]
        clock.add(mids[j][0][2])
        lo, dm, dn = out_call(mids[j][0], clock.at(h), cotangent[cuts[j]], weight[cuts[j]], norms)
        clock.set(dm)
        outs.append(lo)
        dnorm4.append(dn)
        dms.append(dm)
        sides.append((to_core(dm), to_chip(dm)))

    backs = []
    for j in range(CHUNKS):
        args = gathered(dms[j], *sides[j])
        args[0] = clock.at(args[0])
        *dcp, dm_rel, du = mlp_bwd_call(args, mids[j][3], w_mlp)
        clock.set(du)
        clock.add(sides[1][1] if j == 0 else backs[0][0][2])
        backs.append((summed(dcp), dm_rel, du))
    toks = (((0, 1), (0, 1)), ((), ()))

    def over_tokens(x, y):
        return lax.dot_general(x, y, toks, preferred_element_type=F32)

    dhs, dzs, sides = [], [], []
    dnorm23 = []
    grads = []
    for j in range(CHUNKS):
        z, h, c = state[j]
        _, c_rel, r, g = mids[j]
        terms, dm_rel, du = backs[j]
        clock.add(terms[2])
        dh, dz, dn = mid_call(terms, clock.at(h), z, cotangent[cuts[j]], weight[cuts[j]], norms)
        clock.set(dz)
        r, du = clock.at((r, du))
        grads.append((over_tokens(du, c_rel), over_tokens(r, dm_rel)))
        clock.set(dz, *grads[j])
        dhs.append(dh)
        dnorm23.append(dn)
        dzs.append(dz)
        sides.append((to_core(dz), to_chip(dz)))
    grad_up, grad_down = (sum(g[i] for g in grads).astype(BF) for i in range(2))
    buckets_m = bucket_call([clock.at(grad_up), grad_down], own_m.starts, pieces_m, own_m.sizes)
    clock.set(buckets_m[0])

    prev, dqs = [(), ()], []
    sums_m = ScatterSteps(own_m, buckets_m)
    for j in range(CHUNKS):
        _, ot, lse = fwd[j]
        args = gathered(dzs[j], *sides[j])
        dqs.append([])
        for i in range(2):
            args[0] = clock.at(args[0])
            dq, *prev[i] = attn_bwd_call(j, CHUNKS, i, perm, args, w_attn, qt, k4, kt, v4, ot, lse, cos_t, sin_t, tuple(prev[i]))
            clock.set(dq)
            dqs[j].append(dq)
            if i == 0:
                sums_m.step(clock)
                sums_m.pin(clock)
    dk, dv, grad_out = zip(*prev)
    grad_qkv, *dns = qkv_grad_call(perm, [[clock.at(dqs[0][0]), dqs[0][1]], *dqs[1:]], dk, dv, dnorm23, dnorm4, n_rel, w_attn, norms)
    clock.set(grad_qkv)
    sums_m.step(clock)
    sums_m.pin(clock)
    dns = clock.at(dns)
    near, across = to_core(dns[1]), to_core(dns[3])
    da = qkv_in_call(0, CHUNKS, perm, [clock.at(dqs[0][0]), dqs[0][1]], dk, dv, w_attn)
    clock.set(da[0], across)
    norm_side = to_chip(clock.at(dns[2]) + across)
    da_terms = [summed(da, norm_side)]
    norm_sum = dns[0] + near + norm_side
    buckets_a = bucket_call([clock.at(grad_qkv), *grad_out, norm_sum], own_a.starts, pieces_a, own_a.sizes)
    clock.set(buckets_a[0])
    terms_m = sums_m.terms()
    for v in terms_m[0][1:]:
        clock.add(v)
    ring_a = ScatterSteps(own_a, [clock.at(v) for v in buckets_a])
    for j in range(1, CHUNKS):
        da = qkv_in_call(j, CHUNKS, perm, [clock.at(dqs[j][0]), dqs[j][1]], dk, dv, w_attn)
        clock.set(da[0])
        ring_a.step(clock)
        ring_a.pin(clock)
        da_terms.append(summed(da))
    new_m = adam_call(own_m.parts, terms_m, clock.at(rate_m), [by_slot(v) for v in (master_mlp, moment_mlp, square_mlp)])
    clock.set(new_m[0])
    ring_a.step(clock)
    ring_a.pin(clock)
    dxs = []
    for j in range(CHUNKS):
        dxs.append(last_call(da_terms[j], clock.at(tokens[cuts[j]]), dhs[j], norms))
        clock.set(dxs[j])
        ring_a.step(clock)
        ring_a.pin(clock)
    new_a = adam_call(own_a.parts, ring_a.terms(), rate_a, [by_slot(v) for v in (master_attn, moment_attn, square_attn)])
    return (jnp.concatenate(outs, axis=0), jnp.concatenate(dxs, axis=0),
            *(v.reshape(master_attn.shape) for v in new_a), *(v.reshape(master_mlp.shape) for v in new_m))


def solution(mesh):
    tok = P(("dp", "tensor"), None)
    par = P("tensor", "dp", None)
    return jax.shard_map(
        on_device, mesh=mesh,
        in_specs=(tok, tok, P(("dp", "tensor")), P(), P(), par, par, par, par, par, par),
        out_specs=(tok, tok, par, par, par, par, par, par),
        check_vma=False,
    )
```

```python
import functools
import jax
import jax.numpy as jnp
from jax import lax
from jax.sharding import PartitionSpec as P
from jax.experimental import pallas as pl
from jax.experimental.pallas import tpu as pltpu

BF = jnp.bfloat16
F32 = jnp.float32
EPS = 1e-5
HEAD = 64
LANES = 128
QB = 256
CHUNKS = 2
ADAM_STEP = 5


def dot_nn(a, b):
    return lax.dot_general(a, b, (((1,), (0,)), ((), ())), preferred_element_type=F32)


def dot_nt(a, b):
    return lax.dot_general(a, b, (((1,), (1,)), ((), ())), preferred_element_type=F32)


def params(mib):
    return pltpu.CompilerParams(vmem_limit_bytes=mib * 1024 * 1024)


def cost(us):
    return pl.CostEstimate(flops=int(us * 3e6), bytes_accessed=int(us * 1e4), transcendentals=0)


def whole(shape, at=None):
    at = at or (0,) * len(shape)
    return pl.BlockSpec(shape, lambda *_: at)


def shape(dims, dtype):
    return jax.ShapeDtypeStruct(dims, dtype)


def choose(index, refs, into):
    for i in range(4):
        @pl.when(index == i)
        def _():
            if i == 3 and len(refs) == 5:
                half = refs[3].shape[0]
                into[0:half, :] = refs[3][...]
                into[half:, :] = refs[4][...]
            else:
                into[...] = refs[i][...]


def spread(index, refs, value):
    for i in range(4):
        @pl.when(index == i)
        def _():
            if i == 3:
                half = refs[3].shape[0]
                refs[3][...] = value[0:half]
                refs[4][...] = value[half:]
            else:
                refs[i][...] = value


def block_dims(rows, width):
    return [(rows, width)] * 3 + [(rows // 2, width)] * 2


def centre(v):
    mean = jnp.mean(v, axis=-1, keepdims=True)
    vc = v - mean
    s = lax.rsqrt(jnp.mean(vc * vc, axis=-1, keepdims=True) + EPS)
    return vc * s, s


def norm_back(n, s, y, gain):
    dn = y * gain
    return s * (dn - jnp.mean(dn, axis=-1, keepdims=True) - n * jnp.mean(dn * n, axis=-1, keepdims=True))


def total(parts):
    return sum(p[...].astype(F32) for p in parts)


def rows_call(kernel, outs, *args):
    return pl.pallas_call(kernel, out_shape=outs, compiler_params=params(10), cost_estimate=cost(2.5))(*args)


def residual_kernel(p0, p1, p2, x_ref, norms, z_ref, h_ref, c_ref):
    z = total([p0, p1, p2])
    z_ref[...] = z
    n, _ = centre(z)
    h = x_ref[...].astype(F32) + n * norms[2:3, :] + norms[3:4, :]
    h_ref[...] = h
    n, _ = centre(h)
    c_ref[...] = (n * norms[4:5, :] + norms[5:6, :]).astype(BF)


def residual_call(parts, x, norms):
    return rows_call(residual_kernel, [shape(x.shape, F32), shape(x.shape, F32), shape(x.shape, BF)], *parts, x, norms)


def out_kernel(p0, p1, p2, h_ref, ct_ref, wt_ref, norms, lo_ref, dm_ref, dn_ref):
    n, s = centre(total([p0, p1, p2]))
    lo_ref[...] = (h_ref[...] + n * norms[6:7, :] + norms[7:8, :]).astype(BF)
    e = ct_ref[...].astype(F32) * wt_ref[:, 0:1]
    dm_ref[...] = norm_back(n, s, e, norms[6:7, :]).astype(BF)
    dn_ref[0:1, :] = jnp.sum(e * n, axis=0, keepdims=True)
    dn_ref[1:2, :] = jnp.sum(e, axis=0, keepdims=True)


def out_call(parts, h, ct, wt, norms):
    return rows_call(out_kernel, [shape(h.shape, BF), shape(h.shape, BF), shape((2, h.shape[1]), F32)], *parts, h, ct, wt, norms)


def mid_kernel(p0, p1, p2, h_ref, z_ref, ct_ref, wt_ref, norms, dh_ref, dz_ref, dn_ref):
    dc = total([p0, p1, p2])
    n3, s3 = centre(h_ref[...])
    dh = ct_ref[...].astype(F32) * wt_ref[:, 0:1] + norm_back(n3, s3, dc, norms[4:5, :])
    dh_ref[...] = dh
    n2, s2 = centre(z_ref[...])
    dz_ref[...] = norm_back(n2, s2, dh, norms[2:3, :]).astype(BF)
    dn_ref[0:1, :] = jnp.sum(dh * n2, axis=0, keepdims=True)
    dn_ref[1:2, :] = jnp.sum(dh, axis=0, keepdims=True)
    dn_ref[2:3, :] = jnp.sum(dc * n3, axis=0, keepdims=True)
    dn_ref[3:4, :] = jnp.sum(dc, axis=0, keepdims=True)


def mid_call(parts, h, z, ct, wt, norms):
    return rows_call(mid_kernel, [shape(h.shape, F32), shape(h.shape, BF), shape((4, h.shape[1]), F32)],
                     *parts, h, z, ct, wt, norms)


def last_kernel(p0, p1, p2, x_ref, dh_ref, norms, dx_ref):
    n1, s1 = centre(x_ref[...].astype(F32))
    dx_ref[...] = dh_ref[...] + norm_back(n1, s1, total([p0, p1, p2]), norms[0:1, :])


def last_call(parts, x, dh, norms):
    return rows_call(last_kernel, shape(x.shape, F32), *parts, x, dh, norms)


def sum_kernel(keep, *refs):
    fars, out = refs[:-1], refs[-1]
    step = fars[0].shape[0]
    for i, f in enumerate(fars):
        at = slice(i * step, (i + 1) * step)
        out[at, :] = (keep[at, :].astype(F32) + f[...].astype(F32)).astype(BF)


def sum_call(keep, fars):
    return pl.pallas_call(
        sum_kernel, out_shape=shape(keep.shape, BF), compiler_params=params(4), cost_estimate=cost(0.1),
    )(keep, *fars)


def qkv_kernel(perm, *refs):
    xs, gs, (w_ref, cos_ref, sin_ref, norms, n_ref, qt_ref, kt_ref, vt_ref, k4_ref, v4_ref, cur) = refs[:4], refs[4:8], refs[8:]

    @pl.when(pl.program_id(0) == 0)
    def _():
        for t in range(4):
            for i, g in enumerate(gs):
                @pl.when(perm[t] == i)
                def _():
                    norms[2 * t:2 * t + 2, :] = g[0:2, :]

    choose(pl.program_id(0), xs, cur)
    n, _ = centre(cur[...].astype(F32))
    n_ref[0] = n.astype(BF)
    a = (n * norms[0:1, :] + norms[1:2, :]).astype(BF)
    cos, sin = cos_ref[...], sin_ref[...]
    dims = qt_ref.shape[0]
    half = HEAD // 2
    for part in range(3):
        proj = dot_nt(w_ref[part * dims:(part + 1) * dims, :], a)
        for h in range(dims // HEAD):
            lo = slice(h * HEAD, h * HEAD + half)
            hi = slice(h * HEAD + half, (h + 1) * HEAD)
            hd = slice(h * HEAD, (h + 1) * HEAD)
            if part < 2:
                first, second = proj[lo], proj[hi]
                r1 = first * cos - second * sin
                r2 = second * cos + first * sin
                if part == 0:
                    qt_ref[lo, :] = (r1 * 0.125).astype(BF)
                    qt_ref[hi, :] = (r2 * 0.125).astype(BF)
                else:
                    full = jnp.concatenate([r1, r2], axis=0)
                    kt_ref[hd, :] = full.astype(BF)
                    k4_ref[h] = full.T.astype(BF)
            else:
                vt_ref[hd, :] = proj[hd].astype(BF)
                v4_ref[h] = proj[hd].T.astype(BF)


def qkv_call(perm, xs, gains, w, cos_t, sin_t):
    rows, width = xs[0].shape
    n = len(xs)
    dims = w.shape[0] // 4
    heads = dims // HEAD
    length = n * rows
    tok = pl.BlockSpec((dims, rows), lambda k, p: (0, p[k]))
    hd = pl.BlockSpec((heads, rows, HEAD), lambda k, p: (0, p[k], 0))
    tab = pl.BlockSpec((HEAD // 2, rows), lambda k, p: (0, p[k]))
    return pl.pallas_call(
        qkv_kernel,
        grid_spec=pltpu.PrefetchScalarGridSpec(
            num_scalar_prefetch=1, grid=(n,),
            in_specs=[whole((rows, width))] * n + [whole(g.shape) for g in gains] + [whole((3 * dims, width)), tab, tab],
            out_specs=[whole((8, width)), pl.BlockSpec((1, rows, width), lambda k, p: (k, 0, 0)), tok, tok, tok, hd, hd],
            scratch_shapes=[pltpu.VMEM((rows, width), BF)],
        ),
        out_shape=[shape((8, width), F32), shape((n, rows, width), BF)] + [shape((dims, length), BF)] * 3 + [shape((heads, length, HEAD), BF)] * 2,
        compiler_params=params(20), cost_estimate=cost(10),
    )(perm, *xs, *gains, w, cos_t, sin_t)


def visible(chunk, diag):
    return (lax.broadcasted_iota(jnp.int32, (diag, QB), 0)
            <= lax.broadcasted_iota(jnp.int32, (diag, QB), 1) + chunk * QB)


def key_spans(n, wide, diag):
    return ([pl.ds(0, n * wide)] if n else []) + [pl.ds(n * wide, diag)]


def pipelined(heads, first, second, third):
    ahead, behind = first(0), None
    for h in range(heads):
        now = ahead
        if h + 1 < heads:
            ahead = first(h + 1)
        done = second(h, now)
        if behind is not None:
            third(h - 1, behind)
        behind = done
    third(heads - 1, behind)


def attn_fwd_kernel(chunk, chunks, count, perm, qt_ref, k4_ref, vt_ref, wo_ref, *rest):
    zs, (ot_ref, lse_ref, acc) = rest[:5], rest[5:]
    heads = k4_ref.shape[0]
    diag = (chunk + 1) * QB
    seen = visible(chunk, diag)
    hd = [slice(h * HEAD, (h + 1) * HEAD) for h in range(heads)]
    cols = [slice(t * QB, (t + 1) * QB) for t in range(count)]
    mine = [slice((chunks * t + chunk) * QB, (chunks * t + chunk + 1) * QB) for t in range(count)]

    def unit(u):
        t, h = u // heads, u % heads
        return t, h, key_spans(t, chunks * QB, diag)

    def scores(u):
        t, h, spans = unit(u)
        return [dot_nn(k4_ref[h, ks, :], qt_ref[hd[h], mine[t]]) for ks in spans]

    def soft(u, s):
        t, h, _ = unit(u)
        s = s[:-1] + [jnp.where(seen, s[-1], -1e30)]
        m = functools.reduce(jnp.maximum, [jnp.max(v, axis=0, keepdims=True) for v in s])
        p = [jnp.exp(v - m) for v in s]
        l = sum(jnp.sum(v, axis=0, keepdims=True) for v in p)
        lse_ref[h:h + 1, cols[t]] = m + jnp.log(l)
        return [v.astype(BF) for v in p], l

    def attend(u, done):
        t, h, spans = unit(u)
        acc[hd[h], cols[t]] = sum(dot_nn(vt_ref[hd[h], ks], v) for ks, v in zip(spans, done[0])) / done[1]

    pipelined(heads * count, scores, soft, attend)
    ot_ref[...] = acc[...].astype(BF)
    for t in range(count):
        o = acc[:, cols[t]].T.astype(BF)
        spread(perm[t], zs, dot_nn(o, wo_ref[...]).astype(BF))


def attn_fwd_call(chunk, chunks, perm, qt, k4, vt, w):
    dims, length = qt.shape
    width = w.shape[1]
    heads = dims // HEAD
    n = length // (chunks * QB)
    outs = block_dims(QB, width) + [(dims, n * QB)]
    return pl.pallas_call(
        functools.partial(attn_fwd_kernel, chunk, chunks, n),
        grid_spec=pltpu.PrefetchScalarGridSpec(
            num_scalar_prefetch=1, grid=(1,),
            in_specs=[whole(qt.shape), whole(k4.shape), whole(vt.shape), whole((dims, width), (3, 0))],
            out_specs=[whole(d) for d in outs] + [whole((heads, n * QB))],
            scratch_shapes=[pltpu.VMEM((dims, n * QB), F32)],
        ),
        out_shape=[shape(d, BF) for d in outs] + [shape((heads, n * QB), F32)],
        compiler_params=params(22), cost_estimate=cost(9.5 + 1.5 * chunk),
    )(perm, qt, k4, vt, w)


def attn_bwd_kernel(chunk, chunks, count, pair, perm, *refs):
    dzs, refs = refs[:5], refs[5:]
    wo_ref, qt_ref, k4_ref, kt_ref, v4_ref, ot_ref, lse_ref, cos_ref, sin_ref = refs[:9]
    refs = refs[9:]
    if chunk == 0:
        dq_ref, dk_ref, dv_ref, gwo_ref, acc, dot_ref, dl_ref, dz_ref = refs
    else:
        dk0, dv0, gwo0, dq_ref, dkl_ref, dvl_ref, gwo_ref, acc, dot_ref, dl_ref, dz_ref, dk_ref, dv_ref = refs
    heads = k4_ref.shape[0]
    half = HEAD // 2
    wide = chunks * QB
    diag = (chunk + 1) * QB
    seen = visible(chunk, diag)
    hd = [slice(h * HEAD, (h + 1) * HEAD) for h in range(heads)]
    cols = [slice(t * QB, (t + 1) * QB) for t in range(count)]
    mine = [slice((chunks * t + chunk) * QB, (chunks * t + chunk + 1) * QB) for t in range(count)]
    if chunk == 0:
        dk_ref[...] = jnp.zeros_like(dk_ref)
        dv_ref[...] = jnp.zeros_like(dv_ref)
    else:
        dk_ref[...] = dk0[...]
        dv_ref[...] = dv0[...]
    for t in range(count):
        choose(perm[t], dzs, dz_ref.at[t])
        dot_ref[:, cols[t]] = dot_nt(wo_ref[...], dz_ref[t]).astype(BF)
    prod = dot_ref[...].astype(F32) * ot_ref[...].astype(F32)
    for h in range(heads):
        dl_ref[h:h + 1, :] = jnp.sum(prod[hd[h]], axis=0, keepdims=True)

    def unit(u):
        t, h = u // heads, u % heads
        return t, h, key_spans(t, wide, diag)

    def scores(u):
        t, h, spans = unit(u)
        return [(dot_nn(k4_ref[h, ks, :], qt_ref[hd[h], mine[t]]), dot_nn(v4_ref[h, ks, :], dot_ref[hd[h], cols[t]])) for ks in spans]

    def soft(u, pairs):
        t, h, spans = unit(u)
        lse, delta = lse_ref[heads * pair + h:heads * pair + h + 1, cols[t]], dl_ref[h:h + 1, cols[t]]
        out = []
        for i, (s, dp) in enumerate(pairs):
            p = jnp.exp(s - lse)
            if i == len(pairs) - 1:
                p = jnp.where(seen, p, 0.0)
            out.append((p.astype(BF), (p * (dp - delta)).astype(BF)))
        return out

    def back(u, pairs):
        t, h, spans = unit(u)
        q, do = qt_ref[hd[h], mine[t]], dot_ref[hd[h], cols[t]]
        dq = 0.0
        for ks, (p, ds) in zip(spans, pairs):
            dv_ref[hd[h], ks] += dot_nt(do, p)
            dk_ref[hd[h], ks] += dot_nt(q, ds)
            dq = dq + dot_nn(kt_ref[hd[h], ks], ds)
        acc[hd[h], cols[t]] = dq

    pipelined(heads * count, scores, soft, back)
    g = dot_nn(ot_ref[...], dz_ref[...].reshape(count * QB, dz_ref.shape[2]))
    gwo_ref[...] = g if chunk == 0 else gwo0[...] + g

    def unturn(src, at, to, scale, out):
        cos, sin = cos_ref[:, at], sin_ref[:, at]
        for h in range(heads):
            lo = slice(h * HEAD, h * HEAD + half)
            hi = slice(h * HEAD + half, (h + 1) * HEAD)
            g1, g2 = src[lo, to] * scale, src[hi, to] * scale
            out[lo, to] = (g1 * cos + g2 * sin).astype(BF)
            out[hi, to] = (g2 * cos - g1 * sin).astype(BF)

    for t in range(count):
        unturn(acc, mine[t], cols[t], 0.125, dq_ref)
    if chunk == chunks - 1:
        unturn(dk_ref, slice(None), slice(None), 1.0, dkl_ref)
        dvl_ref[...] = dv_ref[...].astype(BF)


def attn_bwd_call(chunk, chunks, pair, perm, dzs, w, qt, k4, kt, v4, ot, lse, cos_t, sin_t, prev=()):
    dims, length = qt.shape[0] // 2, qt.shape[1]
    width = w.shape[1]
    heads = dims // HEAD
    n = length // (chunks * QB)
    full, tb = whole((dims, length), (pair, 0)), whole((dims, n * QB), (pair, 0))
    kv4 = whole((heads, length, HEAD), (pair, 0, 0))
    out_full, out_tb, out_w = whole((dims, length)), whole((dims, n * QB)), whole((dims, width))
    in_specs = [whole(d) for d in block_dims(QB, width)] + [
        whole((dims, width), (6 + pair, 0)), full, kv4, full, kv4, tb, whole(lse.shape), whole(cos_t.shape), whole(sin_t.shape)]
    scratch = [pltpu.VMEM((dims, n * QB), F32), pltpu.VMEM((dims, n * QB), BF), pltpu.VMEM((8, n * QB), F32), pltpu.VMEM((n, QB, width), BF)]
    kv = F32
    if chunk:
        in_specs += [out_full, out_full, out_w]
        scratch += [pltpu.VMEM((dims, length), F32)] * 2
        kv = BF
    return pl.pallas_call(
        functools.partial(attn_bwd_kernel, chunk, chunks, n, pair),
        grid_spec=pltpu.PrefetchScalarGridSpec(
            num_scalar_prefetch=1, grid=(1,), in_specs=in_specs,
            out_specs=[out_tb, out_full, out_full, out_w], scratch_shapes=scratch,
        ),
        out_shape=[shape((dims, n * QB), BF), shape((dims, length), kv), shape((dims, length), kv), shape((dims, width), F32)],
        compiler_params=params(22), cost_estimate=cost(10 + 2 * chunk),
    )(perm, *dzs, w, qt, k4, kt, v4, ot, lse, cos_t, sin_t, *prev)


def stack_rows(refs, into, cols=slice(None)):
    at = 0
    for r in refs:
        into[at:at + r.shape[0], cols] = r[...]
        at += r.shape[0]


def qkv_in_kernel(perm, *refs):
    parts, w_ref, das, dx = refs[:6], refs[6], refs[7:12], refs[12]
    stack_rows(parts, dx)
    grad = dx[...].astype(F32).T.astype(BF)
    spread(perm[pl.program_id(0)], das, dot_nn(grad, w_ref[...]).astype(BF))


def qkv_in_call(chunk, chunks, perm, dq, dk, dv, w):
    dims, length = dk[0].shape
    width = w.shape[1]
    n = length // (chunks * QB)
    at = pl.BlockSpec((dims, QB), lambda t, p: (0, chunks * t + chunk))
    return pl.pallas_call(
        qkv_in_kernel,
        grid_spec=pltpu.PrefetchScalarGridSpec(
            num_scalar_prefetch=1, grid=(n,),
            in_specs=[pl.BlockSpec((dims, QB), lambda t, p: (0, t))] * 2 + [at] * 4 + [whole((6 * dims, width))],
            out_specs=[whole(d) for d in block_dims(QB, width)],
            scratch_shapes=[pltpu.VMEM((6 * dims, QB), BF)],
        ),
        out_shape=[shape(d, BF) for d in block_dims(QB, width)],
        compiler_params=params(8), cost_estimate=cost(5),
    )(perm, *dq, *dk, *dv, w)


def qkv_grad_kernel(chunks, count, perm, *refs):
    dqs, kvs, refs = refs[:2 * chunks], refs[2 * chunks:2 * chunks + 4], refs[2 * chunks + 4:]
    d23, d4, (n_ref, w_ref, norms, gw_ref), dns, (dx, rows, sums_ref) = refs[:chunks], refs[chunks:2 * chunks], refs[2 * chunks:2 * chunks + 4], refs[2 * chunks + 4:2 * chunks + 8], refs[2 * chunks + 8:]
    dims = kvs[0].shape[0]
    wide = chunks * QB

    @pl.when(pl.program_id(0) == 0)
    def _():
        for i in range(chunks):
            for p in range(2):
                for t in range(count):
                    to = slice(t * wide + i * QB, t * wide + (i + 1) * QB)
                    dx[p * dims:(p + 1) * dims, to] = dqs[2 * i + p][:, t * QB:(t + 1) * QB]
        stack_rows(kvs, dx.at[2 * dims:])
        sums_ref[...] = jnp.sum(dx[...].astype(F32), axis=1, keepdims=True)

    grad = sum(dot_nn(dx[:, t * wide:(t + 1) * wide], n_ref[perm[t]]) for t in range(count))
    sums = sums_ref[...]
    w = w_ref[...].astype(F32)
    gw_ref[...] = (grad * norms[0:1, :] + sums * norms[1:2, :]).astype(BF)
    rows[0:1, :] = jnp.sum(grad * w, axis=0, keepdims=True)
    rows[1:2, :] = jnp.sum(sums * w, axis=0, keepdims=True)
    rows[2:6, :] = total(d23)
    rows[6:8, :] = total(d4)
    for i, out in enumerate(dns):
        for t in range(4):
            @pl.when(perm[i] == t)
            def _():
                out[...] = rows[2 * t:2 * t + 2, :]


def qkv_grad_call(perm, dqs, dk, dv, d23, d4, n_rel, w, norms):
    chunks = len(dqs)
    n, rows, width = n_rel.shape
    dims = dk[0].shape[0]
    cols = 256
    args = [v for dq in dqs for v in dq] + [*dk, *dv]
    return pl.pallas_call(
        functools.partial(qkv_grad_kernel, chunks, n),
        grid_spec=pltpu.PrefetchScalarGridSpec(
            num_scalar_prefetch=1, grid=(width // cols,),
            in_specs=[whole(v.shape) for v in args] + [pl.BlockSpec((v.shape[0], cols), lambda i, p: (0, i)) for v in (*d23, *d4)] + [
                pl.BlockSpec((n, rows, cols), lambda i, p: (0, 0, i)), pl.BlockSpec((6 * dims, cols), lambda i, p: (0, i)),
                pl.BlockSpec((8, cols), lambda i, p: (0, i))],
            out_specs=[pl.BlockSpec((6 * dims, cols), lambda i, p: (0, i))] + [pl.BlockSpec((2, cols), lambda i, p: (0, i))] * 4,
            scratch_shapes=[pltpu.VMEM((6 * dims, n * rows), BF), pltpu.VMEM((8, cols), F32), pltpu.VMEM((6 * dims, 1), F32)],
        ),
        out_shape=[shape((6 * dims, width), BF)] + [shape((2, width), F32)] * 4,
        compiler_params=params(16), cost_estimate=cost(7),
    )(perm, *args, *d23, *d4, n_rel, w, norms)


def mlp_fwd_kernel(*refs):
    cs, (w1_ref, w2_ref), ms, (c_ref, r_ref, g_ref) = refs[:5], refs[5:7], refs[7:12], refs[12:]
    k = pl.program_id(0)
    choose(k, cs, c_ref.at[0])
    u = dot_nt(c_ref[0], w1_ref[...])
    cdf = 0.5 * (1.0 + lax.erf(u * 0.7071067811865476))
    r = (u * cdf).astype(BF)
    r_ref[0] = r
    g_ref[0] = (cdf + u * (0.3989422804014327 * jnp.exp(-0.5 * u * u))).astype(BF)
    spread(k, ms, dot_nn(r, w2_ref[...]).astype(BF))


def mlp_fwd_call(cs, w):
    rows, width = cs[0].shape
    n, hid = 4, w.shape[0] // 2
    dims = block_dims(rows, width)
    blk = pl.BlockSpec((1, rows, width), lambda k: (k, 0, 0))
    hb = pl.BlockSpec((1, rows, hid), lambda k: (k, 0, 0))
    return pl.pallas_call(
        mlp_fwd_kernel, grid=(n,),
        in_specs=[whole(c.shape) for c in cs] + [whole((hid, width), (0, 0)), whole((hid, width), (1, 0))],
        out_specs=[whole(d) for d in dims] + [blk, hb, hb],
        out_shape=[shape(d, BF) for d in dims] + [shape((n, rows, width), BF)] + [shape((n, rows, hid), BF)] * 2,
        compiler_params=params(16), cost_estimate=cost(9),
    )(*cs, w, w)


def mlp_bwd_kernel(*refs):
    dms, (g_ref, w1_ref, w2_ref), dcs, (dm_ref, du_ref) = refs[:5], refs[5:8], refs[8:13], refs[13:]
    k = pl.program_id(0)
    choose(k, dms, dm_ref.at[0])
    dr = dot_nt(dm_ref[0], w2_ref[...])
    du = (dr * g_ref[0].astype(F32)).astype(BF)
    du_ref[0] = du
    spread(k, dcs, dot_nn(du, w1_ref[...]).astype(BF))


def mlp_bwd_call(dms, g, w):
    rows, width = dms[0].shape
    n, hid = 4, w.shape[0] // 2
    dims = block_dims(rows, width)
    blk = pl.BlockSpec((1, rows, width), lambda k: (k, 0, 0))
    hb = pl.BlockSpec((1, rows, hid), lambda k: (k, 0, 0))
    return pl.pallas_call(
        mlp_bwd_kernel, grid=(n,),
        in_specs=[whole(d.shape) for d in dms] + [hb, whole((hid, width), (0, 0)), whole((hid, width), (1, 0))],
        out_specs=[whole(d) for d in dims] + [blk, hb],
        out_shape=[shape(d, BF) for d in dims] + [shape((n, rows, width), BF), shape((n, rows, hid), BF)],
        compiler_params=params(16), cost_estimate=cost(8),
    )(*dms, g, w, w)


def wgrad_kernel(*refs):
    n = len(refs) // 2
    out = refs[-1]
    acc = 0.0
    for x, y in zip(refs[:n], refs[n:2 * n]):
        tok = x.shape[0] * x.shape[1]
        acc = acc + lax.dot_general(x[...].reshape(tok, x.shape[2]), y[...].reshape(tok, y.shape[2]), (((0,), (0,)), ((), ())), preferred_element_type=F32)
    out[...] = acc.astype(BF)


def wgrad_call(xs, ys, tile=512):
    blocks, rows, hid = xs[0].shape
    width = ys[0].shape[2]
    return pl.pallas_call(
        wgrad_kernel, grid=(hid // tile,),
        in_specs=[pl.BlockSpec((blocks, rows, tile), lambda i: (0, 0, i))] * len(xs) + [whole(y.shape) for y in ys],
        out_specs=pl.BlockSpec((tile, width), lambda i: (i, 0)),
        out_shape=shape((hid, width), BF),
        compiler_params=params(24), cost_estimate=cost(6),
    )(*xs, *ys)


UNROLL = (58, 57, 56, 48, 46, 43, 42, 40, 22, 20, 18, 16, 8, 6, 4, 3, 2, 1)


def place_kernel(sizes, count, starts, pieces, *refs):
    srcs, out_ref, rest_ref, mid = refs[:-3], refs[-3], refs[-2], refs[-1]
    sub = srcs[0].shape[1]
    for k, src in enumerate(srcs):
        base = starts[k]
        step = next(u for u in UNROLL if sizes[k] % u == 0)

        def body(i, c, src=src, base=base, step=step):
            tos = [pieces[base + i * step + u] for u in range(step)]
            vals = [src[i * step + u].astype(F32) for u in range(step)]
            for u in range(step):
                mid[pl.ds(pl.multiple_of(tos[u] * sub, sub), sub), :] = vals[u]
            return c

        lax.fori_loop(0, sizes[k] // step, body, 0)
    rows = 64

    def spread(i, c):
        r = pl.multiple_of(i * rows, rows)
        for j in range(sub):
            part = mid[pl.ds(r * sub + j, rows, stride=sub), :]
            out_ref[pl.ds(r, rows), j * LANES:(j + 1) * LANES] = part.astype(BF)
        return c

    lax.fori_loop(0, count // rows, spread, 0)
    for j in range(sub):
        rest_ref[:, j * LANES:(j + 1) * LANES] = mid[pl.ds(count * sub + j, 8, stride=sub), :]


def place_call(blocks, starts, pieces, count):
    sub = blocks[0].shape[1]
    sizes = [b.shape[0] for b in blocks]
    return pl.pallas_call(
        functools.partial(place_kernel, sizes, count),
        grid_spec=pltpu.PrefetchScalarGridSpec(
            num_scalar_prefetch=2, grid=(1,),
            in_specs=[whole(b.shape) for b in blocks],
            out_specs=[whole((count, sub * LANES)), whole((8, sub * LANES))],
            scratch_shapes=[pltpu.VMEM(((count + 8) * sub, LANES), F32)],
        ),
        out_shape=[shape((count, sub * LANES), BF), shape((8, sub * LANES), F32)],
        compiler_params=params(10 + count // 146), cost_estimate=cost(count / 450),
    )(starts, pieces, *blocks)


def bucket_kernel(sizes, starts, pieces, *refs):
    n = len(sizes)
    grads, outs, mid = refs[:-n - 1], refs[-n - 1:-1], refs[-1]
    width = grads[0].shape[1]
    sub = width // LANES
    rows = 64
    at = 0
    for g in grads:
        if g.shape[0] % rows:
            for j in range(sub):
                mid[pl.ds(at * sub + j, g.shape[0], stride=sub), :] = g[:, j * LANES:(j + 1) * LANES].astype(F32)
            at += g.shape[0]
            continue

        def split(i, c, g=g, at=at):
            r = pl.multiple_of(i * rows, rows)
            for j in range(sub):
                mid[pl.ds((at + r) * sub + j, rows, stride=sub), :] = g[pl.ds(r, rows), j * LANES:(j + 1) * LANES].astype(F32)
            return c

        lax.fori_loop(0, g.shape[0] // rows, split, 0)
        at += g.shape[0]
    mid[at * sub:(at + 8) * sub, :] = jnp.zeros((8 * sub, LANES), F32)
    for k, out in enumerate(outs):
        base = starts[k]
        step = next(u for u in UNROLL if sizes[k] % u == 0)

        def body(i, c, out=out, base=base, step=step):
            srcs = [pieces[base + i * step + u] for u in range(step)]
            vals = [mid[pl.ds(pl.multiple_of(v * sub, sub), sub), :].astype(BF) for v in srcs]
            for u in range(step):
                out[i * step + u] = vals[u]
            return c

        lax.fori_loop(0, sizes[k] // step, body, 0)


def bucket_call(grads, starts, pieces, sizes):
    width = grads[0].shape[1]
    sub = width // LANES
    count = sum(g.shape[0] for g in grads)
    shapes = [(s, sub, LANES) for s in sizes]
    return pl.pallas_call(
        functools.partial(bucket_kernel, sizes),
        grid_spec=pltpu.PrefetchScalarGridSpec(
            num_scalar_prefetch=2, grid=(1,),
            in_specs=[whole(g.shape) for g in grads],
            out_specs=[whole(s) for s in shapes],
            scratch_shapes=[pltpu.VMEM(((count + 8) * sub, LANES), F32)],
        ),
        out_shape=[jax.ShapeDtypeStruct(s, BF) for s in shapes],
        compiler_params=params(8 + count // 146), cost_estimate=cost(count / 350),
    )(starts, pieces, *grads)


def adam_kernel(bounds, *refs):
    parts, (rate, m_ref, f_ref, s_ref, om, of, os) = refs[:-7], refs[-7:]
    each = len(parts) // len(bounds)
    for i, (lo, hi) in enumerate(bounds):
        at = slice(lo, hi)
        g = total(parts[i * each:(i + 1) * each])
        first = 0.5 * f_ref[at] + 0.5 * g
        second = 0.5 * s_ref[at] + 0.5 * g * g
        of[at] = first
        os[at] = second
        w = m_ref[at]
        first = first / (1.0 - 0.5**ADAM_STEP)
        second = second / (1.0 - 0.5**ADAM_STEP)
        om[at] = w - rate[at] * (first / (jnp.sqrt(second) + 1e-8) + 0.1 * w)


def adam_call(bounds, parts, rate, states):
    cap, sub, lanes = states[0].shape
    step = next(d for d in range(64, 0, -1) if cap % d == 0) if len(bounds) == 1 else cap
    if len(bounds) == 1:
        bounds = [(0, step)]
    blk = pl.BlockSpec((step, sub, lanes), lambda i: (i, 0, 0))
    terms = [v for part in parts for v in part]
    return pl.pallas_call(
        functools.partial(adam_kernel, bounds), grid=(cap // step,),
        in_specs=[blk if len(bounds) == 1 else whole(v.shape) for v in terms] + [
            pl.BlockSpec((step, 1, lanes), lambda i: (i, 0, 0))] + [blk] * 3,
        out_specs=[blk] * 3,
        out_shape=[shape(v.shape, F32) for v in states],
        compiler_params=params(12), cost_estimate=cost(cap / 80),
    )(*terms, rate, *states)


def low_kernel(bounds, x_ref, *outs):
    for (lo, hi), out in zip(bounds, outs):
        out[...] = x_ref[lo:hi].astype(BF)


def low_call(bounds, v):
    return list(pl.pallas_call(
        functools.partial(low_kernel, bounds), out_shape=[shape((hi - lo, *v.shape[1:]), BF) for lo, hi in bounds],
        compiler_params=params(6), cost_estimate=cost(1),
    )(v))


TOP = [(0, 1), (1, 0), (2, 3), (3, 2)]
SIDE = [(0, 2), (1, 3), (2, 0), (3, 1)]
RINGS = {8: [0, 2, 4, 6, 7, 5, 3, 1]}


def to_core(v):
    return lax.ppermute(v, "tensor", TOP)


def to_chip(v):
    return lax.ppermute(v, "tensor", SIDE)


def after(v, *first):
    if not first:
        return v
    return lax.optimization_barrier((v, *first))[0]


class Clock:
    def __init__(self):
        self.last = []

    def set(self, *values):
        self.last = list(values)

    def add(self, value):
        self.last.append(value)

    def at(self, value):
        return lax.optimization_barrier((value, *self.last))[0] if self.last else value


def gather_rel(own):
    side = to_chip(own)
    return [own, to_core(own), side, to_core(side)]


class Owners:
    def __init__(self, cap, halves):
        self.cap, self.count = cap, lax.axis_size("dp")
        self.ring = RINGS.get(self.count)
        self.cut = cap // 2 // 8 * 8
        if self.ring:
            n, ring = self.count, self.ring
            self.right = [(ring[i], ring[(i + 1) % n]) for i in range(n)]
            self.left = [(b, a) for a, b in self.right]
            self.far = n // 2
            self.parts = [(0, self.cut), (self.cut, cap)] if halves else [(0, cap)]
            hops = [0] + [h for s in range(1, self.far) for h in (-s, s)]
            ends = [(0, self.cut), (self.cut, cap)]
            self.sizes = [hi - lo for _ in hops for lo, hi in self.parts] + [hi - lo for lo, hi in ends]
            table = [[] for _ in ring]
            for i, d in enumerate(ring):
                table[d] = [ring[(i + h) % n] * cap + lo for h in hops for lo, _ in self.parts]
                table[d] += [ring[(i + self.far) % n] * cap + lo for lo, _ in ends]
            self.starts = lax.dynamic_index_in_dim(jnp.asarray(table, jnp.int32), lax.axis_index("dp"), 0, keepdims=False)
        else:
            self.parts = [(0, cap)]
            self.sizes = [self.count * cap]
            self.starts = jnp.zeros((1,), jnp.int32)

    def go(self, a, b):
        return [lax.ppermute(v, "dp", self.right) for v in a], [lax.ppermute(v, "dp", self.left) for v in b]


class GatherSteps:
    def __init__(self, own, shard):
        self.own, self.out, self.s = own, list(shard), 1
        self.a = self.b = list(shard)
        self.sent = []
        if own.ring:
            self.step(Clock())

    def step(self, clock):
        own = self.own
        if not own.ring or self.s > own.far:
            return
        a, b = clock.at((self.a, self.b))
        if self.s == own.far:
            a, b = ([a[0]], [b[1]]) if len(own.parts) == 2 else ([a[0][:own.cut]], [b[0][own.cut:]])
        self.sent = [*a, *b]
        self.a, self.b = own.go(a, b)
        self.out += [*self.a, *self.b]
        self.s += 1

    def pin(self, clock):
        for v in self.sent:
            clock.add(v)

    def blocks(self):
        if not self.own.ring:
            return [lax.all_gather(self.out[0], "dp", axis=0, tiled=True)]
        while self.s <= self.own.far:
            self.step(Clock())
        return list(self.out)


class ScatterSteps:
    def __init__(self, own, blocks):
        self.own, self.blocks, self.s = own, blocks, own.count // 2 - 1
        self.sent = []
        if own.ring:
            self.a, self.b = own.go([blocks[-2]], [blocks[-1]])

    def more(self):
        return self.own.ring and self.s > 0

    def step(self, clock):
        own, s = self.own, self.s
        if not self.more():
            return

        def add(x, y):
            return (x.astype(F32) + y.astype(F32)).astype(BF)

        n = len(own.parts)
        y, x = (list(clock.at(self.blocks[m * n:(m + 1) * n])) for m in (2 * s - 1, 2 * s))
        a, b = self.a, self.b
        if s < own.far - 1:
            a, b = [add(v, w) for v, w in zip(x, a)], [add(v, w) for v, w in zip(y, b)]
        elif n == 2:
            a, b = [add(x[0], a[0]), x[1]], [y[0], add(y[1], b[0])]
        else:
            a = [lax.dynamic_update_slice_in_dim(x[0], add(x[0][:own.cut], a[0]), 0, 0)]
            b = [lax.dynamic_update_slice_in_dim(y[0], add(y[0][own.cut:], b[0]), own.cut, 0)]
        self.sent = [*a, *b]
        self.a, self.b = own.go(a, b)
        self.s -= 1

    def pin(self, clock):
        for v in self.sent:
            clock.add(v)

    def terms(self):
        own, blocks = self.own, self.blocks
        if own.ring:
            return [list(v) for v in zip(blocks[:len(own.parts)], self.a, self.b)]
        pad = -own.cap % 8
        v = blocks[0].reshape(own.count, own.cap, *blocks[0].shape[1:])
        v = jnp.pad(v, ((0, 0), (0, pad), (0, 0), (0, 0))).reshape(-1, *blocks[0].shape[1:])
        return [[lax.psum_scatter(v, "dp", scatter_dimension=0, tiled=True)[:own.cap]]]


def slot_rows(assign, slots):
    n = assign.shape[0]
    here = lax.broadcasted_iota(jnp.int32, (n, slots), 1) == assign[:, None]
    back = lax.broadcasted_iota(jnp.int32, (n, slots), 0) - n
    return jnp.sum(jnp.where(here, back, 0), axis=0) + n


def rotary_tables(places):
    half = HEAD // 2
    frequency = 10000.0 ** (-jnp.arange(half, dtype=F32) / half)
    angles = frequency[:, None] * places.astype(F32)[None, :]
    return jnp.cos(angles), jnp.sin(angles)


def on_device(tokens, cotangent, group_ids, assign_attn, assign_mlp,
              master_attn, moment_attn, square_attn, master_mlp, moment_mlp, square_mlp):
    owners = lax.axis_size("dp")
    tensor = lax.axis_size("tensor")
    rows_here, width = tokens.shape
    sub = width // LANES
    length = rows_here * tensor
    me, owner = lax.axis_index("tensor"), lax.axis_index("dp")
    perm = jnp.arange(tensor, dtype=jnp.int32) ^ me
    n_attn, n_mlp = width, assign_mlp.shape[0]
    dims, hidden = width // tensor, n_mlp // 2
    cap_a, cap_m = master_attn.shape[1], master_mlp.shape[1]
    part_rows = rows_here // CHUNKS
    cuts = [slice(j * part_rows, (j + 1) * part_rows) for j in range(CHUNKS)]

    def by_slot(v):
        return v.reshape(v.shape[1], sub, LANES)

    own_a, own_m = Owners(cap_a, False), Owners(cap_m, False)
    slots_a = owner * cap_a + jnp.arange(cap_a, dtype=jnp.int32)
    slots_m = owner * cap_m + jnp.arange(cap_m, dtype=jnp.int32)
    low_a = low_call(own_a.parts, after(by_slot(master_attn), perm, own_a.starts, own_m.starts, slots_a, slots_m))

    def named(slots, part):
        return jnp.any(slots[:, None] == part[None, :], axis=1)

    ring_a = GatherSteps(own_a, low_a)
    side = to_chip(after(tokens, low_a[0]))

    def per_slot(v):
        return jnp.broadcast_to(v.astype(F32)[:, None, None], (v.shape[0], 1, LANES))

    def beside(made):
        made, ring_a.a, ring_a.b = lax.optimization_barrier((made, ring_a.a, ring_a.b))
        return made

    pieces_a = beside(slot_rows(after(assign_attn, low_a[0]), owners * cap_a))
    tokens_near = to_core(after(tokens, pieces_a))
    names_m = after(assign_mlp, ring_a.a[0])
    ring_a.step(Clock())
    pieces_m = beside(slot_rows(names_m, owners * cap_m))
    states_m, places, groups = after((by_slot(master_mlp), jnp.arange(length, dtype=jnp.int32), group_ids), ring_a.a[0])
    ring_a.step(Clock())
    weight = jnp.broadcast_to((0.5 + 0.5 * groups.astype(F32))[:, None], (rows_here, LANES))
    weight, low_m, (cos_t, sin_t) = beside((weight, low_call(own_m.parts, states_m), rotary_tables(places)))
    names_a, names_m = after((assign_attn, assign_mlp), ring_a.a[0])
    ring_a.step(Clock())
    in_norm = (slots_a == names_a[n_attn]) | (slots_a == names_a[n_attn + 1])
    rate_a = per_slot(jnp.where(in_norm, 0.2, jnp.where(named(slots_a, names_a[3 * dims:n_attn]), 0.4, 0.06)))
    rate_m = per_slot(jnp.where(named(slots_m, names_m[hidden:]), 0.03, 0.06))
    rate_a, rate_m = beside((rate_a, rate_m))
    if own_a.ring:
        ring_a.out[-2:] = [*ring_a.a, *ring_a.b]
    side = after(side, *ring_a.sent)
    xs = [tokens, tokens_near, side, to_core(side)]
    blocks_a = ring_a.blocks()
    clock = Clock()
    clock.set(xs[3])
    blocks_a[0] = clock.at(blocks_a[0])
    w_attn, held_norms = place_call(blocks_a, own_a.starts, pieces_a, n_attn)
    clock.set(w_attn)
    ring_m = GatherSteps(own_m, after(low_m, *blocks_a[-2:]))
    norms_side = to_chip(held_norms)
    gains = [held_norms, to_core(held_norms), norms_side, to_core(norms_side)]
    norms, n_rel, qt, kt, vt, k4, v4 = qkv_call(perm, xs, gains, w_attn, cos_t, sin_t)
    clock.set(qt)
    ring_m.step(clock)
    ring_m.pin(clock)

    def summed(parts, *first, late=False):
        far = [to_core(clock.at(p)) for p in parts[3:]]
        sent = after(sum_call(parts[2], far), *first)
        near = to_core(after(parts[1], sent) if late else parts[1])
        clock.set(sent)
        return parts[0], near, to_chip(sent)

    fwd = []
    for j in range(CHUNKS):
        *zp, ot, lse = attn_fwd_call(j, CHUNKS, perm, clock.at(qt), k4, vt, w_attn)
        clock.set(ot)
        if j:
            ring_m.step(clock)
            ring_m.pin(clock)
        fwd.append((summed(zp, *([fwd[-1][0][2]] if j else [])), ot, lse))
    state, sides = [], []
    for j in range(CHUNKS):
        z, h, c = residual_call(fwd[j][0], clock.at(tokens[cuts[j]]), norms)
        clock.set(c)
        state.append((z, h, c))
        sides.append((to_core(c), to_chip(c)))
    ring_m.step(clock)
    ring_m.pin(clock)
    blocks_m = ring_m.blocks()
    blocks_m[0] = clock.at(blocks_m[0])
    w_mlp, _ = place_call(blocks_m, own_m.starts, pieces_m, n_mlp)
    clock.set(w_mlp)

    def gathered(own, near, side):
        half = side.shape[0] // 2
        side = clock.at(side)
        return [own, near, side, to_core(side[:half]), to_core(side[half:])]

    mids = []
    for j in range(CHUNKS):
        cs = gathered(state[j][2], *sides[j])
        cs[0] = clock.at(cs[0])
        *mp, c_rel, r, g = mlp_fwd_call(cs, w_mlp)
        clock.set(r)
        clock.add(sides[1][1] if j == 0 else mids[0][0][2])
        mids.append((summed(mp), c_rel, r, g))
    outs, sides, dms = [], [], []
    dnorm4 = []
    for j in range(CHUNKS):
        z, h, c = state[j]
        clock.add(mids[j][0][2])
        lo, dm, dn = out_call(mids[j][0], clock.at(h), cotangent[cuts[j]], weight[cuts[j]], norms)
        clock.set(dm)
        outs.append(lo)
        dnorm4.append(dn)
        dms.append(dm)
        sides.append((to_core(dm), to_chip(dm)))

    backs = []
    for j in range(CHUNKS):
        args = gathered(dms[j], *sides[j])
        args[0] = clock.at(args[0])
        *dcp, dm_rel, du = mlp_bwd_call(args, mids[j][3], w_mlp)
        clock.set(du)
        if j:
            grad_down = wgrad_call([clock.at(mids[0][2]), mids[1][2]], [backs[0][1], dm_rel])
            clock.set(grad_down)
        clock.add(sides[1][1] if j == 0 else backs[0][0][2])
        backs.append((summed(dcp), dm_rel, du))
    dhs, dzs, sides = [], [], []
    dnorm23 = []
    for j in range(CHUNKS):
        z, h, c = state[j]
        terms = backs[j][0]
        clock.add(terms[2])
        dh, dz, dn = mid_call(terms, clock.at(h), z, cotangent[cuts[j]], weight[cuts[j]], norms)
        clock.set(dz)
        dhs.append(dh)
        dnorm23.append(dn)
        dzs.append(dz)
        sides.append((to_core(dz), to_chip(dz)))
        if j == 0:
            grad_up = wgrad_call([clock.at(b[2]) for b in backs], [m[1] for m in mids])
            clock.set(grad_up)
            buckets_m = bucket_call([clock.at(grad_up), grad_down], own_m.starts, pieces_m, own_m.sizes)
            clock.set(buckets_m[0])
            sums_m = ScatterSteps(own_m, buckets_m)
    sums_m.step(clock)
    sums_m.pin(clock)

    prev, dqs = [(), ()], []
    for j in range(CHUNKS):
        _, ot, lse = fwd[j]
        args = gathered(dzs[j], *sides[j])
        dqs.append([])
        for i in range(2):
            args[0] = clock.at(args[0])
            dq, *prev[i] = attn_bwd_call(j, CHUNKS, i, perm, args, w_attn, qt, k4, kt, v4, ot, lse, cos_t, sin_t, tuple(prev[i]))
            clock.set(dq)
            dqs[j].append(dq)
            if i == 1:
                sums_m.step(clock)
                sums_m.pin(clock)
    dk, dv, grad_out = zip(*prev)
    grad_qkv, *dns = qkv_grad_call(perm, [[clock.at(dqs[0][0]), dqs[0][1]], *dqs[1:]], dk, dv, dnorm23, dnorm4, n_rel, w_attn, norms)
    clock.set(grad_qkv)
    dns = clock.at(dns)
    near, across = to_core(dns[1]), to_core(dns[3])
    da = qkv_in_call(0, CHUNKS, perm, [clock.at(dqs[0][0]), dqs[0][1]], dk, dv, w_attn)
    clock.set(da[0], across)
    norm_side = to_chip(clock.at(dns[2]) + across)
    da_terms = [summed(da, norm_side)]
    norm_sum = dns[0] + near + norm_side
    buckets_a = bucket_call([clock.at(grad_qkv), *grad_out, norm_sum], own_a.starts, pieces_a, own_a.sizes)
    clock.set(buckets_a[0])
    terms_m = sums_m.terms()
    for v in terms_m[0][1:]:
        clock.add(v)
    ring_a = ScatterSteps(own_a, [clock.at(v) for v in buckets_a])
    for j in range(1, CHUNKS):
        da = qkv_in_call(j, CHUNKS, perm, [clock.at(dqs[j][0]), dqs[j][1]], dk, dv, w_attn)
        clock.set(da[0])
        ring_a.step(clock)
        ring_a.pin(clock)
        da_terms.append(summed(da))
    new_m = adam_call(own_m.parts, terms_m, clock.at(rate_m), [by_slot(v) for v in (master_mlp, moment_mlp, square_mlp)])
    clock.set(new_m[0])
    ring_a.step(clock)
    ring_a.pin(clock)
    dxs = []
    for j in range(CHUNKS):
        dxs.append(last_call(da_terms[j], clock.at(tokens[cuts[j]]), dhs[j], norms))
        clock.set(dxs[j])
        ring_a.step(clock)
        ring_a.pin(clock)
    new_a = adam_call(own_a.parts, ring_a.terms(), rate_a, [by_slot(v) for v in (master_attn, moment_attn, square_attn)])
    return (jnp.concatenate(outs, axis=0), jnp.concatenate(dxs, axis=0),
            *(v.reshape(master_attn.shape) for v in new_a), *(v.reshape(master_mlp.shape) for v in new_m))


def solution(mesh):
    tok = P(("dp", "tensor"), None)
    par = P("tensor", "dp", None)
    return jax.shard_map(
        on_device, mesh=mesh,
        in_specs=(tok, tok, P(("dp", "tensor")), P(), P(), par, par, par, par, par, par),
        out_specs=(tok, tok, par, par, par, par, par, par),
        check_vma=False,
    )
```

```python
import functools
import jax
import jax.numpy as jnp
from jax import lax
from jax.sharding import PartitionSpec as P
from jax.experimental import pallas as pl
from jax.experimental.pallas import tpu as pltpu

BF = jnp.bfloat16
F32 = jnp.float32
EPS = 1e-5
HEAD = 64
LANES = 128
QB = 256
CHUNKS = 2
ADAM_STEP = 5


def dot_nn(a, b):
    return lax.dot_general(a, b, (((1,), (0,)), ((), ())), preferred_element_type=F32)


def dot_nt(a, b):
    return lax.dot_general(a, b, (((1,), (1,)), ((), ())), preferred_element_type=F32)


def params(mib):
    return pltpu.CompilerParams(vmem_limit_bytes=mib * 1024 * 1024)


def cost(us):
    return pl.CostEstimate(flops=int(us * 3e6), bytes_accessed=int(us * 1e4), transcendentals=0)


def whole(shape, at=None):
    at = at or (0,) * len(shape)
    return pl.BlockSpec(shape, lambda *_: at)


def shape(dims, dtype):
    return jax.ShapeDtypeStruct(dims, dtype)


def choose(index, refs, into):
    for i in range(4):
        @pl.when(index == i)
        def _():
            if i == 3 and len(refs) == 5:
                half = refs[3].shape[0]
                into[0:half, :] = refs[3][...]
                into[half:, :] = refs[4][...]
            else:
                into[...] = refs[i][...]


def spread(index, refs, value):
    for i in range(4):
        @pl.when(index == i)
        def _():
            if i == 3:
                half = refs[3].shape[0]
                refs[3][...] = value[0:half]
                refs[4][...] = value[half:]
            else:
                refs[i][...] = value


def block_dims(rows, width):
    return [(rows, width)] * 3 + [(rows // 2, width)] * 2


def centre(v):
    mean = jnp.mean(v, axis=-1, keepdims=True)
    vc = v - mean
    s = lax.rsqrt(jnp.mean(vc * vc, axis=-1, keepdims=True) + EPS)
    return vc * s, s


def norm_back(n, s, y, gain):
    dn = y * gain
    return s * (dn - jnp.mean(dn, axis=-1, keepdims=True) - n * jnp.mean(dn * n, axis=-1, keepdims=True))


def total(parts):
    return sum(p[...].astype(F32) for p in parts)


def rows_call(kernel, outs, *args, part=None):
    if part is None:
        return pl.pallas_call(kernel, out_shape=outs, compiler_params=params(10), cost_estimate=cost(2.5))(*args)
    index, count, earlier = part
    rows, width = outs[0].shape
    outs = [shape((rows * count, width), outs[0].dtype), *outs[1:]]
    extra = [] if earlier is None else [earlier]

    def inner(*refs):
        n = len(args)
        kernel(*refs[:n], *refs[n + len(extra):])

    return pl.pallas_call(
        inner, grid=(1,),
        in_specs=[whole(v.shape) for v in args] + [pl.BlockSpec(memory_space=pl.ANY)] * len(extra),
        out_specs=[whole((rows, width), (index, 0))] + [whole(o.shape) for o in outs[1:]],
        out_shape=outs, input_output_aliases={len(args): 0} if extra else {},
        compiler_params=params(10), cost_estimate=cost(2.5),
    )(*args, *extra)


def residual_kernel(p0, p1, p2, x_ref, norms, z_ref, h_ref, c_ref):
    z = total([p0, p1, p2])
    z_ref[...] = z
    n, _ = centre(z)
    h = x_ref[...].astype(F32) + n * norms[2:3, :] + norms[3:4, :]
    h_ref[...] = h
    n, _ = centre(h)
    c_ref[...] = (n * norms[4:5, :] + norms[5:6, :]).astype(BF)


def residual_call(parts, x, norms):
    return rows_call(residual_kernel, [shape(x.shape, F32), shape(x.shape, F32), shape(x.shape, BF)], *parts, x, norms)


def out_kernel(p0, p1, p2, h_ref, ct_ref, wt_ref, norms, lo_ref, dm_ref, dn_ref):
    n, s = centre(total([p0, p1, p2]))
    lo_ref[...] = (h_ref[...] + n * norms[6:7, :] + norms[7:8, :]).astype(BF)
    e = ct_ref[...].astype(F32) * wt_ref[:, 0:1]
    dm_ref[...] = norm_back(n, s, e, norms[6:7, :]).astype(BF)
    dn_ref[0:1, :] = jnp.sum(e * n, axis=0, keepdims=True)
    dn_ref[1:2, :] = jnp.sum(e, axis=0, keepdims=True)


def out_call(parts, h, ct, wt, norms, part):
    return rows_call(out_kernel, [shape(h.shape, BF), shape(h.shape, BF), shape((2, h.shape[1]), F32)], *parts, h, ct, wt, norms, part=part)


def mid_kernel(p0, p1, p2, h_ref, z_ref, ct_ref, wt_ref, norms, dh_ref, dz_ref, dn_ref):
    dc = total([p0, p1, p2])
    n3, s3 = centre(h_ref[...])
    dh = ct_ref[...].astype(F32) * wt_ref[:, 0:1] + norm_back(n3, s3, dc, norms[4:5, :])
    dh_ref[...] = dh
    n2, s2 = centre(z_ref[...])
    dz_ref[...] = norm_back(n2, s2, dh, norms[2:3, :]).astype(BF)
    dn_ref[0:1, :] = jnp.sum(dh * n2, axis=0, keepdims=True)
    dn_ref[1:2, :] = jnp.sum(dh, axis=0, keepdims=True)
    dn_ref[2:3, :] = jnp.sum(dc * n3, axis=0, keepdims=True)
    dn_ref[3:4, :] = jnp.sum(dc, axis=0, keepdims=True)


def mid_call(parts, h, z, ct, wt, norms):
    return rows_call(mid_kernel, [shape(h.shape, F32), shape(h.shape, BF), shape((4, h.shape[1]), F32)],
                     *parts, h, z, ct, wt, norms)


def last_kernel(p0, p1, p2, x_ref, dh_ref, norms, dx_ref):
    n1, s1 = centre(x_ref[...].astype(F32))
    dx_ref[...] = dh_ref[...] + norm_back(n1, s1, total([p0, p1, p2]), norms[0:1, :])


def last_call(parts, x, dh, norms, part):
    return rows_call(last_kernel, [shape(x.shape, F32)], *parts, x, dh, norms, part=part)[0]


def sum_kernel(keep, *refs):
    fars, out = refs[:-1], refs[-1]
    step = fars[0].shape[0]
    for i, f in enumerate(fars):
        at = slice(i * step, (i + 1) * step)
        out[at, :] = (keep[at, :].astype(F32) + f[...].astype(F32)).astype(BF)


def sum_call(keep, fars):
    return pl.pallas_call(
        sum_kernel, out_shape=shape(keep.shape, BF), compiler_params=params(4), cost_estimate=cost(0.1),
    )(keep, *fars)


def qkv_kernel(perm, *refs):
    xs, gs, (w_ref, cos_ref, sin_ref, norms, n_ref, qt_ref, kt_ref, vt_ref, k4_ref, v4_ref, cur) = refs[:4], refs[4:8], refs[8:]

    @pl.when(pl.program_id(0) == 0)
    def _():
        for t in range(4):
            for i, g in enumerate(gs):
                @pl.when(perm[t] == i)
                def _():
                    norms[2 * t:2 * t + 2, :] = g[0:2, :]

    choose(pl.program_id(0), xs, cur)
    n, _ = centre(cur[...].astype(F32))
    n_ref[0] = n.astype(BF)
    a = (n * norms[0:1, :] + norms[1:2, :]).astype(BF)
    cos, sin = cos_ref[...], sin_ref[...]
    dims = qt_ref.shape[0]
    half = HEAD // 2
    for part in range(3):
        proj = dot_nt(w_ref[part * dims:(part + 1) * dims, :], a)
        for h in range(dims // HEAD):
            lo = slice(h * HEAD, h * HEAD + half)
            hi = slice(h * HEAD + half, (h + 1) * HEAD)
            hd = slice(h * HEAD, (h + 1) * HEAD)
            if part < 2:
                first, second = proj[lo], proj[hi]
                r1 = first * cos - second * sin
                r2 = second * cos + first * sin
                if part == 0:
                    qt_ref[lo, :] = (r1 * 0.125).astype(BF)
                    qt_ref[hi, :] = (r2 * 0.125).astype(BF)
                else:
                    full = jnp.concatenate([r1, r2], axis=0)
                    kt_ref[hd, :] = full.astype(BF)
                    k4_ref[h] = full.T.astype(BF)
            else:
                vt_ref[hd, :] = proj[hd].astype(BF)
                v4_ref[h] = proj[hd].T.astype(BF)


def qkv_call(perm, xs, gains, w, cos_t, sin_t):
    rows, width = xs[0].shape
    n = len(xs)
    dims = w.shape[0] // 4
    heads = dims // HEAD
    length = n * rows
    tok = pl.BlockSpec((dims, rows), lambda k, p: (0, p[k]))
    hd = pl.BlockSpec((heads, rows, HEAD), lambda k, p: (0, p[k], 0))
    tab = pl.BlockSpec((HEAD // 2, rows), lambda k, p: (0, p[k]))
    return pl.pallas_call(
        qkv_kernel,
        grid_spec=pltpu.PrefetchScalarGridSpec(
            num_scalar_prefetch=1, grid=(n,),
            in_specs=[whole((rows, width))] * n + [whole(g.shape) for g in gains] + [whole((3 * dims, width)), tab, tab],
            out_specs=[whole((8, width)), pl.BlockSpec((1, rows, width), lambda k, p: (k, 0, 0)), tok, tok, tok, hd, hd],
            scratch_shapes=[pltpu.VMEM((rows, width), BF)],
        ),
        out_shape=[shape((8, width), F32), shape((n, rows, width), BF)] + [shape((dims, length), BF)] * 3 + [shape((heads, length, HEAD), BF)] * 2,
        compiler_params=params(20), cost_estimate=cost(10),
    )(perm, *xs, *gains, w, cos_t, sin_t)


def visible(chunk, diag):
    return (lax.broadcasted_iota(jnp.int32, (diag, QB), 0)
            <= lax.broadcasted_iota(jnp.int32, (diag, QB), 1) + chunk * QB)


def key_spans(n, wide, diag):
    return ([pl.ds(0, n * wide)] if n else []) + [pl.ds(n * wide, diag)]


def pipelined(heads, first, second, third):
    ahead, behind = first(0), None
    for h in range(heads):
        now = ahead
        if h + 1 < heads:
            ahead = first(h + 1)
        done = second(h, now)
        if behind is not None:
            third(h - 1, behind)
        behind = done
    third(heads - 1, behind)


def attn_fwd_kernel(chunk, chunks, count, perm, qt_ref, k4_ref, vt_ref, wo_ref, *rest):
    zs, (ot_ref, lse_ref, acc) = rest[:5], rest[5:]
    heads = k4_ref.shape[0]
    diag = (chunk + 1) * QB
    seen = visible(chunk, diag)
    hd = [slice(h * HEAD, (h + 1) * HEAD) for h in range(heads)]
    cols = [slice(t * QB, (t + 1) * QB) for t in range(count)]
    mine = [slice((chunks * t + chunk) * QB, (chunks * t + chunk + 1) * QB) for t in range(count)]

    def unit(u):
        t, h = u // heads, u % heads
        return t, h, key_spans(t, chunks * QB, diag)

    def scores(u):
        t, h, spans = unit(u)
        return [dot_nn(k4_ref[h, ks, :], qt_ref[hd[h], mine[t]]) for ks in spans]

    def soft(u, s):
        t, h, _ = unit(u)
        s = s[:-1] + [jnp.where(seen, s[-1], -1e30)]
        m = functools.reduce(jnp.maximum, [jnp.max(v, axis=0, keepdims=True) for v in s])
        p = [jnp.exp(v - m) for v in s]
        l = sum(jnp.sum(v, axis=0, keepdims=True) for v in p)
        lse_ref[h:h + 1, cols[t]] = m + jnp.log(l)
        return [v.astype(BF) for v in p], l

    def attend(u, done):
        t, h, spans = unit(u)
        acc[hd[h], cols[t]] = sum(dot_nn(vt_ref[hd[h], ks], v) for ks, v in zip(spans, done[0])) / done[1]

    pipelined(heads * count, scores, soft, attend)
    ot_ref[...] = acc[...].astype(BF)
    for t in range(count):
        o = acc[:, cols[t]].T.astype(BF)
        spread(perm[t], zs, dot_nn(o, wo_ref[...]).astype(BF))


def attn_fwd_call(chunk, chunks, perm, qt, k4, vt, w):
    dims, length = qt.shape
    width = w.shape[1]
    heads = dims // HEAD
    n = length // (chunks * QB)
    outs = block_dims(QB, width) + [(dims, n * QB)]
    return pl.pallas_call(
        functools.partial(attn_fwd_kernel, chunk, chunks, n),
        grid_spec=pltpu.PrefetchScalarGridSpec(
            num_scalar_prefetch=1, grid=(1,),
            in_specs=[whole(qt.shape), whole(k4.shape), whole(vt.shape), whole((dims, width), (3, 0))],
            out_specs=[whole(d) for d in outs] + [whole((heads, n * QB))],
            scratch_shapes=[pltpu.VMEM((dims, n * QB), F32)],
        ),
        out_shape=[shape(d, BF) for d in outs] + [shape((heads, n * QB), F32)],
        compiler_params=params(22), cost_estimate=cost(9.5 + 1.5 * chunk),
    )(perm, qt, k4, vt, w)


def attn_bwd_kernel(chunk, chunks, count, pair, perm, *refs):
    dzs, refs = refs[:5], refs[5:]
    wo_ref, qt_ref, k4_ref, kt_ref, v4_ref, ot_ref, lse_ref, cos_ref, sin_ref = refs[:9]
    refs = refs[9:]
    if chunk == 0:
        dq_ref, dk_ref, dv_ref, gwo_ref, acc, dot_ref, dl_ref, dz_ref = refs
    else:
        dk0, dv0, gwo0, dq_ref, dkl_ref, dvl_ref, gwo_ref, acc, dot_ref, dl_ref, dz_ref, dk_ref, dv_ref = refs
    heads = k4_ref.shape[0]
    half = HEAD // 2
    wide = chunks * QB
    diag = (chunk + 1) * QB
    seen = visible(chunk, diag)
    hd = [slice(h * HEAD, (h + 1) * HEAD) for h in range(heads)]
    cols = [slice(t * QB, (t + 1) * QB) for t in range(count)]
    mine = [slice((chunks * t + chunk) * QB, (chunks * t + chunk + 1) * QB) for t in range(count)]
    if chunk == 0:
        dk_ref[...] = jnp.zeros_like(dk_ref)
        dv_ref[...] = jnp.zeros_like(dv_ref)
    else:
        dk_ref[...] = dk0[...]
        dv_ref[...] = dv0[...]
    for t in range(count):
        choose(perm[t], dzs, dz_ref.at[t])
        dot_ref[:, cols[t]] = dot_nt(wo_ref[...], dz_ref[t]).astype(BF)
    prod = dot_ref[...].astype(F32) * ot_ref[...].astype(F32)
    for h in range(heads):
        dl_ref[h:h + 1, :] = jnp.sum(prod[hd[h]], axis=0, keepdims=True)

    def unit(u):
        t, h = u // heads, u % heads
        return t, h, key_spans(t, wide, diag)

    def scores(u):
        t, h, spans = unit(u)
        return [(dot_nn(k4_ref[h, ks, :], qt_ref[hd[h], mine[t]]), dot_nn(v4_ref[h, ks, :], dot_ref[hd[h], cols[t]])) for ks in spans]

    def soft(u, pairs):
        t, h, spans = unit(u)
        lse, delta = lse_ref[heads * pair + h:heads * pair + h + 1, cols[t]], dl_ref[h:h + 1, cols[t]]
        out = []
        for i, (s, dp) in enumerate(pairs):
            p = jnp.exp(s - lse)
            if i == len(pairs) - 1:
                p = jnp.where(seen, p, 0.0)
            out.append((p.astype(BF), (p * (dp - delta)).astype(BF)))
        return out

    def back(u, pairs):
        t, h, spans = unit(u)
        q, do = qt_ref[hd[h], mine[t]], dot_ref[hd[h], cols[t]]
        dq = 0.0
        for ks, (p, ds) in zip(spans, pairs):
            dv_ref[hd[h], ks] += dot_nt(do, p)
            dk_ref[hd[h], ks] += dot_nt(q, ds)
            dq = dq + dot_nn(kt_ref[hd[h], ks], ds)
        acc[hd[h], cols[t]] = dq

    pipelined(heads * count, scores, soft, back)
    g = dot_nn(ot_ref[...], dz_ref[...].reshape(count * QB, dz_ref.shape[2]))
    gwo_ref[...] = g if chunk == 0 else gwo0[...] + g

    def unturn(src, at, to, scale, out):
        cos, sin = cos_ref[:, at], sin_ref[:, at]
        for h in range(heads):
            lo = slice(h * HEAD, h * HEAD + half)
            hi = slice(h * HEAD + half, (h + 1) * HEAD)
            g1, g2 = src[lo, to] * scale, src[hi, to] * scale
            out[lo, to] = (g1 * cos + g2 * sin).astype(BF)
            out[hi, to] = (g2 * cos - g1 * sin).astype(BF)

    for t in range(count):
        unturn(acc, mine[t], cols[t], 0.125, dq_ref)
    if chunk == chunks - 1:
        unturn(dk_ref, slice(None), slice(None), 1.0, dkl_ref)
        dvl_ref[...] = dv_ref[...].astype(BF)


def attn_bwd_call(chunk, chunks, pair, perm, dzs, w, qt, k4, kt, v4, ot, lse, cos_t, sin_t, prev=()):
    dims, length = qt.shape[0] // 2, qt.shape[1]
    width = w.shape[1]
    heads = dims // HEAD
    n = length // (chunks * QB)
    full, tb = whole((dims, length), (pair, 0)), whole((dims, n * QB), (pair, 0))
    kv4 = whole((heads, length, HEAD), (pair, 0, 0))
    out_full, out_tb, out_w = whole((dims, length)), whole((dims, n * QB)), whole((dims, width))
    in_specs = [whole(d) for d in block_dims(QB, width)] + [
        whole((dims, width), (6 + pair, 0)), full, kv4, full, kv4, tb, whole(lse.shape), whole(cos_t.shape), whole(sin_t.shape)]
    scratch = [pltpu.VMEM((dims, n * QB), F32), pltpu.VMEM((dims, n * QB), BF), pltpu.VMEM((8, n * QB), F32), pltpu.VMEM((n, QB, width), BF)]
    kv = F32
    if chunk:
        in_specs += [out_full, out_full, out_w]
        scratch += [pltpu.VMEM((dims, length), F32)] * 2
        kv = BF
    return pl.pallas_call(
        functools.partial(attn_bwd_kernel, chunk, chunks, n, pair),
        grid_spec=pltpu.PrefetchScalarGridSpec(
            num_scalar_prefetch=1, grid=(1,), in_specs=in_specs,
            out_specs=[out_tb, out_full, out_full, out_w], scratch_shapes=scratch,
        ),
        out_shape=[shape((dims, n * QB), BF), shape((dims, length), kv), shape((dims, length), kv), shape((dims, width), F32)],
        compiler_params=params(22), cost_estimate=cost(10 + 2 * chunk),
    )(perm, *dzs, w, qt, k4, kt, v4, ot, lse, cos_t, sin_t, *prev)


def stack_rows(refs, into, cols=slice(None)):
    at = 0
    for r in refs:
        into[at:at + r.shape[0], cols] = r[...]
        at += r.shape[0]


def qkv_in_kernel(perm, *refs):
    parts, w_ref, das, dx = refs[:6], refs[6], refs[7:12], refs[12]
    stack_rows(parts, dx)
    grad = dx[...].astype(F32).T.astype(BF)
    spread(perm[pl.program_id(0)], das, dot_nn(grad, w_ref[...]).astype(BF))


def qkv_in_call(chunk, chunks, perm, dq, dk, dv, w):
    dims, length = dk[0].shape
    width = w.shape[1]
    n = length // (chunks * QB)
    at = pl.BlockSpec((dims, QB), lambda t, p: (0, chunks * t + chunk))
    return pl.pallas_call(
        qkv_in_kernel,
        grid_spec=pltpu.PrefetchScalarGridSpec(
            num_scalar_prefetch=1, grid=(n,),
            in_specs=[pl.BlockSpec((dims, QB), lambda t, p: (0, t))] * 2 + [at] * 4 + [whole((6 * dims, width))],
            out_specs=[whole(d) for d in block_dims(QB, width)],
            scratch_shapes=[pltpu.VMEM((6 * dims, QB), BF)],
        ),
        out_shape=[shape(d, BF) for d in block_dims(QB, width)],
        compiler_params=params(8), cost_estimate=cost(5),
    )(perm, *dq, *dk, *dv, w)


def qkv_grad_kernel(chunks, count, perm, *refs):
    dqs, kvs, refs = refs[:2 * chunks], refs[2 * chunks:2 * chunks + 4], refs[2 * chunks + 4:]
    d23, d4, (n_ref, w_ref, norms, gw_ref), dns, (dx, rows, sums_ref) = refs[:chunks], refs[chunks:2 * chunks], refs[2 * chunks:2 * chunks + 4], refs[2 * chunks + 4:2 * chunks + 8], refs[2 * chunks + 8:]
    dims = kvs[0].shape[0]
    wide = chunks * QB

    @pl.when(pl.program_id(0) == 0)
    def _():
        for i in range(chunks):
            for p in range(2):
                for t in range(count):
                    to = slice(t * wide + i * QB, t * wide + (i + 1) * QB)
                    dx[p * dims:(p + 1) * dims, to] = dqs[2 * i + p][:, t * QB:(t + 1) * QB]
        stack_rows(kvs, dx.at[2 * dims:])
        sums_ref[...] = jnp.sum(dx[...].astype(F32), axis=1, keepdims=True)

    grad = sum(dot_nn(dx[:, t * wide:(t + 1) * wide], n_ref[perm[t]]) for t in range(count))
    sums = sums_ref[...]
    w = w_ref[...].astype(F32)
    gw_ref[...] = (grad * norms[0:1, :] + sums * norms[1:2, :]).astype(BF)
    rows[0:1, :] = jnp.sum(grad * w, axis=0, keepdims=True)
    rows[1:2, :] = jnp.sum(sums * w, axis=0, keepdims=True)
    rows[2:6, :] = total(d23)
    rows[6:8, :] = total(d4)
    for i, out in enumerate(dns):
        for t in range(4):
            @pl.when(perm[i] == t)
            def _():
                out[...] = rows[2 * t:2 * t + 2, :]


def qkv_grad_call(perm, dqs, dk, dv, d23, d4, n_rel, w, norms):
    chunks = len(dqs)
    n, rows, width = n_rel.shape
    dims = dk[0].shape[0]
    cols = 256
    args = [v for dq in dqs for v in dq] + [*dk, *dv]
    return pl.pallas_call(
        functools.partial(qkv_grad_kernel, chunks, n),
        grid_spec=pltpu.PrefetchScalarGridSpec(
            num_scalar_prefetch=1, grid=(width // cols,),
            in_specs=[whole(v.shape) for v in args] + [pl.BlockSpec((v.shape[0], cols), lambda i, p: (0, i)) for v in (*d23, *d4)] + [
                pl.BlockSpec((n, rows, cols), lambda i, p: (0, 0, i)), pl.BlockSpec((6 * dims, cols), lambda i, p: (0, i)),
                pl.BlockSpec((8, cols), lambda i, p: (0, i))],
            out_specs=[pl.BlockSpec((6 * dims, cols), lambda i, p: (0, i))] + [pl.BlockSpec((2, cols), lambda i, p: (0, i))] * 4,
            scratch_shapes=[pltpu.VMEM((6 * dims, n * rows), BF), pltpu.VMEM((8, cols), F32), pltpu.VMEM((6 * dims, 1), F32)],
        ),
        out_shape=[shape((6 * dims, width), BF)] + [shape((2, width), F32)] * 4,
        compiler_params=params(16), cost_estimate=cost(7),
    )(perm, *args, *d23, *d4, n_rel, w, norms)


def mlp_fwd_kernel(*refs):
    cs, (w1_ref, w2_ref), ms, (c_ref, r_ref, g_ref) = refs[:5], refs[5:7], refs[7:12], refs[12:]
    k = pl.program_id(0)
    choose(k, cs, c_ref.at[0])
    u = dot_nt(c_ref[0], w1_ref[...])
    cdf = 0.5 * (1.0 + lax.erf(u * 0.7071067811865476))
    r = (u * cdf).astype(BF)
    r_ref[0] = r
    g_ref[0] = (cdf + u * (0.3989422804014327 * jnp.exp(-0.5 * u * u))).astype(BF)
    spread(k, ms, dot_nn(r, w2_ref[...]).astype(BF))


def mlp_fwd_call(cs, w):
    rows, width = cs[0].shape
    n, hid = 4, w.shape[0] // 2
    dims = block_dims(rows, width)
    blk = pl.BlockSpec((1, rows, width), lambda k: (k, 0, 0))
    hb = pl.BlockSpec((1, rows, hid), lambda k: (k, 0, 0))
    return pl.pallas_call(
        mlp_fwd_kernel, grid=(n,),
        in_specs=[whole(c.shape) for c in cs] + [whole((hid, width), (0, 0)), whole((hid, width), (1, 0))],
        out_specs=[whole(d) for d in dims] + [blk, hb, hb],
        out_shape=[shape(d, BF) for d in dims] + [shape((n, rows, width), BF)] + [shape((n, rows, hid), BF)] * 2,
        compiler_params=params(16), cost_estimate=cost(9),
    )(*cs, w, w)


def mlp_bwd_kernel(*refs):
    dms, (g_ref, w1_ref, w2_ref), dcs, (dm_ref, du_ref) = refs[:5], refs[5:8], refs[8:13], refs[13:]
    k = pl.program_id(0)
    choose(k, dms, dm_ref.at[0])
    dr = dot_nt(dm_ref[0], w2_ref[...])
    du = (dr * g_ref[0].astype(F32)).astype(BF)
    du_ref[0] = du
    spread(k, dcs, dot_nn(du, w1_ref[...]).astype(BF))


def mlp_bwd_call(dms, g, w):
    rows, width = dms[0].shape
    n, hid = 4, w.shape[0] // 2
    dims = block_dims(rows, width)
    blk = pl.BlockSpec((1, rows, width), lambda k: (k, 0, 0))
    hb = pl.BlockSpec((1, rows, hid), lambda k: (k, 0, 0))
    return pl.pallas_call(
        mlp_bwd_kernel, grid=(n,),
        in_specs=[whole(d.shape) for d in dms] + [hb, whole((hid, width), (0, 0)), whole((hid, width), (1, 0))],
        out_specs=[whole(d) for d in dims] + [blk, hb],
        out_shape=[shape(d, BF) for d in dims] + [shape((n, rows, width), BF), shape((n, rows, hid), BF)],
        compiler_params=params(16), cost_estimate=cost(8),
    )(*dms, g, w, w)


def wgrad_kernel(*refs):
    n = len(refs) // 2
    out = refs[-1]
    acc = 0.0
    for x, y in zip(refs[:n], refs[n:2 * n]):
        tok = x.shape[0] * x.shape[1]
        acc = acc + lax.dot_general(x[...].reshape(tok, x.shape[2]), y[...].reshape(tok, y.shape[2]), (((0,), (0,)), ((), ())), preferred_element_type=F32)
    out[...] = acc.astype(BF)


def wgrad_call(xs, ys, tile=512):
    blocks, rows, hid = xs[0].shape
    width = ys[0].shape[2]
    return pl.pallas_call(
        wgrad_kernel, grid=(hid // tile,),
        in_specs=[pl.BlockSpec((blocks, rows, tile), lambda i: (0, 0, i))] * len(xs) + [whole(y.shape) for y in ys],
        out_specs=pl.BlockSpec((tile, width), lambda i: (i, 0)),
        out_shape=shape((hid, width), BF),
        compiler_params=params(24), cost_estimate=cost(6),
    )(*xs, *ys)


UNROLL = (58, 57, 56, 48, 46, 43, 42, 40, 22, 20, 18, 16, 8, 6, 4, 3, 2, 1)


def place_kernel(sizes, count, starts, pieces, *refs):
    srcs, out_ref, rest_ref, mid = refs[:-3], refs[-3], refs[-2], refs[-1]
    sub = srcs[0].shape[1]
    for k, src in enumerate(srcs):
        base = starts[k]
        step = next(u for u in UNROLL if sizes[k] % u == 0)

        def body(i, c, src=src, base=base, step=step):
            tos = [pieces[base + i * step + u] for u in range(step)]
            vals = [src[i * step + u].astype(F32) for u in range(step)]
            for u in range(step):
                mid[pl.ds(pl.multiple_of(tos[u] * sub, sub), sub), :] = vals[u]
            return c

        lax.fori_loop(0, sizes[k] // step, body, 0)
    rows = 64

    def spread(i, c):
        r = pl.multiple_of(i * rows, rows)
        for j in range(sub):
            part = mid[pl.ds(r * sub + j, rows, stride=sub), :]
            out_ref[pl.ds(r, rows), j * LANES:(j + 1) * LANES] = part.astype(BF)
        return c

    lax.fori_loop(0, count // rows, spread, 0)
    for j in range(sub):
        rest_ref[:, j * LANES:(j + 1) * LANES] = mid[pl.ds(count * sub + j, 8, stride=sub), :]


def place_call(blocks, starts, pieces, count):
    sub = blocks[0].shape[1]
    sizes = [b.shape[0] for b in blocks]
    return pl.pallas_call(
        functools.partial(place_kernel, sizes, count),
        grid_spec=pltpu.PrefetchScalarGridSpec(
            num_scalar_prefetch=2, grid=(1,),
            in_specs=[whole(b.shape) for b in blocks],
            out_specs=[whole((count, sub * LANES)), whole((8, sub * LANES))],
            scratch_shapes=[pltpu.VMEM(((count + 8) * sub, LANES), F32)],
        ),
        out_shape=[shape((count, sub * LANES), BF), shape((8, sub * LANES), F32)],
        compiler_params=params(10 + count // 146), cost_estimate=cost(count / 450),
    )(starts, pieces, *blocks)


def bucket_kernel(sizes, starts, pieces, *refs):
    n = len(sizes)
    grads, outs, mid = refs[:-n - 1], refs[-n - 1:-1], refs[-1]
    width = grads[0].shape[1]
    sub = width // LANES
    rows = 64
    at = 0
    for g in grads:
        if g.shape[0] % rows:
            for j in range(sub):
                mid[pl.ds(at * sub + j, g.shape[0], stride=sub), :] = g[:, j * LANES:(j + 1) * LANES].astype(F32)
            at += g.shape[0]
            continue

        def split(i, c, g=g, at=at):
            r = pl.multiple_of(i * rows, rows)
            for j in range(sub):
                mid[pl.ds((at + r) * sub + j, rows, stride=sub), :] = g[pl.ds(r, rows), j * LANES:(j + 1) * LANES].astype(F32)
            return c

        lax.fori_loop(0, g.shape[0] // rows, split, 0)
        at += g.shape[0]
    mid[at * sub:(at + 8) * sub, :] = jnp.zeros((8 * sub, LANES), F32)
    for k, out in enumerate(outs):
        base = starts[k]
        step = next(u for u in UNROLL if sizes[k] % u == 0)

        def body(i, c, out=out, base=base, step=step):
            srcs = [pieces[base + i * step + u] for u in range(step)]
            vals = [mid[pl.ds(pl.multiple_of(v * sub, sub), sub), :].astype(BF) for v in srcs]
            for u in range(step):
                out[i * step + u] = vals[u]
            return c

        lax.fori_loop(0, sizes[k] // step, body, 0)


def bucket_call(grads, starts, pieces, sizes):
    width = grads[0].shape[1]
    sub = width // LANES
    count = sum(g.shape[0] for g in grads)
    shapes = [(s, sub, LANES) for s in sizes]
    return pl.pallas_call(
        functools.partial(bucket_kernel, sizes),
        grid_spec=pltpu.PrefetchScalarGridSpec(
            num_scalar_prefetch=2, grid=(1,),
            in_specs=[whole(g.shape) for g in grads],
            out_specs=[whole(s) for s in shapes],
            scratch_shapes=[pltpu.VMEM(((count + 8) * sub, LANES), F32)],
        ),
        out_shape=[jax.ShapeDtypeStruct(s, BF) for s in shapes],
        compiler_params=params(8 + count // 146), cost_estimate=cost(count / 350),
    )(starts, pieces, *grads)


def adam_kernel(bounds, *refs):
    parts, (rate, m_ref, f_ref, s_ref, om, of, os) = refs[:-7], refs[-7:]
    each = len(parts) // len(bounds)
    for i, (lo, hi) in enumerate(bounds):
        at = slice(lo, hi)
        g = total(parts[i * each:(i + 1) * each])
        first = 0.5 * f_ref[at] + 0.5 * g
        second = 0.5 * s_ref[at] + 0.5 * g * g
        of[at] = first
        os[at] = second
        w = m_ref[at]
        first = first / (1.0 - 0.5**ADAM_STEP)
        second = second / (1.0 - 0.5**ADAM_STEP)
        om[at] = w - rate[at] * (first / (jnp.sqrt(second) + 1e-8) + 0.1 * w)


def adam_call(bounds, parts, rate, states):
    cap, sub, lanes = states[0].shape
    step = next(d for d in range(64, 0, -1) if cap % d == 0) if len(bounds) == 1 else cap
    if len(bounds) == 1:
        bounds = [(0, step)]
    blk = pl.BlockSpec((step, sub, lanes), lambda i: (i, 0, 0))
    terms = [v for part in parts for v in part]
    return pl.pallas_call(
        functools.partial(adam_kernel, bounds), grid=(cap // step,),
        in_specs=[blk if len(bounds) == 1 else whole(v.shape) for v in terms] + [
            pl.BlockSpec((step, 1, lanes), lambda i: (i, 0, 0))] + [blk] * 3,
        out_specs=[blk] * 3,
        out_shape=[shape(v.shape, F32) for v in states],
        compiler_params=params(12), cost_estimate=cost(cap / 80),
    )(*terms, rate, *states)


def low_kernel(bounds, x_ref, *outs):
    for (lo, hi), out in zip(bounds, outs):
        out[...] = x_ref[lo:hi].astype(BF)


def low_call(bounds, v):
    return list(pl.pallas_call(
        functools.partial(low_kernel, bounds), out_shape=[shape((hi - lo, *v.shape[1:]), BF) for lo, hi in bounds],
        compiler_params=params(6), cost_estimate=cost(1),
    )(v))


TOP = [(0, 1), (1, 0), (2, 3), (3, 2)]
SIDE = [(0, 2), (1, 3), (2, 0), (3, 1)]
RINGS = {8: [0, 2, 4, 6, 7, 5, 3, 1]}


def to_core(v):
    return lax.ppermute(v, "tensor", TOP)


def to_chip(v):
    return lax.ppermute(v, "tensor", SIDE)


def after(v, *first):
    if not first:
        return v
    return lax.optimization_barrier((v, *first))[0]


class Clock:
    def __init__(self):
        self.last = []

    def set(self, *values):
        self.last = list(values)

    def add(self, value):
        self.last.append(value)

    def at(self, value):
        return lax.optimization_barrier((value, *self.last))[0] if self.last else value


def gather_rel(own):
    side = to_chip(own)
    return [own, to_core(own), side, to_core(side)]


class Owners:
    def __init__(self, cap, halves):
        self.cap, self.count = cap, lax.axis_size("dp")
        self.ring = RINGS.get(self.count)
        self.cut = cap // 2 // 8 * 8
        if self.ring:
            n, ring = self.count, self.ring
            self.right = [(ring[i], ring[(i + 1) % n]) for i in range(n)]
            self.left = [(b, a) for a, b in self.right]
            self.far = n // 2
            self.parts = [(0, self.cut), (self.cut, cap)] if halves else [(0, cap)]
            hops = [0] + [h for s in range(1, self.far) for h in (-s, s)]
            ends = [(0, self.cut), (self.cut, cap)]
            self.sizes = [hi - lo for _ in hops for lo, hi in self.parts] + [hi - lo for lo, hi in ends]
            table = [[] for _ in ring]
            for i, d in enumerate(ring):
                table[d] = [ring[(i + h) % n] * cap + lo for h in hops for lo, _ in self.parts]
                table[d] += [ring[(i + self.far) % n] * cap + lo for lo, _ in ends]
            self.starts = lax.dynamic_index_in_dim(jnp.asarray(table, jnp.int32), lax.axis_index("dp"), 0, keepdims=False)
        else:
            self.parts = [(0, cap)]
            self.sizes = [self.count * cap]
            self.starts = jnp.zeros((1,), jnp.int32)

    def go(self, a, b):
        return [lax.ppermute(v, "dp", self.right) for v in a], [lax.ppermute(v, "dp", self.left) for v in b]


class GatherSteps:
    def __init__(self, own, shard):
        self.own, self.out, self.s = own, list(shard), 1
        self.a = self.b = list(shard)
        self.sent = []
        if own.ring:
            self.step(Clock())

    def step(self, clock):
        own = self.own
        if not own.ring or self.s > own.far:
            return
        a, b = clock.at((self.a, self.b))
        if self.s == own.far:
            a, b = ([a[0]], [b[1]]) if len(own.parts) == 2 else ([a[0][:own.cut]], [b[0][own.cut:]])
        self.sent = [*a, *b]
        self.a, self.b = own.go(a, b)
        self.out += [*self.a, *self.b]
        self.s += 1

    def pin(self, clock):
        for v in self.sent:
            clock.add(v)

    def blocks(self):
        if not self.own.ring:
            return [lax.all_gather(self.out[0], "dp", axis=0, tiled=True)]
        while self.s <= self.own.far:
            self.step(Clock())
        return list(self.out)


class ScatterSteps:
    def __init__(self, own, blocks):
        self.own, self.blocks, self.s = own, blocks, own.count // 2 - 1
        self.sent = []
        if own.ring:
            self.a, self.b = own.go([blocks[-2]], [blocks[-1]])

    def more(self):
        return self.own.ring and self.s > 0

    def step(self, clock):
        own, s = self.own, self.s
        if not self.more():
            return

        def add(x, y):
            return (x.astype(F32) + y.astype(F32)).astype(BF)

        n = len(own.parts)
        y, x = (list(clock.at(self.blocks[m * n:(m + 1) * n])) for m in (2 * s - 1, 2 * s))
        a, b = self.a, self.b
        if s < own.far - 1:
            a, b = [add(v, w) for v, w in zip(x, a)], [add(v, w) for v, w in zip(y, b)]
        elif n == 2:
            a, b = [add(x[0], a[0]), x[1]], [y[0], add(y[1], b[0])]
        else:
            a = [lax.dynamic_update_slice_in_dim(x[0], add(x[0][:own.cut], a[0]), 0, 0)]
            b = [lax.dynamic_update_slice_in_dim(y[0], add(y[0][own.cut:], b[0]), own.cut, 0)]
        self.sent = [*a, *b]
        self.a, self.b = own.go(a, b)
        self.s -= 1

    def pin(self, clock):
        for v in self.sent:
            clock.add(v)

    def terms(self):
        own, blocks = self.own, self.blocks
        if own.ring:
            return [list(v) for v in zip(blocks[:len(own.parts)], self.a, self.b)]
        pad = -own.cap % 8
        v = blocks[0].reshape(own.count, own.cap, *blocks[0].shape[1:])
        v = jnp.pad(v, ((0, 0), (0, pad), (0, 0), (0, 0))).reshape(-1, *blocks[0].shape[1:])
        return [[lax.psum_scatter(v, "dp", scatter_dimension=0, tiled=True)[:own.cap]]]


def slot_rows(assign, slots):
    n = assign.shape[0]
    here = lax.broadcasted_iota(jnp.int32, (n, slots), 1) == assign[:, None]
    back = lax.broadcasted_iota(jnp.int32, (n, slots), 0) - n
    return jnp.sum(jnp.where(here, back, 0), axis=0) + n


def rotary_tables(places):
    half = HEAD // 2
    frequency = 10000.0 ** (-jnp.arange(half, dtype=F32) / half)
    angles = frequency[:, None] * places.astype(F32)[None, :]
    return jnp.cos(angles), jnp.sin(angles)


def on_device(tokens, cotangent, group_ids, assign_attn, assign_mlp,
              master_attn, moment_attn, square_attn, master_mlp, moment_mlp, square_mlp):
    owners = lax.axis_size("dp")
    tensor = lax.axis_size("tensor")
    rows_here, width = tokens.shape
    sub = width // LANES
    length = rows_here * tensor
    me, owner = lax.axis_index("tensor"), lax.axis_index("dp")
    perm = jnp.arange(tensor, dtype=jnp.int32) ^ me
    n_attn, n_mlp = width, assign_mlp.shape[0]
    dims, hidden = width // tensor, n_mlp // 2
    cap_a, cap_m = master_attn.shape[1], master_mlp.shape[1]
    part_rows = rows_here // CHUNKS
    cuts = [slice(j * part_rows, (j + 1) * part_rows) for j in range(CHUNKS)]

    def by_slot(v):
        return v.reshape(v.shape[1], sub, LANES)

    own_a, own_m = Owners(cap_a, False), Owners(cap_m, False)
    slots_a = owner * cap_a + jnp.arange(cap_a, dtype=jnp.int32)
    slots_m = owner * cap_m + jnp.arange(cap_m, dtype=jnp.int32)
    low_a = low_call(own_a.parts, after(by_slot(master_attn), perm, own_a.starts, own_m.starts, slots_a, slots_m))

    def named(slots, part):
        return jnp.any(slots[:, None] == part[None, :], axis=1)

    ring_a = GatherSteps(own_a, low_a)
    side = to_chip(after(tokens, low_a[0]))

    def per_slot(v):
        return jnp.broadcast_to(v.astype(F32)[:, None, None], (v.shape[0], 1, LANES))

    def beside(made):
        made, ring_a.a, ring_a.b = lax.optimization_barrier((made, ring_a.a, ring_a.b))
        return made

    pieces_a = beside(slot_rows(after(assign_attn, low_a[0]), owners * cap_a))
    tokens_near = to_core(after(tokens, pieces_a))
    names_m = after(assign_mlp, ring_a.a[0])
    ring_a.step(Clock())
    pieces_m = beside(slot_rows(names_m, owners * cap_m))
    states_m, places, groups = after((by_slot(master_mlp), jnp.arange(length, dtype=jnp.int32), group_ids), ring_a.a[0])
    ring_a.step(Clock())
    weight = jnp.broadcast_to((0.5 + 0.5 * groups.astype(F32))[:, None], (rows_here, LANES))
    weight, low_m, (cos_t, sin_t) = beside((weight, low_call(own_m.parts, states_m), rotary_tables(places)))
    names_a, names_m = after((assign_attn, assign_mlp), ring_a.a[0])
    ring_a.step(Clock())
    in_norm = (slots_a == names_a[n_attn]) | (slots_a == names_a[n_attn + 1])
    rate_a = per_slot(jnp.where(in_norm, 0.2, jnp.where(named(slots_a, names_a[3 * dims:n_attn]), 0.4, 0.06)))
    rate_m = per_slot(jnp.where(named(slots_m, names_m[hidden:]), 0.03, 0.06))
    rate_a, rate_m = beside((rate_a, rate_m))
    if own_a.ring:
        ring_a.out[-2:] = [*ring_a.a, *ring_a.b]
    side = after(side, *ring_a.sent)
    xs = [tokens, tokens_near, side, to_core(side)]
    blocks_a = ring_a.blocks()
    clock = Clock()
    clock.set(xs[3])
    blocks_a[0] = clock.at(blocks_a[0])
    w_attn, held_norms = place_call(blocks_a, own_a.starts, pieces_a, n_attn)
    clock.set(w_attn)
    ring_m = GatherSteps(own_m, after(low_m, *blocks_a[-2:]))
    norms_side = to_chip(held_norms)
    gains = [held_norms, to_core(held_norms), norms_side, to_core(norms_side)]
    norms, n_rel, qt, kt, vt, k4, v4 = qkv_call(perm, xs, gains, w_attn, cos_t, sin_t)
    clock.set(qt)
    ring_m.step(clock)
    ring_m.pin(clock)

    def summed(parts, *first, late=False):
        far = [to_core(clock.at(p)) for p in parts[3:]]
        sent = after(sum_call(parts[2], far), *first)
        near = to_core(after(parts[1], sent) if late else parts[1])
        clock.set(sent)
        return parts[0], near, to_chip(sent)

    fwd = []
    for j in range(CHUNKS):
        *zp, ot, lse = attn_fwd_call(j, CHUNKS, perm, clock.at(qt), k4, vt, w_attn)
        clock.set(ot)
        if j:
            ring_m.step(clock)
            ring_m.pin(clock)
        fwd.append((summed(zp, *([fwd[-1][0][2]] if j else [])), ot, lse))
    state, sides = [], []
    for j in range(CHUNKS):
        z, h, c = residual_call(fwd[j][0], clock.at(tokens[cuts[j]]), norms)
        clock.set(c)
        state.append((z, h, c))
        sides.append((to_core(c), to_chip(c)))
    ring_m.step(clock)
    ring_m.pin(clock)
    blocks_m = ring_m.blocks()
    blocks_m[0] = clock.at(blocks_m[0])
    w_mlp, _ = place_call(blocks_m, own_m.starts, pieces_m, n_mlp)
    clock.set(w_mlp)

    def gathered(own, near, side):
        half = side.shape[0] // 2
        side = clock.at(side)
        return [own, near, side, to_core(side[:half]), to_core(side[half:])]

    mids, sums = [], []
    cs = gathered(state[0][2], *sides[0])
    for j in range(CHUNKS):
        cs[0] = clock.at(cs[0])
        *mp, c_rel, r, g = mlp_fwd_call(cs, w_mlp)
        clock.set(r)
        if j + 1 < CHUNKS:
            clock.add(sides[j + 1][1])
            cs = gathered(state[j + 1][2], *sides[j + 1])
            sums.append(summed(mp, *cs[3:]))
        else:
            sums.append(summed(mp, sums[-1][2]))
        mids.append((sums[j], c_rel, r, g))
    out, sides, dms = None, [], []
    dnorm4 = []
    for j in range(CHUNKS):
        z, h, c = state[j]
        clock.add(mids[j][0][2])
        out, dm, dn = out_call(mids[j][0], clock.at(h), cotangent[cuts[j]], weight[cuts[j]], norms, (j, CHUNKS, out))
        clock.set(dm)
        dnorm4.append(dn)
        dms.append(dm)
        sides.append((to_core(dm), to_chip(dm)))

    backs, sums = [], []
    args = gathered(dms[0], *sides[0])
    for j in range(CHUNKS):
        args[0] = clock.at(args[0])
        *dcp, dm_rel, du = mlp_bwd_call(args, mids[j][3], w_mlp)
        clock.set(du)
        if j + 1 < CHUNKS:
            clock.add(sides[j + 1][1])
            args = gathered(dms[j + 1], *sides[j + 1])
            sums.append(summed(dcp, *args[3:]))
        else:
            grad_down = wgrad_call([clock.at(mids[0][2]), mids[1][2]], [backs[0][1], dm_rel])
            sums.append(summed(dcp, grad_down, sums[-1][2]))
        backs.append((sums[j], dm_rel, du))
    dhs, dzs, sides = [], [], []
    dnorm23 = []
    for j in range(CHUNKS):
        z, h, c = state[j]
        terms = backs[j][0]
        clock.add(terms[2])
        dh, dz, dn = mid_call(terms, clock.at(h), z, cotangent[cuts[j]], weight[cuts[j]], norms)
        clock.set(dz)
        dhs.append(dh)
        dnorm23.append(dn)
        dzs.append(dz)
        sides.append((to_core(dz), to_chip(dz)))
        if j == 0:
            grad_up = wgrad_call([clock.at(b[2]) for b in backs], [m[1] for m in mids])
            clock.set(grad_up)
            buckets_m = bucket_call([clock.at(grad_up), grad_down], own_m.starts, pieces_m, own_m.sizes)
            clock.set(buckets_m[0])
            sums_m = ScatterSteps(own_m, buckets_m)
    sums_m.step(clock)
    sums_m.pin(clock)

    prev, dqs = [(), ()], []
    for j in range(CHUNKS):
        _, ot, lse = fwd[j]
        args = gathered(dzs[j], *sides[j])
        dqs.append([])
        for i in range(2):
            args[0] = clock.at(args[0])
            dq, *prev[i] = attn_bwd_call(j, CHUNKS, i, perm, args, w_attn, qt, k4, kt, v4, ot, lse, cos_t, sin_t, tuple(prev[i]))
            clock.set(dq)
            dqs[j].append(dq)
            if i == 1:
                sums_m.step(clock)
                sums_m.pin(clock)
    dk, dv, grad_out = zip(*prev)
    grad_qkv, *dns = qkv_grad_call(perm, [[clock.at(dqs[0][0]), dqs[0][1]], *dqs[1:]], dk, dv, dnorm23, dnorm4, n_rel, w_attn, norms)
    clock.set(grad_qkv)
    dns = clock.at(dns)
    near, across = to_core(dns[1]), to_core(dns[3])
    da = qkv_in_call(0, CHUNKS, perm, [clock.at(dqs[0][0]), dqs[0][1]], dk, dv, w_attn)
    clock.set(da[0], across)
    norm_side = to_chip(clock.at(dns[2]) + across)
    da_terms = [summed(da, norm_side)]
    norm_sum = dns[0] + near + norm_side
    buckets_a = bucket_call([clock.at(grad_qkv), *grad_out, norm_sum], own_a.starts, pieces_a, own_a.sizes)
    clock.set(buckets_a[0])
    terms_m = sums_m.terms()
    for v in terms_m[0][1:]:
        clock.add(v)
    ring_a = ScatterSteps(own_a, [clock.at(v) for v in buckets_a])
    for j in range(1, CHUNKS):
        da = qkv_in_call(j, CHUNKS, perm, [clock.at(dqs[j][0]), dqs[j][1]], dk, dv, w_attn)
        clock.set(da[0])
        ring_a.step(clock)
        ring_a.pin(clock)
        da_terms.append(summed(da))
    new_m = adam_call(own_m.parts, terms_m, clock.at(rate_m), [by_slot(v) for v in (master_mlp, moment_mlp, square_mlp)])
    clock.set(new_m[0])
    ring_a.step(clock)
    ring_a.pin(clock)
    dx = None
    for j in range(CHUNKS):
        dx = last_call(da_terms[j], clock.at(tokens[cuts[j]]), dhs[j], norms, (j, CHUNKS, dx))
        clock.set(dx)
        ring_a.step(clock)
        ring_a.pin(clock)
    new_a = adam_call(own_a.parts, ring_a.terms(), rate_a, [by_slot(v) for v in (master_attn, moment_attn, square_attn)])
    return (out, dx,
            *(v.reshape(master_attn.shape) for v in new_a), *(v.reshape(master_mlp.shape) for v in new_m))


def solution(mesh):
    tok = P(("dp", "tensor"), None)
    par = P("tensor", "dp", None)
    return jax.shard_map(
        on_device, mesh=mesh,
        in_specs=(tok, tok, P(("dp", "tensor")), P(), P(), par, par, par, par, par, par),
        out_specs=(tok, tok, par, par, par, par, par, par),
        check_vma=False,
    )
```

```python
import functools
import jax
import jax.numpy as jnp
from jax import lax
from jax.sharding import PartitionSpec as P
from jax.experimental import pallas as pl
from jax.experimental.pallas import tpu as pltpu

BF = jnp.bfloat16
F32 = jnp.float32
EPS = 1e-5
HEAD = 64
LANES = 128
QB = 256
CHUNKS = 2
ADAM_STEP = 5


def dot_nn(a, b):
    return lax.dot_general(a, b, (((1,), (0,)), ((), ())), preferred_element_type=F32)


def dot_nt(a, b):
    return lax.dot_general(a, b, (((1,), (1,)), ((), ())), preferred_element_type=F32)


def params(mib):
    return pltpu.CompilerParams(vmem_limit_bytes=mib * 1024 * 1024)


def cost(us):
    return pl.CostEstimate(flops=int(us * 3e6), bytes_accessed=int(us * 1e4), transcendentals=0)


def whole(shape, at=None):
    at = at or (0,) * len(shape)
    return pl.BlockSpec(shape, lambda *_: at)


def shape(dims, dtype):
    return jax.ShapeDtypeStruct(dims, dtype)


def choose(index, refs, into):
    for i in range(4):
        @pl.when(index == i)
        def _():
            if i == 3 and len(refs) == 5:
                half = refs[3].shape[0]
                into[0:half, :] = refs[3][...]
                into[half:, :] = refs[4][...]
            else:
                into[...] = refs[i][...]


def spread(index, refs, value):
    for i in range(4):
        @pl.when(index == i)
        def _():
            if i == 3:
                half = refs[3].shape[0]
                refs[3][...] = value[0:half]
                refs[4][...] = value[half:]
            else:
                refs[i][...] = value


def block_dims(rows, width):
    return [(rows, width)] * 3 + [(rows // 2, width)] * 2


def centre(v):
    mean = jnp.mean(v, axis=-1, keepdims=True)
    vc = v - mean
    s = lax.rsqrt(jnp.mean(vc * vc, axis=-1, keepdims=True) + EPS)
    return vc * s, s


def norm_back(n, s, y, gain):
    dn = y * gain
    return s * (dn - jnp.mean(dn, axis=-1, keepdims=True) - n * jnp.mean(dn * n, axis=-1, keepdims=True))


def total(parts):
    return sum(p[...].astype(F32) for p in parts)


def rows_call(kernel, outs, *args, part=None):
    if part is None:
        return pl.pallas_call(kernel, out_shape=outs, compiler_params=params(10), cost_estimate=cost(2.5))(*args)
    index, count, earlier = part
    rows, width = outs[0].shape
    outs = [shape((rows * count, width), outs[0].dtype), *outs[1:]]
    extra = [] if earlier is None else [earlier]

    def inner(*refs):
        n = len(args)
        kernel(*refs[:n], *refs[n + len(extra):])

    return pl.pallas_call(
        inner, grid=(1,),
        in_specs=[whole(v.shape) for v in args] + [pl.BlockSpec(memory_space=pl.ANY)] * len(extra),
        out_specs=[whole((rows, width), (index, 0))] + [whole(o.shape) for o in outs[1:]],
        out_shape=outs, input_output_aliases={len(args): 0} if extra else {},
        compiler_params=params(10), cost_estimate=cost(2.5),
    )(*args, *extra)


def residual_kernel(p0, p1, p2, x_ref, norms, z_ref, h_ref, c_ref):
    z = total([p0, p1, p2])
    z_ref[...] = z
    n, _ = centre(z)
    h = x_ref[...].astype(F32) + n * norms[2:3, :] + norms[3:4, :]
    h_ref[...] = h
    n, _ = centre(h)
    c_ref[...] = (n * norms[4:5, :] + norms[5:6, :]).astype(BF)


def residual_call(parts, x, norms):
    return rows_call(residual_kernel, [shape(x.shape, F32), shape(x.shape, F32), shape(x.shape, BF)], *parts, x, norms)


def out_kernel(p0, p1, p2, h_ref, ct_ref, wt_ref, norms, lo_ref, dm_ref, dn_ref):
    n, s = centre(total([p0, p1, p2]))
    lo_ref[...] = (h_ref[...] + n * norms[6:7, :] + norms[7:8, :]).astype(BF)
    e = ct_ref[...].astype(F32) * wt_ref[:, 0:1]
    dm_ref[...] = norm_back(n, s, e, norms[6:7, :]).astype(BF)
    dn_ref[0:1, :] = jnp.sum(e * n, axis=0, keepdims=True)
    dn_ref[1:2, :] = jnp.sum(e, axis=0, keepdims=True)


def out_call(parts, h, ct, wt, norms, part):
    return rows_call(out_kernel, [shape(h.shape, BF), shape(h.shape, BF), shape((2, h.shape[1]), F32)], *parts, h, ct, wt, norms, part=part)


def mid_kernel(p0, p1, p2, h_ref, z_ref, ct_ref, wt_ref, norms, dh_ref, dz_ref, dn_ref):
    dc = total([p0, p1, p2])
    n3, s3 = centre(h_ref[...])
    dh = ct_ref[...].astype(F32) * wt_ref[:, 0:1] + norm_back(n3, s3, dc, norms[4:5, :])
    dh_ref[...] = dh
    n2, s2 = centre(z_ref[...])
    dz_ref[...] = norm_back(n2, s2, dh, norms[2:3, :]).astype(BF)
    dn_ref[0:1, :] = jnp.sum(dh * n2, axis=0, keepdims=True)
    dn_ref[1:2, :] = jnp.sum(dh, axis=0, keepdims=True)
    dn_ref[2:3, :] = jnp.sum(dc * n3, axis=0, keepdims=True)
    dn_ref[3:4, :] = jnp.sum(dc, axis=0, keepdims=True)


def mid_call(parts, h, z, ct, wt, norms):
    return rows_call(mid_kernel, [shape(h.shape, F32), shape(h.shape, BF), shape((4, h.shape[1]), F32)],
                     *parts, h, z, ct, wt, norms)


def last_kernel(p0, p1, p2, x_ref, dh_ref, norms, dx_ref):
    n1, s1 = centre(x_ref[...].astype(F32))
    dx_ref[...] = dh_ref[...] + norm_back(n1, s1, total([p0, p1, p2]), norms[0:1, :])


def last_call(parts, x, dh, norms, part):
    return rows_call(last_kernel, [shape(x.shape, F32)], *parts, x, dh, norms, part=part)[0]


def sum_kernel(keep, *refs):
    fars, out = refs[:-1], refs[-1]
    step = fars[0].shape[0]
    for i, f in enumerate(fars):
        at = slice(i * step, (i + 1) * step)
        out[at, :] = (keep[at, :].astype(F32) + f[...].astype(F32)).astype(BF)


def sum_call(keep, fars):
    return pl.pallas_call(
        sum_kernel, out_shape=shape(keep.shape, BF), compiler_params=params(4), cost_estimate=cost(0.1),
    )(keep, *fars)


def qkv_kernel(perm, *refs):
    xs, gs, (w_ref, cos_ref, sin_ref, norms, n_ref, qt_ref, kt_ref, vt_ref, k4_ref, v4_ref, cur) = refs[:4], refs[4:8], refs[8:]

    @pl.when(pl.program_id(0) == 0)
    def _():
        for t in range(4):
            for i, g in enumerate(gs):
                @pl.when(perm[t] == i)
                def _():
                    norms[2 * t:2 * t + 2, :] = g[0:2, :]

    choose(pl.program_id(0), xs, cur)
    n, _ = centre(cur[...].astype(F32))
    n_ref[0] = n.astype(BF)
    a = (n * norms[0:1, :] + norms[1:2, :]).astype(BF)
    cos, sin = cos_ref[...], sin_ref[...]
    dims = qt_ref.shape[0]
    half = HEAD // 2
    for part in range(3):
        proj = dot_nt(w_ref[part * dims:(part + 1) * dims, :], a)
        for h in range(dims // HEAD):
            lo = slice(h * HEAD, h * HEAD + half)
            hi = slice(h * HEAD + half, (h + 1) * HEAD)
            hd = slice(h * HEAD, (h + 1) * HEAD)
            if part < 2:
                first, second = proj[lo], proj[hi]
                r1 = first * cos - second * sin
                r2 = second * cos + first * sin
                if part == 0:
                    qt_ref[lo, :] = (r1 * 0.125).astype(BF)
                    qt_ref[hi, :] = (r2 * 0.125).astype(BF)
                else:
                    full = jnp.concatenate([r1, r2], axis=0)
                    kt_ref[hd, :] = full.astype(BF)
                    k4_ref[h] = full.T.astype(BF)
            else:
                vt_ref[hd, :] = proj[hd].astype(BF)
                v4_ref[h] = proj[hd].T.astype(BF)


def qkv_call(perm, xs, gains, w, cos_t, sin_t):
    rows, width = xs[0].shape
    n = len(xs)
    dims = w.shape[0] // 4
    heads = dims // HEAD
    length = n * rows
    tok = pl.BlockSpec((dims, rows), lambda k, p: (0, p[k]))
    hd = pl.BlockSpec((heads, rows, HEAD), lambda k, p: (0, p[k], 0))
    tab = pl.BlockSpec((HEAD // 2, rows), lambda k, p: (0, p[k]))
    return pl.pallas_call(
        qkv_kernel,
        grid_spec=pltpu.PrefetchScalarGridSpec(
            num_scalar_prefetch=1, grid=(n,),
            in_specs=[whole((rows, width))] * n + [whole(g.shape) for g in gains] + [whole((3 * dims, width)), tab, tab],
            out_specs=[whole((8, width)), pl.BlockSpec((1, rows, width), lambda k, p: (k, 0, 0)), tok, tok, tok, hd, hd],
            scratch_shapes=[pltpu.VMEM((rows, width), BF)],
        ),
        out_shape=[shape((8, width), F32), shape((n, rows, width), BF)] + [shape((dims, length), BF)] * 3 + [shape((heads, length, HEAD), BF)] * 2,
        compiler_params=params(20), cost_estimate=cost(10),
    )(perm, *xs, *gains, w, cos_t, sin_t)


def visible(chunk, diag):
    return (lax.broadcasted_iota(jnp.int32, (diag, QB), 0)
            <= lax.broadcasted_iota(jnp.int32, (diag, QB), 1) + chunk * QB)


def key_spans(n, wide, diag):
    return ([pl.ds(0, n * wide)] if n else []) + [pl.ds(n * wide, diag)]


def pipelined(heads, first, second, third):
    ahead, behind = first(0), None
    for h in range(heads):
        now = ahead
        if h + 1 < heads:
            ahead = first(h + 1)
        done = second(h, now)
        if behind is not None:
            third(h - 1, behind)
        behind = done
    third(heads - 1, behind)


def attn_fwd_kernel(chunk, chunks, count, perm, qt_ref, k4_ref, vt_ref, wo_ref, *rest):
    zs, (ot_ref, lse_ref, acc) = rest[:5], rest[5:]
    heads = k4_ref.shape[0]
    diag = (chunk + 1) * QB
    seen = visible(chunk, diag)
    hd = [slice(h * HEAD, (h + 1) * HEAD) for h in range(heads)]
    cols = [slice(t * QB, (t + 1) * QB) for t in range(count)]
    mine = [slice((chunks * t + chunk) * QB, (chunks * t + chunk + 1) * QB) for t in range(count)]

    def unit(u):
        t, h = u // heads, u % heads
        return t, h, key_spans(t, chunks * QB, diag)

    def scores(u):
        t, h, spans = unit(u)
        return [dot_nn(k4_ref[h, ks, :], qt_ref[hd[h], mine[t]]) for ks in spans]

    def soft(u, s):
        t, h, _ = unit(u)
        s = s[:-1] + [jnp.where(seen, s[-1], -1e30)]
        m = functools.reduce(jnp.maximum, [jnp.max(v, axis=0, keepdims=True) for v in s])
        p = [jnp.exp(v - m) for v in s]
        l = sum(jnp.sum(v, axis=0, keepdims=True) for v in p)
        lse_ref[h:h + 1, cols[t]] = m + jnp.log(l)
        return [v.astype(BF) for v in p], l

    def attend(u, done):
        t, h, spans = unit(u)
        acc[hd[h], cols[t]] = sum(dot_nn(vt_ref[hd[h], ks], v) for ks, v in zip(spans, done[0])) / done[1]

    pipelined(heads * count, scores, soft, attend)
    ot_ref[...] = acc[...].astype(BF)
    for t in range(count):
        o = acc[:, cols[t]].T.astype(BF)
        spread(perm[t], zs, dot_nn(o, wo_ref[...]).astype(BF))


def attn_fwd_call(chunk, chunks, perm, qt, k4, vt, w):
    dims, length = qt.shape
    width = w.shape[1]
    heads = dims // HEAD
    n = length // (chunks * QB)
    outs = block_dims(QB, width) + [(dims, n * QB)]
    return pl.pallas_call(
        functools.partial(attn_fwd_kernel, chunk, chunks, n),
        grid_spec=pltpu.PrefetchScalarGridSpec(
            num_scalar_prefetch=1, grid=(1,),
            in_specs=[whole(qt.shape), whole(k4.shape), whole(vt.shape), whole((dims, width), (3, 0))],
            out_specs=[whole(d) for d in outs] + [whole((heads, n * QB))],
            scratch_shapes=[pltpu.VMEM((dims, n * QB), F32)],
        ),
        out_shape=[shape(d, BF) for d in outs] + [shape((heads, n * QB), F32)],
        compiler_params=params(22), cost_estimate=cost(9.5 + 1.5 * chunk),
    )(perm, qt, k4, vt, w)


def attn_bwd_kernel(chunk, chunks, count, pair, perm, *refs):
    dzs, refs = refs[:5], refs[5:]
    wo_ref, qt_ref, k4_ref, kt_ref, v4_ref, ot_ref, lse_ref, cos_ref, sin_ref = refs[:9]
    refs = refs[9:]
    if chunk == 0:
        dq_ref, dk_ref, dv_ref, gwo_ref, acc, dot_ref, dl_ref, dz_ref = refs
    else:
        dk0, dv0, gwo0, dq_ref, dkl_ref, dvl_ref, gwo_ref, acc, dot_ref, dl_ref, dz_ref, dk_ref, dv_ref = refs
    heads = k4_ref.shape[0]
    half = HEAD // 2
    wide = chunks * QB
    diag = (chunk + 1) * QB
    seen = visible(chunk, diag)
    hd = [slice(h * HEAD, (h + 1) * HEAD) for h in range(heads)]
    cols = [slice(t * QB, (t + 1) * QB) for t in range(count)]
    mine = [slice((chunks * t + chunk) * QB, (chunks * t + chunk + 1) * QB) for t in range(count)]
    if chunk == 0:
        dk_ref[...] = jnp.zeros_like(dk_ref)
        dv_ref[...] = jnp.zeros_like(dv_ref)
    else:
        dk_ref[...] = dk0[...]
        dv_ref[...] = dv0[...]
    for t in range(count):
        choose(perm[t], dzs, dz_ref.at[t])
        dot_ref[:, cols[t]] = dot_nt(wo_ref[...], dz_ref[t]).astype(BF)
    prod = dot_ref[...].astype(F32) * ot_ref[...].astype(F32)
    for h in range(heads):
        dl_ref[h:h + 1, :] = jnp.sum(prod[hd[h]], axis=0, keepdims=True)

    def unit(u):
        t, h = u // heads, u % heads
        return t, h, key_spans(t, wide, diag)

    def scores(u):
        t, h, spans = unit(u)
        return [(dot_nn(k4_ref[h, ks, :], qt_ref[hd[h], mine[t]]), dot_nn(v4_ref[h, ks, :], dot_ref[hd[h], cols[t]])) for ks in spans]

    def soft(u, pairs):
        t, h, spans = unit(u)
        lse, delta = lse_ref[heads * pair + h:heads * pair + h + 1, cols[t]], dl_ref[h:h + 1, cols[t]]
        out = []
        for i, (s, dp) in enumerate(pairs):
            p = jnp.exp(s - lse)
            if i == len(pairs) - 1:
                p = jnp.where(seen, p, 0.0)
            out.append((p.astype(BF), (p * (dp - delta)).astype(BF)))
        return out

    def back(u, pairs):
        t, h, spans = unit(u)
        q, do = qt_ref[hd[h], mine[t]], dot_ref[hd[h], cols[t]]
        dq = 0.0
        for ks, (p, ds) in zip(spans, pairs):
            dv_ref[hd[h], ks] += dot_nt(do, p)
            dk_ref[hd[h], ks] += dot_nt(q, ds)
            dq = dq + dot_nn(kt_ref[hd[h], ks], ds)
        acc[hd[h], cols[t]] = dq

    pipelined(heads * count, scores, soft, back)
    g = dot_nn(ot_ref[...], dz_ref[...].reshape(count * QB, dz_ref.shape[2]))
    gwo_ref[...] = g if chunk == 0 else gwo0[...] + g

    def unturn(src, at, to, scale, out):
        cos, sin = cos_ref[:, at], sin_ref[:, at]
        for h in range(heads):
            lo = slice(h * HEAD, h * HEAD + half)
            hi = slice(h * HEAD + half, (h + 1) * HEAD)
            g1, g2 = src[lo, to] * scale, src[hi, to] * scale
            out[lo, to] = (g1 * cos + g2 * sin).astype(BF)
            out[hi, to] = (g2 * cos - g1 * sin).astype(BF)

    for t in range(count):
        unturn(acc, mine[t], cols[t], 0.125, dq_ref)
    if chunk == chunks - 1:
        unturn(dk_ref, slice(None), slice(None), 1.0, dkl_ref)
        dvl_ref[...] = dv_ref[...].astype(BF)


def attn_bwd_call(chunk, chunks, pair, perm, dzs, w, qt, k4, kt, v4, ot, lse, cos_t, sin_t, prev=()):
    dims, length = qt.shape[0] // 2, qt.shape[1]
    width = w.shape[1]
    heads = dims // HEAD
    n = length // (chunks * QB)
    full, tb = whole((dims, length), (pair, 0)), whole((dims, n * QB), (pair, 0))
    kv4 = whole((heads, length, HEAD), (pair, 0, 0))
    out_full, out_tb, out_w = whole((dims, length)), whole((dims, n * QB)), whole((dims, width))
    in_specs = [whole(d) for d in block_dims(QB, width)] + [
        whole((dims, width), (6 + pair, 0)), full, kv4, full, kv4, tb, whole(lse.shape), whole(cos_t.shape), whole(sin_t.shape)]
    scratch = [pltpu.VMEM((dims, n * QB), F32), pltpu.VMEM((dims, n * QB), BF), pltpu.VMEM((8, n * QB), F32), pltpu.VMEM((n, QB, width), BF)]
    kv = F32
    if chunk:
        in_specs += [out_full, out_full, out_w]
        scratch += [pltpu.VMEM((dims, length), F32)] * 2
        kv = BF
    return pl.pallas_call(
        functools.partial(attn_bwd_kernel, chunk, chunks, n, pair),
        grid_spec=pltpu.PrefetchScalarGridSpec(
            num_scalar_prefetch=1, grid=(1,), in_specs=in_specs,
            out_specs=[out_tb, out_full, out_full, out_w], scratch_shapes=scratch,
        ),
        out_shape=[shape((dims, n * QB), BF), shape((dims, length), kv), shape((dims, length), kv), shape((dims, width), F32)],
        compiler_params=params(22), cost_estimate=cost(10 + 2 * chunk),
    )(perm, *dzs, w, qt, k4, kt, v4, ot, lse, cos_t, sin_t, *prev)


def stack_rows(refs, into, cols=slice(None)):
    at = 0
    for r in refs:
        into[at:at + r.shape[0], cols] = r[...]
        at += r.shape[0]


def qkv_in_kernel(perm, *refs):
    parts, w_ref, das, dx = refs[:6], refs[6], refs[7:12], refs[12]
    stack_rows(parts, dx)
    grad = dx[...].astype(F32).T.astype(BF)
    spread(perm[pl.program_id(0)], das, dot_nn(grad, w_ref[...]).astype(BF))


def qkv_in_call(chunk, chunks, perm, dq, dk, dv, w):
    dims, length = dk[0].shape
    width = w.shape[1]
    n = length // (chunks * QB)
    at = pl.BlockSpec((dims, QB), lambda t, p: (0, chunks * t + chunk))
    return pl.pallas_call(
        qkv_in_kernel,
        grid_spec=pltpu.PrefetchScalarGridSpec(
            num_scalar_prefetch=1, grid=(n,),
            in_specs=[pl.BlockSpec((dims, QB), lambda t, p: (0, t))] * 2 + [at] * 4 + [whole((6 * dims, width))],
            out_specs=[whole(d) for d in block_dims(QB, width)],
            scratch_shapes=[pltpu.VMEM((6 * dims, QB), BF)],
        ),
        out_shape=[shape(d, BF) for d in block_dims(QB, width)],
        compiler_params=params(8), cost_estimate=cost(5),
    )(perm, *dq, *dk, *dv, w)


def qkv_grad_kernel(chunks, count, perm, *refs):
    dqs, kvs, refs = refs[:2 * chunks], refs[2 * chunks:2 * chunks + 4], refs[2 * chunks + 4:]
    d23, d4, (n_ref, w_ref, norms, gw_ref), dns, (dx, rows, sums_ref) = refs[:chunks], refs[chunks:2 * chunks], refs[2 * chunks:2 * chunks + 4], refs[2 * chunks + 4:2 * chunks + 8], refs[2 * chunks + 8:]
    dims = kvs[0].shape[0]
    wide = chunks * QB

    @pl.when(pl.program_id(0) == 0)
    def _():
        for i in range(chunks):
            for p in range(2):
                for t in range(count):
                    to = slice(t * wide + i * QB, t * wide + (i + 1) * QB)
                    dx[p * dims:(p + 1) * dims, to] = dqs[2 * i + p][:, t * QB:(t + 1) * QB]
        stack_rows(kvs, dx.at[2 * dims:])
        sums_ref[...] = jnp.sum(dx[...].astype(F32), axis=1, keepdims=True)

    grad = sum(dot_nn(dx[:, t * wide:(t + 1) * wide], n_ref[perm[t]]) for t in range(count))
    sums = sums_ref[...]
    w = w_ref[...].astype(F32)
    gw_ref[...] = (grad * norms[0:1, :] + sums * norms[1:2, :]).astype(BF)
    rows[0:1, :] = jnp.sum(grad * w, axis=0, keepdims=True)
    rows[1:2, :] = jnp.sum(sums * w, axis=0, keepdims=True)
    rows[2:6, :] = total(d23)
    rows[6:8, :] = total(d4)
    for i, out in enumerate(dns):
        for t in range(4):
            @pl.when(perm[i] == t)
            def _():
                out[...] = rows[2 * t:2 * t + 2, :]


def qkv_grad_call(perm, dqs, dk, dv, d23, d4, n_rel, w, norms):
    chunks = len(dqs)
    n, rows, width = n_rel.shape
    dims = dk[0].shape[0]
    cols = 256
    args = [v for dq in dqs for v in dq] + [*dk, *dv]
    return pl.pallas_call(
        functools.partial(qkv_grad_kernel, chunks, n),
        grid_spec=pltpu.PrefetchScalarGridSpec(
            num_scalar_prefetch=1, grid=(width // cols,),
            in_specs=[whole(v.shape) for v in args] + [pl.BlockSpec((v.shape[0], cols), lambda i, p: (0, i)) for v in (*d23, *d4)] + [
                pl.BlockSpec((n, rows, cols), lambda i, p: (0, 0, i)), pl.BlockSpec((6 * dims, cols), lambda i, p: (0, i)),
                pl.BlockSpec((8, cols), lambda i, p: (0, i))],
            out_specs=[pl.BlockSpec((6 * dims, cols), lambda i, p: (0, i))] + [pl.BlockSpec((2, cols), lambda i, p: (0, i))] * 4,
            scratch_shapes=[pltpu.VMEM((6 * dims, n * rows), BF), pltpu.VMEM((8, cols), F32), pltpu.VMEM((6 * dims, 1), F32)],
        ),
        out_shape=[shape((6 * dims, width), BF)] + [shape((2, width), F32)] * 4,
        compiler_params=params(16), cost_estimate=cost(7),
    )(perm, *args, *d23, *d4, n_rel, w, norms)


def mlp_fwd_kernel(*refs):
    cs, (w1_ref, w2_ref), ms, (c_ref, r_ref, g_ref) = refs[:5], refs[5:7], refs[7:12], refs[12:]
    k = pl.program_id(0)
    choose(k, cs, c_ref.at[0])
    u = dot_nt(c_ref[0], w1_ref[...])
    cdf = 0.5 * (1.0 + lax.erf(u * 0.7071067811865476))
    r = (u * cdf).astype(BF)
    r_ref[0] = r
    g_ref[0] = (cdf + u * (0.3989422804014327 * jnp.exp(-0.5 * u * u))).astype(BF)
    spread(k, ms, dot_nn(r, w2_ref[...]).astype(BF))


def mlp_fwd_call(cs, w):
    rows, width = cs[0].shape
    n, hid = 4, w.shape[0] // 2
    dims = block_dims(rows, width)
    blk = pl.BlockSpec((1, rows, width), lambda k: (k, 0, 0))
    hb = pl.BlockSpec((1, rows, hid), lambda k: (k, 0, 0))
    return pl.pallas_call(
        mlp_fwd_kernel, grid=(n,),
        in_specs=[whole(c.shape) for c in cs] + [whole((hid, width), (0, 0)), whole((hid, width), (1, 0))],
        out_specs=[whole(d) for d in dims] + [blk, hb, hb],
        out_shape=[shape(d, BF) for d in dims] + [shape((n, rows, width), BF)] + [shape((n, rows, hid), BF)] * 2,
        compiler_params=params(16), cost_estimate=cost(9),
    )(*cs, w, w)


def mlp_bwd_kernel(*refs):
    dms, (g_ref, w1_ref, w2_ref), dcs, (dm_ref, du_ref) = refs[:5], refs[5:8], refs[8:13], refs[13:]
    k = pl.program_id(0)
    choose(k, dms, dm_ref.at[0])
    dr = dot_nt(dm_ref[0], w2_ref[...])
    du = (dr * g_ref[0].astype(F32)).astype(BF)
    du_ref[0] = du
    spread(k, dcs, dot_nn(du, w1_ref[...]).astype(BF))


def mlp_bwd_call(dms, g, w):
    rows, width = dms[0].shape
    n, hid = 4, w.shape[0] // 2
    dims = block_dims(rows, width)
    blk = pl.BlockSpec((1, rows, width), lambda k: (k, 0, 0))
    hb = pl.BlockSpec((1, rows, hid), lambda k: (k, 0, 0))
    return pl.pallas_call(
        mlp_bwd_kernel, grid=(n,),
        in_specs=[whole(d.shape) for d in dms] + [hb, whole((hid, width), (0, 0)), whole((hid, width), (1, 0))],
        out_specs=[whole(d) for d in dims] + [blk, hb],
        out_shape=[shape(d, BF) for d in dims] + [shape((n, rows, width), BF), shape((n, rows, hid), BF)],
        compiler_params=params(16), cost_estimate=cost(8),
    )(*dms, g, w, w)


def wgrad_kernel(*refs):
    n = len(refs) // 2
    out = refs[-1]
    acc = 0.0
    for x, y in zip(refs[:n], refs[n:2 * n]):
        tok = x.shape[0] * x.shape[1]
        acc = acc + lax.dot_general(x[...].reshape(tok, x.shape[2]), y[...].reshape(tok, y.shape[2]), (((0,), (0,)), ((), ())), preferred_element_type=F32)
    out[...] = acc.astype(BF)


def wgrad_call(xs, ys, tile=512):
    blocks, rows, hid = xs[0].shape
    width = ys[0].shape[2]
    return pl.pallas_call(
        wgrad_kernel, grid=(hid // tile,),
        in_specs=[pl.BlockSpec((blocks, rows, tile), lambda i: (0, 0, i))] * len(xs) + [whole(y.shape) for y in ys],
        out_specs=pl.BlockSpec((tile, width), lambda i: (i, 0)),
        out_shape=shape((hid, width), BF),
        compiler_params=params(24), cost_estimate=cost(6),
    )(*xs, *ys)


UNROLL = (58, 57, 56, 48, 46, 43, 42, 40, 22, 20, 18, 16, 8, 6, 4, 3, 2, 1)


def place_kernel(sizes, count, starts, pieces, *refs):
    srcs, out_ref, rest_ref, mid = refs[:-3], refs[-3], refs[-2], refs[-1]
    sub = srcs[0].shape[1]
    for k, src in enumerate(srcs):
        base = starts[k]
        step = next(u for u in UNROLL if sizes[k] % u == 0)

        def body(i, c, src=src, base=base, step=step):
            tos = [pieces[base + i * step + u] for u in range(step)]
            vals = [src[i * step + u].astype(F32) for u in range(step)]
            for u in range(step):
                mid[pl.ds(pl.multiple_of(tos[u] * sub, sub), sub), :] = vals[u]
            return c

        lax.fori_loop(0, sizes[k] // step, body, 0)
    rows = 64

    def spread(i, c):
        r = pl.multiple_of(i * rows, rows)
        for j in range(sub):
            part = mid[pl.ds(r * sub + j, rows, stride=sub), :]
            out_ref[pl.ds(r, rows), j * LANES:(j + 1) * LANES] = part.astype(BF)
        return c

    lax.fori_loop(0, count // rows, spread, 0)
    for j in range(sub):
        rest_ref[:, j * LANES:(j + 1) * LANES] = mid[pl.ds(count * sub + j, 8, stride=sub), :]


def place_call(blocks, starts, pieces, count):
    sub = blocks[0].shape[1]
    sizes = [b.shape[0] for b in blocks]
    return pl.pallas_call(
        functools.partial(place_kernel, sizes, count),
        grid_spec=pltpu.PrefetchScalarGridSpec(
            num_scalar_prefetch=2, grid=(1,),
            in_specs=[whole(b.shape) for b in blocks],
            out_specs=[whole((count, sub * LANES)), whole((8, sub * LANES))],
            scratch_shapes=[pltpu.VMEM(((count + 8) * sub, LANES), F32)],
        ),
        out_shape=[shape((count, sub * LANES), BF), shape((8, sub * LANES), F32)],
        compiler_params=params(10 + count // 146), cost_estimate=cost(count / 450),
    )(starts, pieces, *blocks)


def bucket_kernel(sizes, starts, pieces, *refs):
    n = len(sizes)
    grads, outs, mid = refs[:-n - 1], refs[-n - 1:-1], refs[-1]
    width = grads[0].shape[1]
    sub = width // LANES
    rows = 64
    at = 0
    for g in grads:
        if g.shape[0] % rows:
            for j in range(sub):
                mid[pl.ds(at * sub + j, g.shape[0], stride=sub), :] = g[:, j * LANES:(j + 1) * LANES].astype(F32)
            at += g.shape[0]
            continue

        def split(i, c, g=g, at=at):
            r = pl.multiple_of(i * rows, rows)
            for j in range(sub):
                mid[pl.ds((at + r) * sub + j, rows, stride=sub), :] = g[pl.ds(r, rows), j * LANES:(j + 1) * LANES].astype(F32)
            return c

        lax.fori_loop(0, g.shape[0] // rows, split, 0)
        at += g.shape[0]
    mid[at * sub:(at + 8) * sub, :] = jnp.zeros((8 * sub, LANES), F32)
    for k, out in enumerate(outs):
        base = starts[k]
        step = next(u for u in UNROLL if sizes[k] % u == 0)

        def body(i, c, out=out, base=base, step=step):
            srcs = [pieces[base + i * step + u] for u in range(step)]
            vals = [mid[pl.ds(pl.multiple_of(v * sub, sub), sub), :].astype(BF) for v in srcs]
            for u in range(step):
                out[i * step + u] = vals[u]
            return c

        lax.fori_loop(0, sizes[k] // step, body, 0)


def bucket_call(grads, starts, pieces, sizes):
    width = grads[0].shape[1]
    sub = width // LANES
    count = sum(g.shape[0] for g in grads)
    shapes = [(s, sub, LANES) for s in sizes]
    return pl.pallas_call(
        functools.partial(bucket_kernel, sizes),
        grid_spec=pltpu.PrefetchScalarGridSpec(
            num_scalar_prefetch=2, grid=(1,),
            in_specs=[whole(g.shape) for g in grads],
            out_specs=[whole(s) for s in shapes],
            scratch_shapes=[pltpu.VMEM(((count + 8) * sub, LANES), F32)],
        ),
        out_shape=[jax.ShapeDtypeStruct(s, BF) for s in shapes],
        compiler_params=params(8 + count // 146), cost_estimate=cost(count / 350),
    )(starts, pieces, *grads)


def adam_kernel(bounds, *refs):
    parts, (rate, m_ref, f_ref, s_ref, om, of, os) = refs[:-7], refs[-7:]
    each = len(parts) // len(bounds)
    for i, (lo, hi) in enumerate(bounds):
        at = slice(lo, hi)
        g = total(parts[i * each:(i + 1) * each])
        first = 0.5 * f_ref[at] + 0.5 * g
        second = 0.5 * s_ref[at] + 0.5 * g * g
        of[at] = first
        os[at] = second
        w = m_ref[at]
        first = first / (1.0 - 0.5**ADAM_STEP)
        second = second / (1.0 - 0.5**ADAM_STEP)
        om[at] = w - rate[at] * (first / (jnp.sqrt(second) + 1e-8) + 0.1 * w)


def adam_call(bounds, parts, rate, states):
    cap, sub, lanes = states[0].shape
    step = next(d for d in range(64, 0, -1) if cap % d == 0) if len(bounds) == 1 else cap
    if len(bounds) == 1:
        bounds = [(0, step)]
    blk = pl.BlockSpec((step, sub, lanes), lambda i: (i, 0, 0))
    terms = [v for part in parts for v in part]
    return pl.pallas_call(
        functools.partial(adam_kernel, bounds), grid=(cap // step,),
        in_specs=[blk if len(bounds) == 1 else whole(v.shape) for v in terms] + [
            pl.BlockSpec((step, 1, lanes), lambda i: (i, 0, 0))] + [blk] * 3,
        out_specs=[blk] * 3,
        out_shape=[shape(v.shape, F32) for v in states],
        compiler_params=params(12), cost_estimate=cost(cap / 80),
    )(*terms, rate, *states)


def low_kernel(bounds, x_ref, *outs):
    for (lo, hi), out in zip(bounds, outs):
        out[...] = x_ref[lo:hi].astype(BF)


def low_call(bounds, v):
    return list(pl.pallas_call(
        functools.partial(low_kernel, bounds), out_shape=[shape((hi - lo, *v.shape[1:]), BF) for lo, hi in bounds],
        compiler_params=params(6), cost_estimate=cost(1),
    )(v))


TOP = [(0, 1), (1, 0), (2, 3), (3, 2)]
SIDE = [(0, 2), (1, 3), (2, 0), (3, 1)]
RINGS = {8: [0, 2, 4, 6, 7, 5, 3, 1]}


def to_core(v):
    return lax.ppermute(v, "tensor", TOP)


def to_chip(v):
    return lax.ppermute(v, "tensor", SIDE)


def after(v, *first):
    if not first:
        return v
    return lax.optimization_barrier((v, *first))[0]


class Clock:
    def __init__(self):
        self.last = []

    def set(self, *values):
        self.last = list(values)

    def add(self, value):
        self.last.append(value)

    def at(self, value):
        return lax.optimization_barrier((value, *self.last))[0] if self.last else value


def gather_rel(own):
    side = to_chip(own)
    return [own, to_core(own), side, to_core(side)]


class Owners:
    def __init__(self, cap, halves):
        self.cap, self.count = cap, lax.axis_size("dp")
        self.ring = RINGS.get(self.count)
        self.cut = cap // 2 // 8 * 8
        if self.ring:
            n, ring = self.count, self.ring
            self.right = [(ring[i], ring[(i + 1) % n]) for i in range(n)]
            self.left = [(b, a) for a, b in self.right]
            self.far = n // 2
            self.parts = [(0, self.cut), (self.cut, cap)] if halves else [(0, cap)]
            hops = [0] + [h for s in range(1, self.far) for h in (-s, s)]
            ends = [(0, self.cut), (self.cut, cap)]
            self.sizes = [hi - lo for _ in hops for lo, hi in self.parts] + [hi - lo for lo, hi in ends]
            table = [[] for _ in ring]
            for i, d in enumerate(ring):
                table[d] = [ring[(i + h) % n] * cap + lo for h in hops for lo, _ in self.parts]
                table[d] += [ring[(i + self.far) % n] * cap + lo for lo, _ in ends]
            self.starts = lax.dynamic_index_in_dim(jnp.asarray(table, jnp.int32), lax.axis_index("dp"), 0, keepdims=False)
        else:
            self.parts = [(0, cap)]
            self.sizes = [self.count * cap]
            self.starts = jnp.zeros((1,), jnp.int32)

    def go(self, a, b):
        return [lax.ppermute(v, "dp", self.right) for v in a], [lax.ppermute(v, "dp", self.left) for v in b]


class GatherSteps:
    def __init__(self, own, shard):
        self.own, self.out, self.s = own, list(shard), 1
        self.a = self.b = list(shard)
        self.sent = []
        if own.ring:
            self.step(Clock())

    def step(self, clock):
        own = self.own
        if not own.ring or self.s > own.far:
            return
        a, b = clock.at((self.a, self.b))
        if self.s == own.far:
            a, b = ([a[0]], [b[1]]) if len(own.parts) == 2 else ([a[0][:own.cut]], [b[0][own.cut:]])
        self.sent = [*a, *b]
        self.a, self.b = own.go(a, b)
        self.out += [*self.a, *self.b]
        self.s += 1

    def pin(self, clock):
        for v in self.sent:
            clock.add(v)

    def blocks(self):
        if not self.own.ring:
            return [lax.all_gather(self.out[0], "dp", axis=0, tiled=True)]
        while self.s <= self.own.far:
            self.step(Clock())
        return list(self.out)


class ScatterSteps:
    def __init__(self, own, blocks):
        self.own, self.blocks, self.s = own, blocks, own.count // 2 - 1
        self.sent = []
        if own.ring:
            self.a, self.b = own.go([blocks[-2]], [blocks[-1]])

    def more(self):
        return self.own.ring and self.s > 0

    def step(self, clock):
        own, s = self.own, self.s
        if not self.more():
            return

        def add(x, y):
            return (x.astype(F32) + y.astype(F32)).astype(BF)

        n = len(own.parts)
        y, x = (list(clock.at(self.blocks[m * n:(m + 1) * n])) for m in (2 * s - 1, 2 * s))
        a, b = self.a, self.b
        if s < own.far - 1:
            a, b = [add(v, w) for v, w in zip(x, a)], [add(v, w) for v, w in zip(y, b)]
        elif n == 2:
            a, b = [add(x[0], a[0]), x[1]], [y[0], add(y[1], b[0])]
        else:
            a = [lax.dynamic_update_slice_in_dim(x[0], add(x[0][:own.cut], a[0]), 0, 0)]
            b = [lax.dynamic_update_slice_in_dim(y[0], add(y[0][own.cut:], b[0]), own.cut, 0)]
        self.sent = [*a, *b]
        self.a, self.b = own.go(a, b)
        self.s -= 1

    def pin(self, clock):
        for v in self.sent:
            clock.add(v)

    def terms(self):
        own, blocks = self.own, self.blocks
        if own.ring:
            return [list(v) for v in zip(blocks[:len(own.parts)], self.a, self.b)]
        pad = -own.cap % 8
        v = blocks[0].reshape(own.count, own.cap, *blocks[0].shape[1:])
        v = jnp.pad(v, ((0, 0), (0, pad), (0, 0), (0, 0))).reshape(-1, *blocks[0].shape[1:])
        return [[lax.psum_scatter(v, "dp", scatter_dimension=0, tiled=True)[:own.cap]]]


def slot_rows(assign, slots):
    n = assign.shape[0]
    here = lax.broadcasted_iota(jnp.int32, (n, slots), 1) == assign[:, None]
    back = lax.broadcasted_iota(jnp.int32, (n, slots), 0) - n
    return jnp.sum(jnp.where(here, back, 0), axis=0) + n


def rotary_tables(places):
    half = HEAD // 2
    frequency = 10000.0 ** (-jnp.arange(half, dtype=F32) / half)
    angles = frequency[:, None] * places.astype(F32)[None, :]
    return jnp.cos(angles), jnp.sin(angles)


def on_device(tokens, cotangent, group_ids, assign_attn, assign_mlp,
              master_attn, moment_attn, square_attn, master_mlp, moment_mlp, square_mlp):
    owners = lax.axis_size("dp")
    tensor = lax.axis_size("tensor")
    rows_here, width = tokens.shape
    sub = width // LANES
    length = rows_here * tensor
    me, owner = lax.axis_index("tensor"), lax.axis_index("dp")
    perm = jnp.arange(tensor, dtype=jnp.int32) ^ me
    n_attn, n_mlp = width, assign_mlp.shape[0]
    dims, hidden = width // tensor, n_mlp // 2
    cap_a, cap_m = master_attn.shape[1], master_mlp.shape[1]
    part_rows = rows_here // CHUNKS
    cuts = [slice(j * part_rows, (j + 1) * part_rows) for j in range(CHUNKS)]

    def by_slot(v):
        return v.reshape(v.shape[1], sub, LANES)

    own_a, own_m = Owners(cap_a, False), Owners(cap_m, False)
    slots_a = owner * cap_a + jnp.arange(cap_a, dtype=jnp.int32)
    slots_m = owner * cap_m + jnp.arange(cap_m, dtype=jnp.int32)
    low_a = low_call(own_a.parts, after(by_slot(master_attn), perm, own_a.starts, own_m.starts, slots_a, slots_m))

    def named(slots, part):
        return jnp.any(slots[:, None] == part[None, :], axis=1)

    ring_a = GatherSteps(own_a, low_a)
    side = to_chip(after(tokens, low_a[0]))

    def per_slot(v):
        return jnp.broadcast_to(v.astype(F32)[:, None, None], (v.shape[0], 1, LANES))

    def beside(made):
        made, ring_a.a, ring_a.b = lax.optimization_barrier((made, ring_a.a, ring_a.b))
        return made

    pieces_a = beside(slot_rows(after(assign_attn, low_a[0]), owners * cap_a))
    tokens_near = to_core(after(tokens, pieces_a))
    names_m = after(assign_mlp, ring_a.a[0])
    ring_a.step(Clock())
    pieces_m = beside(slot_rows(names_m, owners * cap_m))
    states_m, places, groups = after((by_slot(master_mlp), jnp.arange(length, dtype=jnp.int32), group_ids), ring_a.a[0])
    ring_a.step(Clock())
    weight = jnp.broadcast_to((0.5 + 0.5 * groups.astype(F32))[:, None], (rows_here, LANES))
    weight, low_m, (cos_t, sin_t) = beside((weight, low_call(own_m.parts, states_m), rotary_tables(places)))
    names_a, names_m = after((assign_attn, assign_mlp), ring_a.a[0])
    ring_a.step(Clock())
    in_norm = (slots_a == names_a[n_attn]) | (slots_a == names_a[n_attn + 1])
    rate_a = per_slot(jnp.where(in_norm, 0.2, jnp.where(named(slots_a, names_a[3 * dims:n_attn]), 0.4, 0.06)))
    rate_m = per_slot(jnp.where(named(slots_m, names_m[hidden:]), 0.03, 0.06))
    rate_a, rate_m = beside((rate_a, rate_m))
    if own_a.ring:
        ring_a.out[-2:] = [*ring_a.a, *ring_a.b]
    side = after(side, *ring_a.sent)
    xs = [tokens, tokens_near, side, to_core(side)]
    blocks_a = ring_a.blocks()
    clock = Clock()
    clock.set(xs[3])
    blocks_a[0] = clock.at(blocks_a[0])
    w_attn, held_norms = place_call(blocks_a, own_a.starts, pieces_a, n_attn)
    clock.set(w_attn)
    ring_m = GatherSteps(own_m, after(low_m, *blocks_a[-2:]))
    norms_side = to_chip(held_norms)
    gains = [held_norms, to_core(held_norms), norms_side, to_core(norms_side)]
    norms, n_rel, qt, kt, vt, k4, v4 = qkv_call(perm, xs, gains, w_attn, cos_t, sin_t)
    clock.set(qt)
    ring_m.step(clock)
    ring_m.pin(clock)

    def summed(parts, *first, late=False):
        far = [to_core(clock.at(p)) for p in parts[3:]]
        sent = after(sum_call(parts[2], far), *first)
        near = to_core(after(parts[1], sent) if late else parts[1])
        clock.set(sent)
        return parts[0], near, to_chip(sent)

    fwd = []
    for j in range(CHUNKS):
        *zp, ot, lse = attn_fwd_call(j, CHUNKS, perm, clock.at(qt), k4, vt, w_attn)
        clock.set(ot)
        if j:
            ring_m.step(clock)
            ring_m.pin(clock)
        fwd.append((summed(zp, *([fwd[-1][0][2]] if j else [])), ot, lse))
    state, sides = [], []
    for j in range(CHUNKS):
        z, h, c = residual_call(fwd[j][0], clock.at(tokens[cuts[j]]), norms)
        clock.set(c)
        state.append((z, h, c))
        sides.append((to_core(c), to_chip(c)))
    ring_m.step(clock)
    ring_m.pin(clock)
    blocks_m = ring_m.blocks()
    blocks_m[0] = clock.at(blocks_m[0])
    w_mlp, _ = place_call(blocks_m, own_m.starts, pieces_m, n_mlp)
    clock.set(w_mlp)

    def gathered(own, near, side):
        half = side.shape[0] // 2
        side = clock.at(side)
        return [own, near, side, to_core(side[:half]), to_core(side[half:])]

    mids, sums = [], []
    cs = gathered(state[0][2], *sides[0])
    for j in range(CHUNKS):
        cs[0] = clock.at(cs[0])
        *mp, c_rel, r, g = mlp_fwd_call(cs, w_mlp)
        clock.set(r)
        if j + 1 < CHUNKS:
            clock.add(sides[j + 1][1])
            cs = gathered(state[j + 1][2], *sides[j + 1])
            sums.append(summed(mp, *cs[3:]))
        else:
            sums.append(summed(mp, sums[-1][2]))
        mids.append((sums[j], c_rel, r, g))
    outs, sides, dms = [], [], []
    dnorm4 = []
    for j in range(CHUNKS):
        z, h, c = state[j]
        clock.add(mids[j][0][2])
        lo, dm, dn = out_call(mids[j][0], clock.at(h), cotangent[cuts[j]], weight[cuts[j]], norms, None)
        clock.set(dm)
        dnorm4.append(dn)
        outs.append(lo)
        dms.append(dm)
        sides.append((to_core(dm), to_chip(dm)))

    backs, sums = [], []
    args = gathered(dms[0], *sides[0])
    for j in range(CHUNKS):
        args[0] = clock.at(args[0])
        *dcp, dm_rel, du = mlp_bwd_call(args, mids[j][3], w_mlp)
        clock.set(du)
        if j + 1 < CHUNKS:
            clock.add(sides[j + 1][1])
            args = gathered(dms[j + 1], *sides[j + 1])
            sums.append(summed(dcp, *args[3:]))
        else:
            grad_down = wgrad_call([clock.at(mids[0][2]), mids[1][2]], [backs[0][1], dm_rel])
            sums.append(summed(dcp, grad_down, sums[-1][2]))
        backs.append((sums[j], dm_rel, du))
    dhs, dzs, sides = [], [], []
    dnorm23 = []
    for j in range(CHUNKS):
        z, h, c = state[j]
        terms = backs[j][0]
        clock.add(terms[2])
        dh, dz, dn = mid_call(terms, clock.at(h), z, cotangent[cuts[j]], weight[cuts[j]], norms)
        clock.set(dz)
        dhs.append(dh)
        dnorm23.append(dn)
        dzs.append(dz)
        sides.append((to_core(dz), to_chip(dz)))
        if j == 0:
            grad_up = wgrad_call([clock.at(b[2]) for b in backs], [m[1] for m in mids])
            clock.set(grad_up)
            buckets_m = bucket_call([clock.at(grad_up), grad_down], own_m.starts, pieces_m, own_m.sizes)
            clock.set(buckets_m[0])
            sums_m = ScatterSteps(own_m, buckets_m)
    sums_m.step(clock)
    sums_m.pin(clock)

    prev, dqs = [(), ()], []
    for j in range(CHUNKS):
        _, ot, lse = fwd[j]
        args = gathered(dzs[j], *sides[j])
        dqs.append([])
        for i in range(2):
            args[0] = clock.at(args[0])
            dq, *prev[i] = attn_bwd_call(j, CHUNKS, i, perm, args, w_attn, qt, k4, kt, v4, ot, lse, cos_t, sin_t, tuple(prev[i]))
            clock.set(dq)
            dqs[j].append(dq)
            if i == 1:
                sums_m.step(clock)
                sums_m.pin(clock)
    dk, dv, grad_out = zip(*prev)
    grad_qkv, *dns = qkv_grad_call(perm, [[clock.at(dqs[0][0]), dqs[0][1]], *dqs[1:]], dk, dv, dnorm23, dnorm4, n_rel, w_attn, norms)
    clock.set(grad_qkv)
    dns = clock.at(dns)
    near, across = to_core(dns[1]), to_core(dns[3])
    da = qkv_in_call(0, CHUNKS, perm, [clock.at(dqs[0][0]), dqs[0][1]], dk, dv, w_attn)
    clock.set(da[0], across)
    norm_side = to_chip(clock.at(dns[2]) + across)
    da_terms = [summed(da, norm_side)]
    norm_sum = dns[0] + near + norm_side
    buckets_a = bucket_call([clock.at(grad_qkv), *grad_out, norm_sum], own_a.starts, pieces_a, own_a.sizes)
    clock.set(buckets_a[0])
    terms_m = sums_m.terms()
    for v in terms_m[0][1:]:
        clock.add(v)
    ring_a = ScatterSteps(own_a, [clock.at(v) for v in buckets_a])
    for j in range(1, CHUNKS):
        da = qkv_in_call(j, CHUNKS, perm, [clock.at(dqs[j][0]), dqs[j][1]], dk, dv, w_attn)
        clock.set(da[0])
        ring_a.step(clock)
        ring_a.pin(clock)
        da_terms.append(summed(da))
    new_m = adam_call(own_m.parts, terms_m, clock.at(rate_m), [by_slot(v) for v in (master_mlp, moment_mlp, square_mlp)])
    clock.set(new_m[0])
    ring_a.step(clock)
    ring_a.pin(clock)
    dx = None
    for j in range(CHUNKS):
        dx = last_call(da_terms[j], clock.at(tokens[cuts[j]]), dhs[j], norms, (j, CHUNKS, dx))
        clock.set(dx)
        ring_a.step(clock)
        ring_a.pin(clock)
    new_a = adam_call(own_a.parts, ring_a.terms(), rate_a, [by_slot(v) for v in (master_attn, moment_attn, square_attn)])
    return (jnp.concatenate(outs, axis=0), dx,
            *(v.reshape(master_attn.shape) for v in new_a), *(v.reshape(master_mlp.shape) for v in new_m))


def solution(mesh):
    tok = P(("dp", "tensor"), None)
    par = P("tensor", "dp", None)
    return jax.shard_map(
        on_device, mesh=mesh,
        in_specs=(tok, tok, P(("dp", "tensor")), P(), P(), par, par, par, par, par, par),
        out_specs=(tok, tok, par, par, par, par, par, par),
        check_vma=False,
    )
```
